32 devices in a mesh: band: 4 (over y, core), tile: 8 (over z, x).
Axes of the slice: x: 2, y: 2, z: 4, core: 2. Of those that a mesh axis runs over, the one named last changes fastest.
Arguments:
- cond_x: float32 [8, 512, 2048], P('band', 'tile'), may hold values from 0.2 to 5
- cond_y: float32 [8, 512, 2048], P('band', 'tile'), may hold values from 0.2 to 5
- via_cond: float32 [8, 512, 2048], P('band', 'tile'), may hold values from 0.5 to 8
- via_mask: int32 [8, 512, 2048], P('band', 'tile'), may hold values 0 or 1
- capacitance: float32 [8, 512, 2048], P('band', 'tile'), may hold values from 0.5 to 4
- pad_mask: int32 [8, 512, 2048], P('band', 'tile'), may hold values 0 or 1
- observe: float32 [2, 8, 512, 2048], P(None, 'band', 'tile'), may hold values from -40 to 40
Outputs:
- adjoint: float32 [2, 8, 512, 2048], P(None, 'band', 'tile')
The draws below stay inside these ranges and needn't reach their ends.
All inputs are finite; a program needn't handle non-finite values. No bound on the sum of `via_mask` or of `pad_mask` on one device may be relied on, other than what follows from the above.
Results may differ from the reference program's by a relative error of at most 0.0003.
Values sent between devices are 32-bit elements; how exact they have to be, the bound alone decides.
No kernel may reach another device: no remote copies, remote signals or barrier semaphores. Data moves between devices by JAX's collectives and lax.ppermute only.
A program may use at most 128 MiB of HBM per device.

```python
import math
import jax
import jax.numpy as jnp

NB = 8
NY = 2048
STEPS = 2
ITERS = 2
NX = 512


def draw_observe(key, part):
    first_key = jax.random.fold_in(key, 0)
    shape = (STEPS, NB, NX, NY)
    rows = jnp.arange(NX, dtype=jnp.float32) / max(NX - 1, 1)
    ramp = (1.0 + 2.0 * rows)[None, None, :, None]
    base = jnp.clip(jax.random.normal(first_key, shape, jnp.float32), -4.0, 4.0)
    return base * ramp


def place_ends(result, stream_key, low, high):
    index_at = [jax.random.randint(jax.random.fold_in(stream_key, axis), (), 0, length) for axis, length in enumerate(result.shape)]
    widest = result.shape.index(max(result.shape))
    neighbour = index_at[:widest] + [(index_at[widest] + 1) % result.shape[widest]] + index_at[widest + 1:]
    return result.at[tuple(index_at)].set(low).at[tuple(neighbour)].set(high)


def level_of(own_key, extent, pieces, low, largest):
    def one(axis_at, blocks):
        draws = jax.random.uniform(jax.random.fold_in(jax.random.fold_in(own_key, 6), axis_at), (blocks,), jnp.float32, low / len(pieces), largest / len(pieces))
        return jnp.repeat(jnp.exp(draws), extent[axis_at] // blocks).reshape((-1,) + (1,) * (len(extent) - axis_at - 1))

    level = one(*pieces[0])
    for cut in pieces[1:]:
        level = level * one(*cut)
    return level


def setup_inputs(seed: int = 0) -> dict:
    arg_keys = jax.random.split(jax.random.key(seed), 8)
    return {
        "cond_x": jnp.clip(jnp.exp(math.log(5.0) - 3.218876 * jax.random.uniform(arg_keys[0], (NB, NX, NY), jnp.float32) ** level_of(arg_keys[0], (NB, NX, NY), ((0, 4), (1, 8)), -0.2, 0.2)), 0.2, 5.0),
        "cond_y": jnp.clip(jnp.exp(math.log(5.0) - 3.218876 * jax.random.uniform(arg_keys[1], (NB, NX, NY), jnp.float32) ** level_of(arg_keys[1], (NB, NX, NY), ((0, 4), (1, 8)), -0.2, 0.2)), 0.2, 5.0),
        "via_cond": jnp.clip(jnp.exp(math.log(8.0) - 2.7725887 * jax.random.uniform(arg_keys[2], (NB, NX, NY), jnp.float32) ** level_of(arg_keys[2], (NB, NX, NY), ((0, 4), (1, 8)), -0.2, 0.2)), 0.5, 8.0),
        "via_mask": place_ends((jax.random.randint(arg_keys[3], (NB, NX, NY), 0, 4) < 1).astype(jnp.int32), jax.random.fold_in(arg_keys[3], 1), 0, 1),
        "capacitance": jnp.clip(jnp.exp(math.log(4.0) - 2.0794415 * jax.random.uniform(arg_keys[4], (NB, NX, NY), jnp.float32) ** level_of(arg_keys[4], (NB, NX, NY), ((0, 4), (1, 8)), -0.2, 0.2)), 0.5, 4.0),
        "pad_mask": place_ends((jax.random.randint(arg_keys[5], (NB, NX, NY), 0, 16) < 1).astype(jnp.int32), jax.random.fold_in(arg_keys[5], 1), 0, 1),
        "observe": draw_observe(jax.random.fold_in(arg_keys[7], 71), 0),
    }


pad_conductance = 4.0


def apply_operator(padded, rims_coeff, diagonal):
    center = padded[1:-1, 1:-1, 1:-1]
    here = rims_coeff[:, 1:-1, 1:-1, 1:-1]
    total = diagonal * center
    total = total + here[0] * (center - padded[1:-1, 2:, 1:-1]) + rims_coeff[0, 1:-1, :-2, 1:-1] * (center - padded[1:-1, :-2, 1:-1])
    total = total + here[1] * (center - padded[1:-1, 1:-1, 2:]) + rims_coeff[1, 1:-1, 1:-1, :-2] * (center - padded[1:-1, 1:-1, :-2])
    total = total + here[2] * (center - padded[2:, 1:-1, 1:-1]) + rims_coeff[2, :-2, 1:-1, 1:-1] * (center - padded[:-2, 1:-1, 1:-1])
    return total


def jacobi_scale(rims_coeff, diagonal):
    here = rims_coeff[:, 1:-1, 1:-1, 1:-1]
    return (diagonal + here[0] + here[1] + here[2] + rims_coeff[0, 1:-1, :-2, 1:-1]
            + rims_coeff[1, 1:-1, 1:-1, :-2] + rims_coeff[2, :-2, 1:-1, 1:-1])


def solve_pcg(right_side, start, operator_fn, scale):
    residual = right_side - operator_fn(start)
    search = residual / scale
    norm_now = jnp.sum(residual * search)
    answer = start
    for iteration in range(ITERS):
        image_vec = operator_fn(search)
        step_len = norm_now / jnp.sum(search * image_vec)
        answer = answer + step_len * search
        residual = residual - step_len * image_vec
        if iteration + 1 < ITERS:
            precond_res = residual / scale
            norm_next = jnp.sum(residual * precond_res)
            search = precond_res + (norm_next / norm_now) * search
            norm_now = norm_next
    return answer


def reference(cond_x, cond_y, via_cond, via_mask, capacitance, pad_mask, observe):
    keep = (jnp.arange(NB) < NB - 1).astype(jnp.float32)[:, None, None]
    via_g = via_cond * via_mask.astype(jnp.float32) * keep
    coeffs = jnp.stack([cond_x, cond_y, via_g])
    rims_coeff = jnp.pad(coeffs, ((0, 0), (1, 1), (1, 1), (1, 1)))
    diagonal = capacitance + pad_conductance * pad_mask.astype(jnp.float32)
    scale = jacobi_scale(rims_coeff, diagonal)

    def operator_fn(values):
        return apply_operator(jnp.pad(values, 1), rims_coeff, diagonal)

    later = jnp.zeros_like(capacitance)
    results = [later] * STEPS
    for time_step in range(STEPS - 1, -1, -1):
        right_side = capacitance * later + observe[time_step]
        if time_step == STEPS - 1:
            start = right_side / scale
        else:
            start = later
        later = solve_pcg(right_side, start, operator_fn, scale)
        results[time_step] = later
    return jnp.stack(results)
```

```python
import jax
import jax.numpy as jnp
from jax import lax
from jax.experimental import pallas as pl
from jax.experimental.pallas import tpu as pltpu
from jax.sharding import PartitionSpec as P

NB = 8
ROWS = 8
AXES = ("band", "tile")
F32 = jnp.float32

pad_conductance = 4.0


def sizes():
    return lax.axis_size("band"), lax.axis_size("tile")


def joint_permute(x, partner):
    nb, nt = sizes()
    pairs = []
    for b in range(nb):
        for t in range(nt):
            pb, pt = partner(b, t)
            pairs.append((b * nt + t, pb * nt + pt))
    return lax.ppermute(x, AXES, pairs)


def core_swap(x):
    nb, _ = sizes()
    return lax.ppermute(x, "band", [(b, b ^ 1) for b in range(nb)])


def outer_swap(x):
    nb, nt = sizes()

    def partner(b, t):
        if b in (0, nb - 1):
            return b, t ^ 2
        return (b + 1 if b % 2 else b - 1), t

    return joint_permute(x, partner)


def even_swap(x):
    _, nt = sizes()
    return lax.ppermute(x, "tile", [(t, t ^ 1) for t in range(nt)])


def odd_swap(x):
    nb, nt = sizes()

    def partner(b, t):
        if t in (0, nt - 1):
            return b ^ 1, t
        return b, (t + 1 if t % 2 else t - 1)

    return joint_permute(x, partner)


def all_total(parts):
    return lax.all_to_all(parts, AXES, 0, 0, tiled=True)


def call(body, outs, *args, name):
    vmem = pl.BlockSpec(memory_space=pltpu.VMEM)
    moved = sum(a.size for a in args) + sum(o.size for o in outs)
    return pl.pallas_call(
        body,
        out_shape=outs,
        in_specs=[vmem] * len(args),
        out_specs=[vmem] * len(outs),
        name=name,
        cost_estimate=pl.CostEstimate(flops=moved * 4, bytes_accessed=moved, transcendentals=0),
        compiler_params=pltpu.CompilerParams(vmem_limit_bytes=40 * 1024 * 1024),
    )(*args)


def shape(*dims):
    return jax.ShapeDtypeStruct(dims, F32)


def inner_at():
    return 1 - lax.rem(lax.axis_index("band"), 2)


def tile_is_odd():
    return lax.rem(lax.axis_index("tile"), 2) == 1


def put_rows(first, last, even_ref, odd_ref):
    odd = tile_is_odd()
    even_ref[...] = jnp.where(odd, first, last)
    odd_ref[...] = jnp.where(odd, last, first)


def take_rows(even_ref, odd_ref):
    odd = tile_is_odd()
    tile = lax.axis_index("tile")
    even, other = even_ref[...], odd_ref[...]
    above = jnp.where(tile == 0, 0.0, jnp.where(odd, even, other))
    below = jnp.where(tile == lax.axis_size("tile") - 1, 0.0, jnp.where(odd, other, even))
    return above, below


def row_at(width, at):
    return lax.broadcasted_iota(jnp.int32, (ROWS, width), 0) == at


def fold(total):
    width = total.shape[1]
    acc = total[:, :128]
    for at in range(128, width, 128):
        acc = acc + total[:, at : at + 128]
    return acc


def in_band(v_ref, cond_x_ref, at, cond_y, carried, below, k, chunks):
    width = v_ref.shape[-1]
    r = k * ROWS
    x = v_ref[r : r + ROWS, :]
    cx = cond_x_ref[at, r : r + ROWS, :]
    cy = cond_y[r : r + ROWS, :]
    after = below if k == chunks - 1 else v_ref[r + ROWS : r + ROWS + 1, :]
    down = jnp.where(row_at(width, ROWS - 1), after, pltpu.roll(x, ROWS - 1, 0))
    flux = cx * x
    up = jnp.where(row_at(width, 0), carried, pltpu.roll(flux, 1, 0))
    total = cx * down + up + cy * pltpu.roll(x, width - 1, 1) + pltpu.roll(cy * x, 1, 1)
    return x, total, flux[ROWS - 1 :, :]


def first_kernel(via_ref, mask_ref, cond_x_ref, link_ref, even_ref, odd_ref):
    local = via_ref.shape[0]
    top = lax.axis_index("band") * local + local - 1
    keep = jnp.where(top < NB - 1, 1.0, 0.0)
    link_ref[...] = via_ref[local - 1] * (mask_ref[local - 1].astype(F32) * keep)
    i = inner_at()
    rows = cond_x_ref.shape[1]
    last = jnp.concatenate([cond_x_ref[i, rows - 1 :, :], cond_x_ref[1 - i, rows - 1 :, :]], 0)
    put_rows(last, last, even_ref, odd_ref)


def prepare_kernel(
    cond_x_ref, cond_y_ref, via_ref, mask_ref, cap_ref, pad_ref, observe_ref, link_ref, near_ref, far_ref, even_ref, odd_ref,
    cy_ref, c_io_ref, c_in_ref, c_out_ref, diag_ref, inv_ref, s_i_ref, s_o_ref, edge_ref, s_even_ref, s_odd_ref,
):
    rows, width = s_i_ref.shape
    chunks = rows // ROWS
    i = inner_at()
    band = lax.axis_index("band")
    above, _ = take_rows(even_ref, odd_ref)
    edge_ref[...] = above
    lane = lax.broadcasted_iota(jnp.int32, (ROWS, width), 1)
    has_outer = jnp.where(jnp.logical_and(i == 1, band == 0), 0.0, 1.0)
    firsts, lasts = [], []
    carried = [above[0:1], above[1:2]]
    for k in range(chunks):
        rs = slice(k * ROWS, (k + 1) * ROWS)
        c_io = via_ref[0, rs, :] * mask_ref[0, rs, :].astype(F32)
        link = link_ref[rs, :]
        c_in = jnp.where(i == 1, link, near_ref[rs, :])
        c_out = jnp.where(i == 1, far_ref[rs, :] * has_outer, link)
        c_io_ref[rs, :] = c_io
        c_in_ref[rs, :] = c_in
        c_out_ref[rs, :] = c_out
        for side, at, to, out in ((0, i, c_in, s_i_ref), (1, 1 - i, c_out, s_o_ref)):
            cx = cond_x_ref[at, rs, :]
            cy = cond_y_ref[at, rs, :]
            cut = jnp.where(lane == width - 1, 0.0, cy)
            cy_ref[side, rs, :] = cut
            cx_up = jnp.where(row_at(width, 0), carried[side], pltpu.roll(cx, 1, 0))
            carried[side] = cx[ROWS - 1 :, :]
            diag = cap_ref[at, rs, :] + pad_conductance * pad_ref[at, rs, :].astype(F32)
            diag = diag + cx + cy + c_io + to + cx_up + pltpu.roll(cut, 1, 1)
            inv = 1.0 / diag
            diag_ref[side, rs, :] = diag
            inv_ref[side, rs, :] = inv
            s = observe_ref[0, at, rs, :] * inv
            out[rs, :] = s
            if k == 0:
                firsts.append(s[:1])
            if k == chunks - 1:
                lasts.append(s[ROWS - 1 :])
    put_rows(jnp.concatenate(firsts, 0), jnp.concatenate(lasts, 0), s_even_ref, s_odd_ref)


def spread_kernel(
    n_sums, u_i_ref, u_o_ref, near_ref, even_ref, odd_ref, cond_x_ref, cy_ref, c_io_ref, c_in_ref, inv_ref, edge_ref,
    v_i_ref, part_ref, sums_ref,
):
    rows, width = u_i_ref.shape
    chunks = rows // ROWS
    i = inner_at()
    above, below = take_rows(even_ref, odd_ref)
    flux = above * edge_ref[...]
    carry_i, carry_o = flux[0:1], flux[1:2]
    sums = [jnp.zeros((ROWS, width), F32) for _ in range(2)]
    for k in range(chunks):
        rs = slice(k * ROWS, (k + 1) * ROWS)
        x_i, part_i, carry_i = in_band(u_i_ref, cond_x_ref, i, cy_ref[0], carry_i, below[0:1], k, chunks)
        x_o, part_o, carry_o = in_band(u_o_ref, cond_x_ref, 1 - i, cy_ref[1], carry_o, below[1:2], k, chunks)
        c_io = c_io_ref[rs, :]
        part_i = part_i + c_io * x_o + c_in_ref[rs, :] * near_ref[rs, :]
        part_ref[rs, :] = part_o + c_io * x_i
        v_i = inv_ref[0, rs, :] * part_i
        v_i_ref[rs, :] = v_i
        sums[0] = sums[0] + x_i * part_i
        sums[1] = sums[1] + v_i * part_i
    sums_ref[0:ROWS, :] = fold(sums[0])
    sums_ref[ROWS : 2 * ROWS, :] = fold(sums[1])


def finish_kernel(
    u_o_ref, part_ref, far_ref, c_out_ref, inv_ref, v_i_ref, sums_ref,
    v_o_ref, even_ref, odd_ref, totals_ref,
):
    rows, width = u_o_ref.shape
    sums = [jnp.zeros((ROWS, width), F32) for _ in range(2)]
    for k in range(rows // ROWS):
        rs = slice(k * ROWS, (k + 1) * ROWS)
        part = part_ref[rs, :] + c_out_ref[rs, :] * far_ref[rs, :]
        v = inv_ref[1, rs, :] * part
        v_o_ref[rs, :] = v
        sums[0] = sums[0] + u_o_ref[rs, :] * part
        sums[1] = sums[1] + v * part
    totals_ref[0:ROWS, :] = fold(sums[0]) + sums_ref[0:ROWS, :]
    totals_ref[ROWS : 2 * ROWS, :] = fold(sums[1]) + sums_ref[ROWS : 2 * ROWS, :]
    put_rows(
        jnp.concatenate([v_i_ref[0:1, :], v_o_ref[0:1, :]], 0),
        jnp.concatenate([v_i_ref[rows - 1 :, :], v_o_ref[rows - 1 :, :]], 0),
        even_ref,
        odd_ref,
    )


def mail_kernel(t0_ref, t1_ref, t2_ref, mail_ref, *, picks):
    refs = (t0_ref, t1_ref, t2_ref)
    rows = [jnp.sum(refs[a][b * ROWS : (b + 1) * ROWS, :], 0, keepdims=True) for a, b in picks]
    block = jnp.concatenate(rows + rows, 0)
    for at in range(0, mail_ref.shape[0], ROWS):
        mail_ref[at : at + ROWS, :] = block


def weights(mail_ref):
    block = mail_ref[0:ROWS, :]
    for at in range(ROWS, mail_ref.shape[0], ROWS):
        block = block + mail_ref[at : at + ROWS, :]
    g = jnp.sum(block[0:4] + block[4:8], 1, keepdims=True)
    g0, g1, g2, g3 = (g[k : k + 1] for k in range(4))
    mu = g1 / g0
    h = g2 - mu * g1
    t = h / (h - (g3 - 2.0 * mu * g2 + mu * mu * g1))
    a = g0 / (g0 - g1 - h * t)
    b = t * a
    return a - mu * b, b


def step_kernel(
    mail_ref, s_i_ref, s_o_ref, v1_i_ref, v1_o_ref, v2_i_ref, v2_o_ref, v3_i_ref, v3_o_ref, cap_ref, observe_ref, diag_ref, inv_ref,
    x_ref, z_i_ref, z_o_ref, even_ref, odd_ref, sums_ref,
):
    rows, width = s_i_ref.shape
    i = inner_at()
    a, b = weights(mail_ref)
    total = jnp.zeros((ROWS, width), F32)
    for k in range(rows // ROWS):
        rs = slice(k * ROWS, (k + 1) * ROWS)
        for side, at, s_ref, p_ref, q_ref, r_ref, z_ref in (
            (0, i, s_i_ref, v1_i_ref, v2_i_ref, v3_i_ref, z_i_ref),
            (1, 1 - i, s_o_ref, v1_o_ref, v2_o_ref, v3_o_ref, z_o_ref),
        ):
            p, q = p_ref[rs, :], q_ref[rs, :]
            x = s_ref[rs, :] + a * p + b * q
            spread = p + a * q + b * r_ref[rs, :]
            x_ref[at, rs, :] = x
            residual = cap_ref[at, rs, :] * x + observe_ref[0, at, rs, :] - diag_ref[side, rs, :] * (x - spread)
            z = residual * inv_ref[side, rs, :]
            z_ref[rs, :] = z
            total = total + residual * z
    sums_ref[...] = fold(total)
    put_rows(
        jnp.concatenate([z_i_ref[0:1, :], z_o_ref[0:1, :]], 0),
        jnp.concatenate([z_i_ref[rows - 1 :, :], z_o_ref[rows - 1 :, :]], 0),
        even_ref,
        odd_ref,
    )


def last_kernel(mail_ref, x_ref, z_i_ref, z_o_ref, q_i_ref, q_o_ref, out_ref):
    rows, width = z_i_ref.shape
    i = inner_at()
    a, b = weights(mail_ref)
    for k in range(rows // ROWS):
        rs = slice(k * ROWS, (k + 1) * ROWS)
        for at, z_ref, q_ref in ((i, z_i_ref, q_i_ref), (1 - i, z_o_ref, q_o_ref)):
            x = x_ref[at, rs, :]
            out_ref[1, at, rs, :] = x
            out_ref[0, at, rs, :] = x + a * z_ref[rs, :] + b * q_ref[rs, :]


def on_device(cond_x, cond_y, via_cond, via_mask, capacitance, pad_mask, observe):
    bands, rows, width = cond_x.shape
    field, edge = shape(rows, width), shape(2, width)
    both = shape(bands, rows, width)
    n_devices = lax.axis_size("band") * lax.axis_size("tile")
    mail = shape(n_devices * 4, 128)
    two = shape(2 * ROWS, 128)
    one = shape(ROWS, 128)

    link, even, odd = call(first_kernel, [field, edge, edge], via_cond, via_mask, cond_x, name="links")
    far, near, even, odd = outer_swap(link), core_swap(link), even_swap(even), odd_swap(odd)
    cy, c_io, c_in, c_out, diag, inv, s_i, s_o, cx_edge, even, odd = call(
        prepare_kernel,
        [both, field, field, field, both, both, field, field, edge, edge, edge],
        cond_x, cond_y, via_cond, via_mask, capacitance, pad_mask, observe[1:2], link, near, far, even, odd,
        name="prepare",
    )

    def spread(u_i, u_o, even, odd, name):
        far, near, even, odd = outer_swap(u_o), core_swap(u_i), even_swap(even), odd_swap(odd)
        v_i, part, sums = call(
            lambda *refs: spread_kernel(2, *refs), [field, field, two],
            u_i, u_o, near, even, odd, cond_x, cy, c_io, c_in, inv, cx_edge, name=name + "_spread",
        )
        v_o, even, odd, totals = call(
            finish_kernel, [field, edge, edge, two], u_o, part, far, c_out, inv, v_i, sums, name=name + "_finish"
        )
        return v_i, v_o, even, odd, totals

    def send(t0, t1, t2, picks, name):
        (parts,) = call(
            lambda *refs: mail_kernel(*refs, picks=picks), [mail], t0, t1, t2, name=name
        )
        return all_total(parts)

    v1_i, v1_o, even, odd, t1 = spread(s_i, s_o, even, odd, "first")
    v2_i, v2_o, even, odd, t2 = spread(v1_i, v1_o, even, odd, "second")
    v3_i, v3_o, _, _, t3 = spread(v2_i, v2_o, even, odd, "third")
    got = send(t1, t2, t3, ((0, 1), (1, 0), (1, 1), (2, 0)), "later_mail")
    x, z_i, z_o, even, odd, t0 = call(
        step_kernel, [both, field, field, edge, edge, one],
        got, s_i, s_o, v1_i, v1_o, v2_i, v2_o, v3_i, v3_o, capacitance, observe[0:1], diag, inv, name="step",
    )
    q_i, q_o, even, odd, t1 = spread(z_i, z_o, even, odd, "fourth")
    _, _, _, _, t2 = spread(q_i, q_o, even, odd, "fifth")
    got = send(t0, t1, t2, ((0, 0), (1, 0), (1, 1), (2, 0)), "earlier_mail")
    (out,) = call(last_kernel, [shape(2, bands, rows, width)], got, x, z_i, z_o, q_i, q_o, name="last")
    return out


def solution(mesh):
    placed = (P("band", "tile", None),) * 6 + (P(None, "band", "tile", None),)
    return jax.shard_map(
        on_device,
        mesh=mesh,
        in_specs=placed,
        out_specs=P(None, "band", "tile", None),
        check_vma=False,
    )
```

```python
import jax
import jax.numpy as jnp
from jax import lax
from jax.experimental import pallas as pl
from jax.experimental.pallas import tpu as pltpu
from jax.sharding import PartitionSpec as P

NB = 8
ROWS = 8
AXES = ("band", "tile")
F32 = jnp.float32

pad_conductance = 4.0


def sizes():
    return lax.axis_size("band"), lax.axis_size("tile")


def core():
    return lax.rem(lax.axis_index("band"), 2)


def upper_chip():
    return lax.axis_index("band") >= 2


def core_swap(x):
    nb, _ = sizes()
    return lax.ppermute(x, "band", [(b, b ^ 1) for b in range(nb)])


def outer_swap(x):
    nb, _ = sizes()
    return lax.ppermute(x, "band", [(b, b ^ 2) for b in range(nb)])


def next_tile(x):
    _, nt = sizes()
    return lax.ppermute(x, "tile", [(t, (t + 1) % nt) for t in range(nt)])


def cross_swap(x):
    nb, nt = sizes()
    pairs = []
    for b in range(nb):
        for t in range(nt):
            other = (t + 1) % nt if b % 2 else (t - 1) % nt
            pairs.append((b * nt + t, (b ^ 1) * nt + other))
    return lax.ppermute(x, AXES, pairs)


def all_total(parts):
    return lax.all_to_all(parts, AXES, 0, 0, tiled=True)


def call(body, outs, *args, name, place=pltpu.VMEM, out_place=pltpu.VMEM, scratch=(), limit=10, cost=10):
    if place == pltpu.HBM:
        args = [pltpu.with_memory_space_constraint(a, pltpu.HBM) for a in args]
    return pl.pallas_call(
        body,
        out_shape=outs,
        in_specs=[pl.BlockSpec(memory_space=place)] * len(args),
        out_specs=[pl.BlockSpec(memory_space=out_place)] * len(outs),
        scratch_shapes=list(scratch),
        name=name,
        cost_estimate=pl.CostEstimate(flops=cost * 10**9, bytes_accessed=cost * 10**6, transcendentals=0),
        compiler_params=pltpu.CompilerParams(vmem_limit_bytes=limit * 1024 * 1024),
    )(*args)


def shape(*dims):
    return jax.ShapeDtypeStruct(dims, F32)


def row_at(width, at):
    return lax.broadcasted_iota(jnp.int32, (ROWS, width), 0) == at


def stack_rows(rows):
    return jnp.concatenate(rows, 0)


def put_rows(first, last, core_ref, cross_ref):
    lower = core() == 1
    core_ref[...] = jnp.where(lower, first, last)
    cross_ref[...] = jnp.where(lower, last, first)


def take_rows(core_ref, cross_ref):
    lower = core() == 1
    tile = lax.axis_index("tile")
    cross = cross_ref[...]
    near = core_ref[0 : cross.shape[0], :]
    above = jnp.where(lower, near, jnp.where(tile == 0, 0.0, cross))
    below = jnp.where(lower, jnp.where(tile == lax.axis_size("tile") - 1, 0.0, cross), near)
    return above, below


def fold(total):
    acc = total[:, :128]
    for at in range(128, total.shape[1], 128):
        acc = acc + total[:, at : at + 128]
    return acc


def band_of(u_o_ref, u_i_ref, j):
    return u_o_ref if j == 0 else u_i_ref.at[j - 1]


def in_band(v_ref, cx_ref, cy_ref, carried, below, k, chunks):
    width = v_ref.shape[-1]
    r = k * ROWS
    x = v_ref[r : r + ROWS, :]
    cx = cx_ref[r : r + ROWS, :]
    cy = cy_ref[r : r + ROWS, :]
    after = below if k == chunks - 1 else v_ref[r + ROWS : r + ROWS + 1, :]
    down = jnp.where(row_at(width, ROWS - 1), after, pltpu.roll(x, ROWS - 1, 0))
    flux = cx * x
    up = jnp.where(row_at(width, 0), carried, pltpu.roll(flux, 1, 0))
    total = cx * down + up + cy * pltpu.roll(x, width - 1, 1) + pltpu.roll(cy * x, 1, 1)
    return x, total, flux[ROWS - 1 :, :]


def couple(xs, parts, c_ref, rs):
    parts = list(parts)
    for j in range(1, len(xs)):
        c = c_ref[j, rs, :]
        parts[j] = parts[j] + c * xs[j - 1]
        parts[j - 1] = parts[j - 1] + c * xs[j]
    return parts


def half_of(which, half):
    return pl.ds(pl.multiple_of(which * half, ROWS), half)


def run_copies(pairs, sems):
    copies = [pltpu.make_async_copy(source, to, sems.at[n]) for n, (source, to) in enumerate(pairs)]
    for copy in copies:
        copy.start()
    for copy in copies:
        copy.wait()


def load_kernel(
    cond_x_ref, cond_y_ref, via_ref, mask_ref, cap_ref, pad_ref, observe_ref,
    mine_ref, send_ref, pay_mine_ref, pay_send_ref, last_ref, middle_ref, via_at, mask_at, pad_at, sems,
):
    half = send_ref.shape[1]
    me = core()
    pairs = [(via_ref, via_at), (mask_ref, mask_at), (pad_ref, pad_at)]
    halves = ((send_ref, pay_send_ref, 1 - me), (mine_ref, pay_mine_ref, me))
    for ref, _, which in halves:
        rs = half_of(which, half)
        pairs += [
            (cond_x_ref.at[:, rs, :], ref.at[0:2]),
            (cond_y_ref.at[:, rs, :], ref.at[2:4]),
            (observe_ref.at[1, :, rs, :], ref.at[8:10]),
            (cap_ref.at[:, rs, :], ref.at[10:12]),
            (observe_ref.at[0, :, rs, :], ref.at[12:14]),
        ]
    run_copies(pairs, sems)
    for ref, pay_ref, which in halves:
        rs = half_of(which, half)
        for band in range(2):
            ref[4 + band] = via_at[band, rs, :] * mask_at[band, rs, :].astype(F32)
            ref[6 + band] = ref[10 + band] + pad_conductance * pad_at[band, rs, :].astype(F32)
        pay_ref[...] = jnp.where(upper_chip(), ref[8], ref[5])
    for band in range(2):
        own, other = mine_ref[band, half - 1 :, :], send_ref[band, half - 1 :, :]
        last_ref[band : band + 1, :] = jnp.where(me == 1, own, other)
        middle_ref[band : band + 1, :] = jnp.where(me == 1, other, own)


def pay_kernel(mine_ref, got_ref, pay_ref):
    pay_ref[...] = jnp.where((core() == 1) == upper_chip(), got_ref[...], mine_ref[...])


def edge_kernel(middle_ref, before_ref, own_ref, send_ref):
    lower = core() == 1
    middle, before = middle_ref[...], before_ref[...]
    own_ref[...] = jnp.where(lower, middle, before)
    send_ref[...] = jnp.where(lower, before, middle)


def place_of(owner, band):
    n = 2 * owner + band
    return jnp.where(upper_chip(), n, 3 - n)


def prepare_kernel(
    mine_ref, got_ref, own_edge_ref, got_edge_ref, link_ref,
    cx_ref, cy_ref, c_ref, diag_ref, inv_i_ref, s_i_ref, inv_o_ref, s_o_ref, edge_ref, core_ref, cross_ref, cap_ref, seen_ref,
):
    half, width = s_o_ref.shape
    me = core()
    upper = upper_chip()
    lane = lax.broadcasted_iota(jnp.int32, (ROWS, width), 1)
    first_tile = jnp.logical_and(me == 0, lax.axis_index("tile") == 0)
    places = []
    for owner, ref, edges in ((me, mine_ref, own_edge_ref), (1 - me, got_ref, got_edge_ref)):
        for band in range(2):
            j = place_of(owner, band)
            places.append((j, ref, band))
            carried = jnp.where(first_tile, 0.0, edges[band : band + 1, :])
            edge_ref[pl.ds(j, 1), :] = carried
            cx_ref[j] = ref[band]
            cap_ref[j] = ref[10 + band]
            seen_ref[j] = ref[12 + band]
            via_at = jnp.where(upper, j + 1, j)

            @pl.when(via_at < 4)
            def _():
                c_ref[via_at] = ref[4 + band]

            for k in range(half // ROWS):
                rs = slice(k * ROWS, (k + 1) * ROWS)
                cx, cy, diag = (ref[2 * n + band, rs, :] for n in (0, 1, 3))
                cut = jnp.where(lane == width - 1, 0.0, cy)
                up = jnp.where(row_at(width, 0), carried, pltpu.roll(cx, 1, 0))
                carried = cx[ROWS - 1 :, :]
                cy_ref[j, rs, :] = cut
                diag_ref[j, rs, :] = diag + cx + cy + up + pltpu.roll(cut, 1, 1)

    @pl.when(upper)
    def _():
        c_ref[0] = link_ref[...]

    for j, ref, band in places:
        @pl.when(j == 0)
        def _():
            s_o_ref[...] = ref[8 + band]

        @pl.when(j > 0)
        def _():
            s_i_ref[j - 1] = ref[8 + band]

    for k in range(half // ROWS):
        rs = slice(k * ROWS, (k + 1) * ROWS)
        c = [c_ref[j, rs, :] for j in range(4)]
        for j in range(4):
            diag = diag_ref[j, rs, :] + c[j]
            if j < 3:
                diag = diag + c[j + 1]
            inv = 1.0 / diag
            diag_ref[j, rs, :] = diag
            band_of(inv_o_ref, inv_i_ref, j)[rs, :] = inv
            s_ref = band_of(s_o_ref, s_i_ref, j)
            s_ref[rs, :] = s_ref[rs, :] * inv
    ends = []
    for r in (0, half - 1):
        at = slice(r, r + 1)
        rows = [band_of(s_o_ref, s_i_ref, j)[at, :] for j in range(4)]
        ends.append(stack_rows(rows + [inv_o_ref[at, :], c_ref[0, at, :]]))
    put_rows(ends[0], ends[1], core_ref, cross_ref)


def own_parts(u_o_ref, u_i_ref, cx_ref, cy_ref, c_ref, pay_ref, scratch_ref):
    rows, width = u_o_ref.shape
    chunks = rows // ROWS
    none = jnp.zeros((1, width), F32)
    carried = none
    for k in range(chunks):
        rs = slice(k * ROWS, (k + 1) * ROWS)
        x, part, carried = in_band(u_o_ref, cx_ref.at[0], cy_ref.at[0], carried, none, k, chunks)
        pay_ref[rs, :] = x
        scratch_ref[rs, :] = part + c_ref[1, rs, :] * u_i_ref[0, rs, :]
    size = pay_ref.shape[0] - rows
    first = jnp.where(upper_chip(), 0, rows - size)
    pay_ref[rows:, :] = scratch_ref[pl.ds(pl.multiple_of(first, ROWS), size), :]


def spread_kernel(
    u_o_ref, u_i_ref, core_ref, cross_ref, cx_ref, cy_ref, c_ref, inv_i_ref, edge_ref,
    v_i_ref, part_ref, sums_ref, tail_ref=None, v_core_ref=None, v_cross_ref=None,
):
    rows, width = u_o_ref.shape
    chunks = rows // ROWS
    above, below = take_rows(core_ref, cross_ref)
    carried = [edge_ref[j : j + 1, :] * above[j : j + 1] for j in range(4)]
    sums = [jnp.zeros((ROWS, width), F32) for _ in range(2)]
    ends = [None, None]
    for k in range(chunks):
        rs = slice(k * ROWS, (k + 1) * ROWS)
        xs, parts = [], []
        for j in range(4):
            x, part, carried[j] = in_band(
                band_of(u_o_ref, u_i_ref, j), cx_ref.at[j], cy_ref.at[j], carried[j], below[j : j + 1], k, chunks
            )
            xs.append(x)
            parts.append(part)
        parts = couple(xs, parts, c_ref, rs)
        part_ref[rs, :] = parts[0]
        vs = [parts[0]]
        for j in range(1, 4):
            v = inv_i_ref[j - 1, rs, :] * parts[j]
            v_i_ref[j - 1, rs, :] = v
            sums[0] = sums[0] + xs[j] * parts[j]
            sums[1] = sums[1] + v * parts[j]
            vs.append(v)
        if k == 0:
            ends[0] = stack_rows([v[:1] for v in vs])
        if k == chunks - 1:
            ends[1] = stack_rows([v[ROWS - 1 :] for v in vs])
    sums_ref[0:ROWS, :] = fold(sums[0])
    sums_ref[ROWS : 2 * ROWS, :] = fold(sums[1])
    if tail_ref is not None:
        fluxes = [edge_ref[0:1, :] * above[0:1], cx_ref[0, rows - 1 :, :] * below[0:1]]
        tail_ref[...] = stack_rows([above[0:1], below[0:1], *fluxes, jnp.zeros((ROWS - 4, width), F32)])
        put_rows(ends[0], ends[1], v_core_ref, v_cross_ref)


def far_first_kernel(
    u_o_ref, part_ref, far_ref, c_ref, inv_ref, v_i_ref, sums_ref, cx_ref, cy_ref, v_ref, core_ref, cross_ref, total_ref, pay_ref,
    scratch_ref,
):
    rows, width = u_o_ref.shape
    total = jnp.zeros((ROWS, width), F32)
    for k in range(rows // ROWS):
        rs = slice(k * ROWS, (k + 1) * ROWS)
        part = part_ref[rs, :] + c_ref[0, rs, :] * far_ref[rs, :]
        v = inv_ref[rs, :] * part
        v_ref[rs, :] = v
        total = total + v * part
    total_ref[...] = fold(total) + sums_ref[ROWS : 2 * ROWS, :]
    ends = [
        stack_rows([v_ref[r : r + 1, :]] + [v_i_ref[j, r : r + 1, :] for j in range(3)]) for r in (0, rows - 1)
    ]
    put_rows(ends[0], ends[1], core_ref, cross_ref)
    own_parts(v_ref, v_i_ref, cx_ref, cy_ref, c_ref, pay_ref, scratch_ref)


def far_kernel(u_o_ref, part_ref, far_ref, c_ref, inv_ref, sums_ref, v_ref, totals_ref):
    rows, width = u_o_ref.shape
    sums = [jnp.zeros((ROWS, width), F32) for _ in range(2)]
    for k in range(rows // ROWS):
        rs = slice(k * ROWS, (k + 1) * ROWS)
        part = part_ref[rs, :] + c_ref[0, rs, :] * far_ref[rs, :]
        v = inv_ref[rs, :] * part
        v_ref[rs, :] = v
        sums[0] = sums[0] + u_o_ref[rs, :] * part
        sums[1] = sums[1] + v * part
    totals_ref[0:ROWS, :] = fold(sums[0]) + sums_ref[0:ROWS, :]
    totals_ref[ROWS : 2 * ROWS, :] = fold(sums[1]) + sums_ref[ROWS : 2 * ROWS, :]


def again_kernel(
    v_o_ref, v_i_ref, core_ref, cross_ref, cx_ref, cy_ref, c_ref, inv_i_ref, edge_ref,
    total_ref, w_i_ref=None, part_ref=None,
):
    rows, width = v_o_ref.shape
    chunks = rows // ROWS
    above, below = take_rows(core_ref, cross_ref)
    none = jnp.zeros((1, width), F32)
    carried = [none] + [edge_ref[j : j + 1, :] * above[j : j + 1] for j in range(1, 4)]
    after = [none] + [below[j : j + 1] for j in range(1, 4)]
    total = jnp.zeros((ROWS, width), F32)
    for k in range(chunks):
        rs = slice(k * ROWS, (k + 1) * ROWS)
        xs, parts = [], []
        for j in range(4):
            x, part, carried[j] = in_band(
                band_of(v_o_ref, v_i_ref, j), cx_ref.at[j], cy_ref.at[j], carried[j], after[j], k, chunks
            )
            xs.append(x)
            parts.append(part)
        parts = couple(xs, parts, c_ref, rs)
        for x, part in zip(xs, parts):
            total = total + x * part
        if w_i_ref is not None:
            part_ref[rs, :] = parts[0]
            for j in range(1, 4):
                w_i_ref[j - 1, rs, :] = inv_i_ref[j - 1, rs, :] * parts[j]
    total_ref[...] = fold(total)


def cross_kernel(
    u_ref, v_ref, got_ref, tail_ref, core_ref, cross_ref, inv_far_ref, c_ref, cx_ref, edge_ref, side_core_ref, side_cross_ref,
    t0_ref, t1_ref, t2_ref, mail_ref, part_ref=None, inv_ref=None, w_ref=None,
):
    rows, width = u_ref.shape
    size = got_ref.shape[0] - rows
    chunks = size // ROWS
    first = jnp.where(upper_chip(), rows - size, 0)
    above, below = take_rows(core_ref, cross_ref)
    side_above, side_below = take_rows(side_core_ref, side_cross_ref)
    up = side_above[4:5] * (above[0:1] + side_above[5:6] * tail_ref[0:1, :])
    down = side_below[4:5] * (below[0:1] + side_below[5:6] * tail_ref[1:2, :])
    up = edge_ref[0:1, :] * up
    down = cx_ref[0, rows - 1 :, :] * down
    far_up = jnp.where(first == 0, tail_ref[2:3, :], 0.0)
    far_down = jnp.where(first + size == rows, tail_ref[3:4, :], 0.0)
    total = jnp.zeros((ROWS, width), F32)
    for k in range(chunks):
        rs = slice(k * ROWS, (k + 1) * ROWS)
        at = pl.ds(pl.multiple_of(first + k * ROWS, ROWS), ROWS)
        c_out = c_ref[0, at, :]
        part = got_ref[rows + k * ROWS : rows + (k + 1) * ROWS, :] + c_out * u_ref[at, :]
        if k == 0:
            part = part + jnp.where(row_at(width, 0), far_up, 0.0)
        if k == chunks - 1:
            part = part + jnp.where(row_at(width, ROWS - 1), far_down, 0.0)
        flow = c_out * (inv_far_ref[at, :] * part)
        total = total + v_ref[at, :] * flow
        if w_ref is not None:
            part = part_ref[rs, :] + flow
            if k == 0:
                part = part + jnp.where(row_at(width, 0), up, 0.0)
            if k == chunks - 1:
                part = part + jnp.where(row_at(width, ROWS - 1), down, 0.0)
            w_ref[rs, :] = inv_ref[rs, :] * part
    ends = up * v_ref[0:1, :] + down * v_ref[rows - 1 :, :]
    last = fold((rows // size) * total + jnp.where(row_at(width, 0), ends, 0.0)) + t2_ref[...]
    terms = (t0_ref[...], t1_ref[0:ROWS, :], t1_ref[ROWS : 2 * ROWS, :], last)
    lines = [jnp.sum(t, 0, keepdims=True) for t in terms]
    block = jnp.concatenate(lines + lines, 0)
    for at in range(0, mail_ref.shape[0], ROWS):
        mail_ref[at : at + ROWS, :] = block


def weights(mail_ref):
    block = mail_ref[0:ROWS, :]
    for at in range(ROWS, mail_ref.shape[0], ROWS):
        block = block + mail_ref[at : at + ROWS, :]
    g = jnp.sum(block[0:4] + block[4:8], 1, keepdims=True)
    g0, g1, g2, g3 = (g[k : k + 1] for k in range(4))
    mu = g1 / g0
    h = g2 - mu * g1
    t = h / (h - (g3 - 2.0 * mu * g2 + mu * mu * g1))
    a = g0 / (g0 - g1 - h * t)
    b = t * a
    return a - mu * b, b


def hand_out(j, value, k, mine_ref, send_ref, first, half):
    n = jnp.where(upper_chip(), j, 3 - j)
    owner, band = n // 2, lax.rem(n, 2)
    size = value.shape[0]

    @pl.when(owner == core())
    def _():
        mine_ref[band, k * ROWS : k * ROWS + size, :] = value

    @pl.when(owner != core())
    def _():
        send_ref[pl.ds(pl.multiple_of(first + band * half + k * ROWS, ROWS), size), :] = value


def step_kernel(
    mail_ref, s_o_ref, s_i_ref, v1_o_ref, v1_i_ref, v2_o_ref, v2_i_ref, v3_o_ref, v3_i_ref, cap_ref, seen_ref,
    diag_ref, inv_o_ref, inv_i_ref, cx_ref, cy_ref, c_ref,
    z_o_ref, z_i_ref, core_ref, cross_ref, total_ref, pay_ref, x_mine_ref, z_mine_ref, scratch_ref,
):
    rows, width = s_o_ref.shape
    chunks = rows // ROWS
    a, b = weights(mail_ref)
    total = jnp.zeros((ROWS, width), F32)
    firsts, lasts = [], []
    for j in range(4):
        for k in range(chunks):
            rs = slice(k * ROWS, (k + 1) * ROWS)
            s, p, q, r, inv = (
                band_of(o, i, j)[rs, :]
                for o, i in (
                    (s_o_ref, s_i_ref), (v1_o_ref, v1_i_ref), (v2_o_ref, v2_i_ref), (v3_o_ref, v3_i_ref),
                    (inv_o_ref, inv_i_ref),
                )
            )
            x = s + a * p + b * q
            residual = cap_ref[j, rs, :] * x + seen_ref[j, rs, :] - diag_ref[j, rs, :] * (x - (p + a * q + b * r))
            z = residual * inv
            band_of(z_o_ref, z_i_ref, j)[rs, :] = z
            total = total + residual * z
            hand_out(j, x, k, x_mine_ref, core_ref, ROWS, rows)
            hand_out(j, z, k, z_mine_ref, core_ref, ROWS + 2 * rows, rows)
            if k == 0:
                firsts.append(z[:1])
            if k == chunks - 1:
                lasts.append(z[ROWS - 1 :])
    total_ref[...] = fold(total)
    none = jnp.zeros((4, width), F32)
    put_rows(stack_rows(firsts + [none]), stack_rows(lasts + [none]), core_ref.at[0:ROWS], cross_ref)
    own_parts(z_o_ref, z_i_ref, cx_ref, cy_ref, c_ref, pay_ref, scratch_ref)


def give_kernel(q_o_ref, q_i_ref, mine_ref, send_ref):
    rows = q_o_ref.shape[0]
    for j in range(4):
        hand_out(j, band_of(q_o_ref, q_i_ref, j)[...], 0, mine_ref, send_ref, 0, rows)


def last_kernel(mail_ref, x_mine_ref, z_mine_ref, got_ref, q_mine_ref, q_got_ref, out_ref, answer, sems):
    half = x_mine_ref.shape[1]
    places = []
    for band in range(2):
        mine = [ref.at[band] for ref in (x_mine_ref, z_mine_ref, q_mine_ref)]
        places.append((band, core(), mine))
        at = ROWS + band * half
        got = [got_ref.at[at : at + half], got_ref.at[at + 2 * half : at + 3 * half]]
        places.append((band, 1 - core(), got + [q_got_ref.at[band * half : (band + 1) * half]]))
    copies = []
    for n, (band, which, (x_ref, _, _)) in enumerate(places):
        copies.append(pltpu.make_async_copy(x_ref, out_ref.at[1, band, half_of(which, half), :], sems.at[n]))
        copies[-1].start()
    a, b = weights(mail_ref)
    for n, (band, which, (x_ref, z_ref, q_ref)) in enumerate(places):
        answer[n] = x_ref[...] + a * z_ref[...] + b * q_ref[...]
        copies.append(
            pltpu.make_async_copy(answer.at[n], out_ref.at[0, band, half_of(which, half), :], sems.at[4 + n])
        )
        copies[-1].start()
    for copy in copies:
        copy.wait()


def on_device(cond_x, cond_y, via_cond, via_mask, capacitance, pad_mask, observe):
    _, rows, width = cond_x.shape
    half = rows // 2
    field, three, four, edge = shape(half, width), shape(3, half, width), shape(4, half, width), shape(4, width)
    six, rim, pair = shape(6, width), shape(2, width), shape(2, half, width)
    mail = shape(lax.axis_size("band") * lax.axis_size("tile") * 4, 128)
    one, two = shape(ROWS, 128), shape(2 * ROWS, 128)
    fourteen = shape(14, half, width)
    whole, whole_int = pltpu.VMEM((2, rows, width), F32), pltpu.VMEM((2, rows, width), jnp.int32)
    own, send, pay, pay_send, last, middle = call(
        load_kernel, [fourteen, fourteen, field, field, rim, rim],
        cond_x, cond_y, via_cond, via_mask, capacitance, pad_mask, observe, name="load", place=pltpu.HBM,
        scratch=[whole, whole_int, whole_int, pltpu.SemaphoreType.DMA((13,))],
    )
    got, before = core_swap(pay_send), next_tile(last)
    got, send = lax.optimization_barrier((got, send))
    (pay,) = call(pay_kernel, [field], pay, got, name="pay")
    link, traded = outer_swap(pay), core_swap(send)
    own_edge, send_edge = call(edge_kernel, [rim, rim], middle, before, name="edges")
    got_edge = core_swap(send_edge)
    cx, cy, c, diag, inv_i, s_i, inv_o, s_o, cx_edge, near, cross, cap, earlier = call(
        prepare_kernel, [four, four, four, four, three, three, field, field, edge, six, six, four, four],
        own, traded, own_edge, got_edge, link, name="prepare",
    )
    far, sides = outer_swap(s_o), (core_swap(near), cross_swap(cross))
    inv_far = outer_swap(inv_o)

    coeffs = (cx, cy, c, inv_i, cx_edge)
    parts_of = [pltpu.VMEM((half, width), F32)]
    v1_i, part, sums = call(spread_kernel, [three, field, two], s_o, s_i, *sides, *coeffs, name="first_spread", cost=0)
    v1_i, inv_far = lax.optimization_barrier((v1_i, inv_far))
    v1_o, near, cross, t0, pay = call(
        far_first_kernel, [field, edge, edge, one, shape(2 * half, width)],
        s_o, part, far, c, inv_o, v1_i, sums, cx, cy, name="first_far", scratch=parts_of,
    )

    def stage(u_o, u_i, pay, near, cross, t0, inv_far, name):
        got, cross, near = outer_swap(pay), cross_swap(cross), core_swap(near)
        whole = pay.shape[0] == 2 * half
        near, cross, inv_far = lax.optimization_barrier((near, cross, inv_far))
        held = near
        v_i, part, sums, tail, near, cross = call(
            spread_kernel, [three, field, two, shape(ROWS, width), edge, edge],
            u_o, u_i, near, cross, *coeffs, name=name + "_spread", cost=0,
        )
        cross, tail, near = cross_swap(cross), outer_swap(tail), core_swap(near)
        v_o, t1 = call(far_kernel, [field, two], u_o, part, got, c, inv_o, sums, name=name + "_far")
        given = ()
        if not whole:
            mine, send = call(give_kernel, [pair, shape(2 * half, width)], v_o, v_i, name="give")
            given = mine, core_swap(send)
        t2, *rest = call(
            again_kernel, [one] + [three, field] * whole, v_o, v_i, near, cross, *coeffs, name=name + "_again"
        )
        args = [u_o, v_o, got, tail, near, cross, inv_far, c, cx, cx_edge, *sides, t0, t1, t2]

        def finish(*refs):
            n = len(args)
            cross_kernel(*refs[:n], *((refs[n + 2], *refs[n : n + 2], refs[n + 3]) if whole else refs[n:]))

        more_args = [rest[1], inv_o] if whole else []
        parts, *w_o = call(finish, [mail] + [field] * whole, *args, *more_args, name=name + "_cross")
        parts, given = lax.optimization_barrier((parts, given))
        return v_o, v_i, all_total(parts), inv_far, held, given, (*w_o, *rest[:1])

    v2_o, v2_i, total, inv_far, _, _, (v3_o, v3_i) = stage(v1_o, v1_i, pay, near, cross, t0, inv_far, "later")
    z_o, z_i, near, cross, t0, pay, x_mine, z_mine = call(
        step_kernel,
        [field, three, shape(ROWS + 4 * half, width), shape(ROWS, width), one, shape(half + half // 2, width), pair, pair],
        total, s_o, s_i, v1_o, v1_i, v2_o, v2_i, v3_o, v3_i, cap, earlier, diag, inv_o, inv_i, cx, cy, c,
        name="step", scratch=parts_of,
    )
    _, _, total, _, got, given, _ = stage(z_o, z_i, pay, near, cross, t0, inv_far, "earlier")
    (out,) = call(
        last_kernel, [shape(2, 2, rows, width)], total, x_mine, z_mine, got, *given, name="last", out_place=pl.ANY,
        scratch=[pltpu.VMEM((4, half, width), F32), pltpu.SemaphoreType.DMA((8,))],
    )
    return out


def solution(mesh):
    placed = (P("band", "tile", None),) * 6 + (P(None, "band", "tile", None),)
    return jax.shard_map(
        on_device,
        mesh=mesh,
        in_specs=placed,
        out_specs=P(None, "band", "tile", None),
        check_vma=False,
    )
```

```python
import jax
import jax.numpy as jnp
from jax import lax
from jax.experimental import pallas as pl
from jax.experimental.pallas import tpu as pltpu
from jax.sharding import PartitionSpec as P

NB = 8
ROWS = 8
AXES = ("band", "tile")
F32 = jnp.float32

pad_conductance = 4.0


def sizes():
    return lax.axis_size("band"), lax.axis_size("tile")


def core():
    return lax.rem(lax.axis_index("band"), 2)


def upper_chip():
    return lax.axis_index("band") >= 2


def core_swap(x):
    nb, _ = sizes()
    return lax.ppermute(x, "band", [(b, b ^ 1) for b in range(nb)])


def outer_swap(x):
    nb, _ = sizes()
    return lax.ppermute(x, "band", [(b, b ^ 2) for b in range(nb)])


def cross_swap(x):
    nb, nt = sizes()
    pairs = []
    for b in range(nb):
        for t in range(nt):
            other = (t + 1) % nt if b % 2 else (t - 1) % nt
            pairs.append((b * nt + t, (b ^ 1) * nt + other))
    return lax.ppermute(x, AXES, pairs)


def all_total(parts):
    return lax.all_to_all(parts, AXES, 0, 0, tiled=True)


def call(body, outs, *args, name, place=pltpu.VMEM, out_place=pltpu.VMEM, scratch=(), limit=10, cost=10):
    if place == pltpu.HBM:
        args = [pltpu.with_memory_space_constraint(a, pltpu.HBM) for a in args]
    return pl.pallas_call(
        body,
        out_shape=outs,
        in_specs=[pl.BlockSpec(memory_space=place)] * len(args),
        out_specs=[pl.BlockSpec(memory_space=out_place)] * len(outs),
        scratch_shapes=list(scratch),
        name=name,
        cost_estimate=pl.CostEstimate(flops=cost * 10**9, bytes_accessed=cost * 10**6, transcendentals=0),
        compiler_params=pltpu.CompilerParams(vmem_limit_bytes=limit * 1024 * 1024),
    )(*args)


def shape(*dims):
    return jax.ShapeDtypeStruct(dims, F32)


def row_at(width, at):
    return lax.broadcasted_iota(jnp.int32, (ROWS, width), 0) == at


def stack_rows(rows):
    return jnp.concatenate(rows, 0)


def put_rows(first, last, core_ref, cross_ref):
    lower = core() == 1
    core_ref[...] = jnp.where(lower, first, last)
    cross_ref[...] = jnp.where(lower, last, first)


def put_two_rows(u_o_ref, u_i_ref, core_ref, cross_ref):
    rows = u_o_ref.shape[0]
    ends = [
        stack_rows([band_of(u_o_ref, u_i_ref, j)[r : r + 1, :] for r in pair for j in range(4)])
        for pair in ((0, 1), (rows - 1, rows - 2))
    ]
    put_rows(ends[0], ends[1], core_ref, cross_ref)


def take_rows(core_ref, cross_ref):
    lower = core() == 1
    tile = lax.axis_index("tile")
    cross = cross_ref[...]
    near = core_ref[0 : cross.shape[0], :]
    above = jnp.where(lower, near, jnp.where(tile == 0, 0.0, cross))
    below = jnp.where(lower, jnp.where(tile == lax.axis_size("tile") - 1, 0.0, cross), near)
    return above, below


def fold(total):
    acc = total[:, :128]
    for at in range(128, total.shape[1], 128):
        acc = acc + total[:, at : at + 128]
    return acc


def band_of(u_o_ref, u_i_ref, j):
    return u_o_ref if j == 0 else u_i_ref.at[j - 1]


def in_band(v_ref, cx_ref, cy_ref, carried, below, k, chunks):
    width = v_ref.shape[-1]
    r = k * ROWS
    x = v_ref[r : r + ROWS, :]
    cx = cx_ref[r : r + ROWS, :]
    cy = cy_ref[r : r + ROWS, :]
    after = below if k == chunks - 1 else v_ref[r + ROWS : r + ROWS + 1, :]
    down = jnp.where(row_at(width, ROWS - 1), after, pltpu.roll(x, ROWS - 1, 0))
    flux = cx * x
    up = jnp.where(row_at(width, 0), carried, pltpu.roll(flux, 1, 0))
    total = cx * down + up + cy * pltpu.roll(x, width - 1, 1) + pltpu.roll(cy * x, 1, 1)
    return x, total, flux[ROWS - 1 :, :]


def couple(xs, parts, c_ref, rs):
    parts = list(parts)
    for j in range(1, len(xs)):
        c = c_ref[j, rs, :]
        parts[j] = parts[j] + c * xs[j - 1]
        parts[j - 1] = parts[j - 1] + c * xs[j]
    return parts


def half_of(which, half):
    return pl.ds(pl.multiple_of(which * half, ROWS), half)


def run_copies(pairs, sems):
    copies = [pltpu.make_async_copy(source, to, sems.at[n]) for n, (source, to) in enumerate(pairs)]
    for copy in copies:
        copy.start()
    for copy in copies:
        copy.wait()


def load_kernel(
    cond_x_ref, cond_y_ref, via_ref, mask_ref, cap_ref, pad_ref, observe_ref,
    mine_ref, send_ref, pay_mine_ref, pay_send_ref, last_ref, middle_ref, via_at, mask_at, pad_at, sems,
):
    half = send_ref.shape[1]
    me = core()
    pairs = [(via_ref, via_at), (mask_ref, mask_at), (pad_ref, pad_at)]
    halves = ((send_ref, pay_send_ref, 1 - me), (mine_ref, pay_mine_ref, me))
    for ref, _, which in halves:
        rs = half_of(which, half)
        pairs += [
            (cond_x_ref.at[:, rs, :], ref.at[0:2]),
            (cond_y_ref.at[:, rs, :], ref.at[2:4]),
            (observe_ref.at[1, :, rs, :], ref.at[8:10]),
            (cap_ref.at[:, rs, :], ref.at[10:12]),
            (observe_ref.at[0, :, rs, :], ref.at[12:14]),
        ]
    run_copies(pairs, sems)
    for ref, pay_ref, which in halves:
        rs = half_of(which, half)
        for band in range(2):
            ref[4 + band] = via_at[band, rs, :] * mask_at[band, rs, :].astype(F32)
            ref[6 + band] = ref[10 + band] + pad_conductance * pad_at[band, rs, :].astype(F32)
        pay_ref[0:half, :] = jnp.where(upper_chip(), ref[8], ref[5])
    for band in range(2):
        own, other = mine_ref[band, half - 1 :, :], send_ref[band, half - 1 :, :]
        last_ref[band : band + 1, :] = jnp.where(me == 1, own, other)
        middle_ref[band : band + 1, :] = jnp.where(me == 1, other, own)
    none = jnp.zeros((ROWS - 4, middle_ref.shape[1]), F32)
    pay_send_ref[half:, :] = stack_rows([middle_ref[...], last_ref[...], none])


def pay_kernel(mine_ref, got_ref, last_ref, pay_ref, all_last_ref):
    pay_ref[...] = jnp.where((core() == 1) == upper_chip(), got_ref[0 : pay_ref.shape[0], :], mine_ref[...])
    half = pay_ref.shape[0]
    own, other = last_ref[...], got_ref[half + 2 : half + 4, :]
    all_last_ref[...] = stack_rows([jnp.where(core() == 0, own, other), jnp.where(core() == 0, other, own)])


def place_of(owner, band):
    n = 2 * owner + band
    return jnp.where(upper_chip(), n, 3 - n)


def prepare_kernel(
    mine_ref, got_ref, link_ref, middle_ref, more_ref, last_ref,
    cx_ref, cy_ref, c_ref, diag_ref, inv_i_ref, s_i_ref, inv_o_ref, s_o_ref, edge_ref, core_ref, cross_ref, cap_ref, seen_ref,
):
    half, width = s_o_ref.shape
    me = core()
    upper = upper_chip()
    lane = lax.broadcasted_iota(jnp.int32, (ROWS, width), 1)
    first_tile = jnp.logical_and(me == 0, lax.axis_index("tile") == 0)
    places = []
    own_edge = jnp.where(me == 1, middle_ref[...], last_ref[0:2, :])
    got_edge = jnp.where(me == 1, more_ref[half : half + 2, :], last_ref[2:4, :])
    for owner, ref, edges in ((me, mine_ref, own_edge), (1 - me, got_ref, got_edge)):
        for band in range(2):
            j = place_of(owner, band)
            places.append((j, ref, band))
            carried = jnp.where(first_tile, 0.0, edges[band : band + 1, :])
            edge_ref[pl.ds(j, 1), :] = carried
            cx_ref[j] = ref[band]
            cap_ref[j] = ref[10 + band]
            seen_ref[j] = ref[12 + band]
            via_at = jnp.where(upper, j + 1, j)

            @pl.when(via_at < 4)
            def _():
                c_ref[via_at] = ref[4 + band]

            for k in range(half // ROWS):
                rs = slice(k * ROWS, (k + 1) * ROWS)
                cx, cy, diag = (ref[2 * n + band, rs, :] for n in (0, 1, 3))
                cut = jnp.where(lane == width - 1, 0.0, cy)
                up = jnp.where(row_at(width, 0), carried, pltpu.roll(cx, 1, 0))
                carried = cx[ROWS - 1 :, :]
                cy_ref[j, rs, :] = cut
                diag_ref[j, rs, :] = diag + cx + cy + up + pltpu.roll(cut, 1, 1)

    @pl.when(upper)
    def _():
        c_ref[0] = link_ref[...]

    for j, ref, band in places:
        @pl.when(j == 0)
        def _():
            s_o_ref[...] = ref[8 + band]

        @pl.when(j > 0)
        def _():
            s_i_ref[j - 1] = ref[8 + band]

    for k in range(half // ROWS):
        rs = slice(k * ROWS, (k + 1) * ROWS)
        c = [c_ref[j, rs, :] for j in range(4)]
        for j in range(4):
            diag = diag_ref[j, rs, :] + c[j]
            if j < 3:
                diag = diag + c[j + 1]
            inv = 1.0 / diag
            diag_ref[j, rs, :] = diag
            band_of(inv_o_ref, inv_i_ref, j)[rs, :] = inv
            s_ref = band_of(s_o_ref, s_i_ref, j)
            s_ref[rs, :] = s_ref[rs, :] * inv
    ends = []
    for r, beyond in ((0, 0), (half - 1, half - 2)):
        at = slice(r, r + 1)
        rows = [band_of(s_o_ref, s_i_ref, j)[at, :] for j in range(4)]
        rows += [band_of(inv_o_ref, inv_i_ref, j)[at, :] for j in range(4)]
        for ref, row in ((cy_ref, r), (c_ref, r), (cx_ref, beyond)):
            rows += [ref[j, row : row + 1, :] for j in range(4)]
        ends.append(stack_rows(rows))
    put_rows(ends[0], ends[1], core_ref, cross_ref)


def own_parts(u_o_ref, u_i_ref, cx_ref, cy_ref, c_ref, pay_ref, scratch_ref):
    rows, width = u_o_ref.shape
    chunks = rows // ROWS
    none = jnp.zeros((1, width), F32)
    carried = none
    for k in range(chunks):
        rs = slice(k * ROWS, (k + 1) * ROWS)
        x, part, carried = in_band(u_o_ref, cx_ref.at[0], cy_ref.at[0], carried, none, k, chunks)
        pay_ref[rs, :] = x
        scratch_ref[rs, :] = part + c_ref[1, rs, :] * u_i_ref[0, rs, :]
    size = rows // 2
    first = jnp.where(upper_chip(), 0, rows - size)
    pay_ref[rows : rows + size, :] = scratch_ref[pl.ds(pl.multiple_of(first, ROWS), size), :]


def spread_kernel(
    u_o_ref, u_i_ref, core_ref, cross_ref, cx_ref, cy_ref, c_ref, inv_i_ref, edge_ref, v_i_ref, part_ref, sums_ref
):
    above, below = take_rows(core_ref, cross_ref)
    spread_rows(u_o_ref, u_i_ref, above, below, cx_ref, cy_ref, c_ref, inv_i_ref, edge_ref, v_i_ref, part_ref, sums_ref)


def spread_rows(u_o_ref, u_i_ref, above, below, cx_ref, cy_ref, c_ref, inv_i_ref, edge_ref, v_i_ref, part_ref, sums_ref):
    rows, width = u_o_ref.shape
    chunks = rows // ROWS
    carried = [edge_ref[j : j + 1, :] * above[j : j + 1] for j in range(4)]
    sums = [jnp.zeros((ROWS, width), F32) for _ in range(2)]
    for k in range(chunks):
        rs = slice(k * ROWS, (k + 1) * ROWS)
        xs, parts = [], []
        for j in range(4):
            x, part, carried[j] = in_band(
                band_of(u_o_ref, u_i_ref, j), cx_ref.at[j], cy_ref.at[j], carried[j], below[j : j + 1], k, chunks
            )
            xs.append(x)
            parts.append(part)
        parts = couple(xs, parts, c_ref, rs)
        part_ref[rs, :] = parts[0]
        for j in range(1, 4):
            v = inv_i_ref[j - 1, rs, :] * parts[j]
            v_i_ref[j - 1, rs, :] = v
            sums[0] = sums[0] + xs[j] * parts[j]
            sums[1] = sums[1] + v * parts[j]
    sums_ref[0:ROWS, :] = fold(sums[0])
    sums_ref[ROWS : 2 * ROWS, :] = fold(sums[1])


def beside(u_o_ref, u_i_ref, above, below, side_above, side_below, edge_ref, cx_ref):
    rows, width = u_o_ref.shape
    here = stack_rows([above[0:4], below[0:4]])
    beyond = stack_rows([above[4:8], below[4:8]])
    inside = [band_of(u_o_ref, u_i_ref, j)[r : r + 1, :] for r in (0, rows - 1) for j in range(4)]
    toward = stack_rows([edge_ref[...]] + [cx_ref[j, rows - 1 :, :] for j in range(4)])
    inv, cy, c, away = (stack_rows([side_above[n : n + 4], side_below[n : n + 4]]) for n in (4, 8, 12, 16))
    c = jnp.where(jnp.logical_or(row_at(width, 0), row_at(width, 4)), 0.0, c)
    total = toward * stack_rows(inside) + away * beyond
    total = total + cy * pltpu.roll(here, width - 1, 1) + pltpu.roll(cy * here, 1, 1)
    return total + c * pltpu.roll(here, 1, 0) + pltpu.roll(c * here, ROWS - 1, 0), inv


def two_spread_kernel(
    u_o_ref, u_i_ref, core_ref, cross_ref, cx_ref, cy_ref, c_ref, inv_i_ref, edge_ref, side_core_ref, side_cross_ref,
    v_i_ref, part_ref, sums_ref, tail_ref, beside_ref, total_ref, w_ref=None,
):
    rows, width = u_o_ref.shape
    chunks = rows // ROWS
    above, below = take_rows(core_ref, cross_ref)
    spread_rows(u_o_ref, u_i_ref, above, below, cx_ref, cy_ref, c_ref, inv_i_ref, edge_ref, v_i_ref, part_ref, sums_ref)
    fluxes = [edge_ref[0:1, :] * above[0:1], cx_ref[0, rows - 1 :, :] * below[0:1]]
    tail_ref[...] = stack_rows([above[0:1], below[0:1], *fluxes, jnp.zeros((ROWS - 4, width), F32)])
    side_above, side_below = take_rows(side_core_ref, side_cross_ref)
    parts_there, inv = beside(u_o_ref, u_i_ref, above, below, side_above, side_below, edge_ref, cx_ref)
    beside_ref[...] = parts_there
    v_there = inv * parts_there
    carried = [edge_ref[j : j + 1, :] * v_there[j : j + 1] for j in range(1, 4)]
    total = jnp.zeros((ROWS, width), F32)
    for k in range(chunks):
        rs = slice(k * ROWS, (k + 1) * ROWS)
        xs, parts = [], []
        for j in range(1, 4):
            x, part, carried[j - 1] = in_band(
                v_i_ref.at[j - 1], cx_ref.at[j], cy_ref.at[j], carried[j - 1], v_there[4 + j : 5 + j], k, chunks
            )
            xs.append(x)
            parts.append(part)
        parts = couple(xs, parts, c_ref.at[pl.ds(1, 3)], rs)
        for j in range(3):
            total = total + xs[j] * parts[j]
            if w_ref is not None:
                w_ref[j, rs, :] = parts[j]
    total_ref[...] = fold(total)


def far_first_kernel(
    u_o_ref, part_ref, far_ref, c_ref, inv_ref, v_i_ref, sums_ref, cx_ref, cy_ref, v_ref, core_ref, cross_ref, total_ref, pay_ref,
    scratch_ref,
):
    rows, width = u_o_ref.shape
    total = jnp.zeros((ROWS, width), F32)
    for k in range(rows // ROWS):
        rs = slice(k * ROWS, (k + 1) * ROWS)
        part = part_ref[rs, :] + c_ref[0, rs, :] * far_ref[rs, :]
        v = inv_ref[rs, :] * part
        v_ref[rs, :] = v
        total = total + v * part
    total_ref[...] = fold(total) + sums_ref[ROWS : 2 * ROWS, :]
    put_two_rows(v_ref, v_i_ref, core_ref, cross_ref)
    own_parts(v_ref, v_i_ref, cx_ref, cy_ref, c_ref, pay_ref, scratch_ref)
    size = rows // 2
    first = pl.multiple_of(jnp.where(upper_chip(), 0, rows - size), ROWS)
    pay_ref[rows + size :, :] = inv_ref[pl.ds(first, size), :]


def finish_kernel(
    u_o_ref, got_ref, tail_ref, v_i_ref, part_ref, sums_ref, beside_ref, inner_ref, inv_far_ref,
    cx_ref, cy_ref, c_ref, inv_ref, edge_ref, side_core_ref, side_cross_ref, t0_ref,
    mail_ref, v_ref, *more,
):
    rows, width = u_o_ref.shape
    chunks = rows // ROWS
    none = jnp.zeros((1, width), F32)
    sums = [jnp.zeros((ROWS, width), F32) for _ in range(4)]
    for k in range(chunks):
        rs = slice(k * ROWS, (k + 1) * ROWS)
        part = part_ref[rs, :] + c_ref[0, rs, :] * got_ref[rs, :]
        v = inv_ref[rs, :] * part
        v_ref[rs, :] = v
        sums[0] = sums[0] + u_o_ref[rs, :] * part
        sums[1] = sums[1] + v * part
    if len(more) == 2:
        w_ref, fix_ref = more
    else:
        w_ref = fix_ref = None
    carried = none
    for k in range(chunks):
        rs = slice(k * ROWS, (k + 1) * ROWS)
        v, part, carried = in_band(v_ref, cx_ref.at[0], cy_ref.at[0], carried, none, k, chunks)
        coupled = c_ref[1, rs, :] * v_i_ref[0, rs, :]
        sums[2] = sums[2] + v * (part + 2.0 * coupled)
        if w_ref is not None:
            w_ref[rs, :] = part + coupled
    side_above, side_below = take_rows(side_core_ref, side_cross_ref)
    up = side_above[4:5] * (beside_ref[0:1, :] + side_above[12:13] * tail_ref[0:1, :])
    down = side_below[4:5] * (beside_ref[4:5, :] + side_below[12:13] * tail_ref[1:2, :])
    up = edge_ref[0:1, :] * up
    down = cx_ref[0, rows - 1 :, :] * down
    if fix_ref is not None:
        fix_ref[...] = stack_rows([up, down])
    size = rows // 2
    first = jnp.where(upper_chip(), rows - size, 0)
    far_up = jnp.where(first == 0, tail_ref[2:3, :], 0.0)
    far_down = jnp.where(first + size == rows, tail_ref[3:4, :], 0.0)
    for k in range(size // ROWS):
        at = pl.ds(pl.multiple_of(first + k * ROWS, ROWS), ROWS)
        c_out = c_ref[0, at, :]
        part = got_ref[rows + k * ROWS : rows + (k + 1) * ROWS, :] + c_out * u_o_ref[at, :]
        if k == 0:
            part = part + jnp.where(row_at(width, 0), far_up, 0.0)
        if k == size // ROWS - 1:
            part = part + jnp.where(row_at(width, ROWS - 1), far_down, 0.0)
        inv_far = inv_far_ref[rows + size + k * ROWS : rows + size + (k + 1) * ROWS, :]
        sums[3] = sums[3] + v_ref[at, :] * (c_out * (inv_far * part))
    ends = up * v_ref[0:1, :] + down * v_ref[rows - 1 :, :]
    last = fold(sums[2] + 2.0 * sums[3] + jnp.where(row_at(width, 0), ends, 0.0)) + inner_ref[...]
    terms = (
        t0_ref[...], fold(sums[0]) + sums_ref[0:ROWS, :], fold(sums[1]) + sums_ref[ROWS : 2 * ROWS, :], last
    )
    lines = [jnp.sum(t, 0, keepdims=True) for t in terms]
    block = jnp.concatenate(lines + lines, 0)
    for at in range(0, mail_ref.shape[0], ROWS):
        mail_ref[at : at + ROWS, :] = block


def weights(mail_ref):
    block = mail_ref[0:ROWS, :]
    for at in range(ROWS, mail_ref.shape[0], ROWS):
        block = block + mail_ref[at : at + ROWS, :]
    g = jnp.sum(block[0:4] + block[4:8], 1, keepdims=True)
    g0, g1, g2, g3 = (g[k : k + 1] for k in range(4))
    mu = g1 / g0
    h = g2 - mu * g1
    t = h / (h - (g3 - 2.0 * mu * g2 + mu * mu * g1))
    a = g0 / (g0 - g1 - h * t)
    b = t * a
    return a - mu * b, b


def hand_out(j, value, k, mine_ref, send_ref, first, half):
    n = jnp.where(upper_chip(), j, 3 - j)
    owner, band = n // 2, lax.rem(n, 2)
    size = value.shape[0]

    @pl.when(owner == core())
    def _():
        mine_ref[band, k * ROWS : k * ROWS + size, :] = value

    @pl.when(owner != core())
    def _():
        send_ref[pl.ds(pl.multiple_of(first + band * half + k * ROWS, ROWS), size), :] = value


def step_kernel(
    mail_ref, s_o_ref, s_i_ref, v1_o_ref, v1_i_ref, v2_o_ref, v2_i_ref, part_i_ref, part_ref, far_ref, fix_ref, cap_ref, seen_ref,
    diag_ref, inv_o_ref, inv_i_ref, cx_ref, cy_ref, c_ref,
    z_o_ref, z_i_ref, core_ref, cross_ref, total_ref, pay_ref, x_mine_ref, z_mine_ref, scratch_ref,
):
    rows, width = s_o_ref.shape
    chunks = rows // ROWS
    a, b = weights(mail_ref)
    total = jnp.zeros((ROWS, width), F32)
    for j in range(4):
        for k in range(chunks):
            rs = slice(k * ROWS, (k + 1) * ROWS)
            s, p, q, inv = (
                band_of(o, i, j)[rs, :]
                for o, i in (
                    (s_o_ref, s_i_ref), (v1_o_ref, v1_i_ref), (v2_o_ref, v2_i_ref),
                    (inv_o_ref, inv_i_ref),
                )
            )
            if j == 0:
                part = part_ref[rs, :] + c_ref[0, rs, :] * far_ref[rs, :]
                if k == 0:
                    part = part + jnp.where(row_at(width, 0), fix_ref[0:1, :], 0.0)
                if k == chunks - 1:
                    part = part + jnp.where(row_at(width, ROWS - 1), fix_ref[1:2, :], 0.0)
            else:
                part = part_i_ref[j - 1, rs, :]
                if j == 1:
                    part = part + c_ref[1, rs, :] * v2_o_ref[rs, :]
            r = inv * part
            x = s + a * p + b * q
            residual = cap_ref[j, rs, :] * x + seen_ref[j, rs, :] - diag_ref[j, rs, :] * (x - (p + a * q + b * r))
            z = residual * inv
            band_of(z_o_ref, z_i_ref, j)[rs, :] = z
            total = total + residual * z
            hand_out(j, x, k, x_mine_ref, core_ref, ROWS, rows)
            hand_out(j, z, k, z_mine_ref, core_ref, ROWS + 2 * rows, rows)
    total_ref[...] = fold(total)
    put_two_rows(z_o_ref, z_i_ref, core_ref.at[0:ROWS], cross_ref)
    own_parts(z_o_ref, z_i_ref, cx_ref, cy_ref, c_ref, pay_ref, scratch_ref)


def give_kernel(q_o_ref, q_i_ref, mine_ref, send_ref):
    rows = q_o_ref.shape[0]
    for j in range(4):
        hand_out(j, band_of(q_o_ref, q_i_ref, j)[...], 0, mine_ref, send_ref, 0, rows)


def last_kernel(mail_ref, x_mine_ref, z_mine_ref, got_ref, q_mine_ref, q_got_ref, out_ref, answer, sems):
    half = x_mine_ref.shape[1]
    places = []
    for band in range(2):
        mine = [ref.at[band] for ref in (x_mine_ref, z_mine_ref, q_mine_ref)]
        places.append((band, core(), mine))
        at = ROWS + band * half
        got = [got_ref.at[at : at + half], got_ref.at[at + 2 * half : at + 3 * half]]
        places.append((band, 1 - core(), got + [q_got_ref.at[band * half : (band + 1) * half]]))
    copies = []
    for n, (band, which, (x_ref, _, _)) in enumerate(places):
        copies.append(pltpu.make_async_copy(x_ref, out_ref.at[1, band, half_of(which, half), :], sems.at[n]))
        copies[-1].start()
    a, b = weights(mail_ref)
    for n, (band, which, (x_ref, z_ref, q_ref)) in enumerate(places):
        answer[n] = x_ref[...] + a * z_ref[...] + b * q_ref[...]
        copies.append(
            pltpu.make_async_copy(answer.at[n], out_ref.at[0, band, half_of(which, half), :], sems.at[4 + n])
        )
        copies[-1].start()
    for copy in copies:
        copy.wait()


def on_device(cond_x, cond_y, via_cond, via_mask, capacitance, pad_mask, observe):
    _, rows, width = cond_x.shape
    half = rows // 2
    field, three, four, edge = shape(half, width), shape(3, half, width), shape(4, half, width), shape(4, width)
    eight, sides = shape(ROWS, width), shape(20, width)
    rim, pair = shape(2, width), shape(2, half, width)
    mail = shape(lax.axis_size("band") * lax.axis_size("tile") * 4, 128)
    one, two = shape(ROWS, 128), shape(2 * ROWS, 128)
    fourteen = shape(14, half, width)
    whole, whole_int = pltpu.VMEM((2, rows, width), F32), pltpu.VMEM((2, rows, width), jnp.int32)
    own, send, pay, pay_send, last, middle = call(
        load_kernel, [fourteen, fourteen, field, shape(half + ROWS, width), rim, rim],
        cond_x, cond_y, via_cond, via_mask, capacitance, pad_mask, observe, name="load", place=pltpu.HBM,
        scratch=[whole, whole_int, whole_int, pltpu.SemaphoreType.DMA((13,))],
    )
    more = core_swap(pay_send)
    more, send = lax.optimization_barrier((more, send))
    pay, last = call(pay_kernel, [field, edge], pay, more, last, name="pay")
    link, traded, last = outer_swap(pay), core_swap(send), cross_swap(last)
    cx, cy, c, diag, inv_i, s_i, inv_o, s_o, cx_edge, near, cross, cap, earlier = call(
        prepare_kernel,
        [four, four, four, four, three, three, field, field, edge, sides, sides, four, four],
        own, traded, link, middle, more, last, name="prepare",
    )
    far, sides = outer_swap(s_o), (core_swap(near), cross_swap(cross))

    coeffs = (cx, cy, c, inv_i, cx_edge)
    parts_of = [pltpu.VMEM((half, width), F32)]
    v1_i, part, sums = call(spread_kernel, [three, field, two], s_o, s_i, *sides, *coeffs, name="first_spread", cost=0)
    v1_o, near, cross, t0, pay = call(
        far_first_kernel, [field, eight, eight, one, shape(2 * half, width)],
        s_o, part, far, c, inv_o, v1_i, sums, cx, cy, name="first_far", scratch=parts_of,
    )

    def stage(u_o, u_i, pay, near, cross, t0, inv_far, name, further):
        got, cross, near = outer_swap(pay), cross_swap(cross), core_swap(near)
        v_i, part, sums, tail, there, inner, *w_i = call(
            two_spread_kernel, [three, field, two, eight, eight, one] + [three] * further,
            u_o, u_i, near, cross, *coeffs, *sides, name=name + "_spread", cost=0,
        )
        parts, v_o, *more = call(
            finish_kernel, [mail, field] + [field, rim] * further,
            u_o, got, outer_swap(tail), v_i, part, sums, there, inner, got if further else inv_far,
            cx, cy, c, inv_o, cx_edge, *sides, t0, name=name + "_finish",
        )
        if further:
            more = *w_i, *more, outer_swap(v_o)
        else:
            mine, send = call(give_kernel, [pair, shape(2 * half, width)], v_o, v_i, name="give")
            more = mine, core_swap(send)
        return v_o, v_i, all_total(parts), got, near, more

    v2_o, v2_i, total, inv_far, _, (part_i, part, fix, far) = stage(v1_o, v1_i, pay, near, cross, t0, None, "later", True)
    z_o, z_i, near, cross, t0, pay, x_mine, z_mine = call(
        step_kernel,
        [field, three, shape(ROWS + 4 * half, width), shape(ROWS, width), one, shape(half + half // 2, width), pair, pair],
        total, s_o, s_i, v1_o, v1_i, v2_o, v2_i, part_i, part, far, fix, cap, earlier, diag, inv_o, inv_i, cx, cy, c,
        name="step", scratch=parts_of,
    )
    _, _, total, _, got, given = stage(z_o, z_i, pay, near, cross, t0, inv_far, "earlier", False)
    (out,) = call(
        last_kernel, [shape(2, 2, rows, width)], total, x_mine, z_mine, got, *given, name="last", out_place=pl.ANY,
        scratch=[pltpu.VMEM((4, half, width), F32), pltpu.SemaphoreType.DMA((8,))],
    )
    return out


def solution(mesh):
    placed = (P("band", "tile", None),) * 6 + (P(None, "band", "tile", None),)
    return jax.shard_map(
        on_device,
        mesh=mesh,
        in_specs=placed,
        out_specs=P(None, "band", "tile", None),
        check_vma=False,
    )
```

```python
import jax
import jax.numpy as jnp
from jax import lax
from jax.experimental import pallas as pl
from jax.experimental.pallas import tpu as pltpu
from jax.sharding import PartitionSpec as P

NB = 8
ROWS = 8
AXES = ("band", "tile")
F32 = jnp.float32

pad_conductance = 4.0


def sizes():
    return lax.axis_size("band"), lax.axis_size("tile")


def core():
    return lax.rem(lax.axis_index("band"), 2)


def upper_chip():
    return lax.axis_index("band") >= 2


def core_swap(x):
    nb, _ = sizes()
    return lax.ppermute(x, "band", [(b, b ^ 1) for b in range(nb)])


def outer_swap(x):
    nb, _ = sizes()
    return lax.ppermute(x, "band", [(b, b ^ 2) for b in range(nb)])


def cross_swap(x):
    nb, nt = sizes()
    pairs = []
    for b in range(nb):
        for t in range(nt):
            other = (t + 1) % nt if b % 2 else (t - 1) % nt
            pairs.append((b * nt + t, (b ^ 1) * nt + other))
    return lax.ppermute(x, AXES, pairs)


def all_total(parts):
    return lax.all_to_all(parts, AXES, 0, 0, tiled=True)


def call(body, outs, *args, name, place=pltpu.VMEM, out_place=pltpu.VMEM, scratch=(), limit=10, cost=10):
    if place == pltpu.HBM:
        args = [pltpu.with_memory_space_constraint(a, pltpu.HBM) for a in args]
    return pl.pallas_call(
        body,
        out_shape=outs,
        in_specs=[pl.BlockSpec(memory_space=place)] * len(args),
        out_specs=[pl.BlockSpec(memory_space=out_place)] * len(outs),
        scratch_shapes=list(scratch),
        name=name,
        cost_estimate=pl.CostEstimate(flops=cost * 10**9, bytes_accessed=cost * 10**6, transcendentals=0),
        compiler_params=pltpu.CompilerParams(vmem_limit_bytes=limit * 1024 * 1024),
    )(*args)


def shape(*dims):
    return jax.ShapeDtypeStruct(dims, F32)


def row_at(width, at):
    return lax.broadcasted_iota(jnp.int32, (ROWS, width), 0) == at


def stack_rows(rows):
    return jnp.concatenate(rows, 0)


def put_rows(first, last, core_ref, cross_ref):
    lower = core() == 1
    core_ref[...] = jnp.where(lower, first, last)
    cross_ref[...] = jnp.where(lower, last, first)


def put_two_rows(u_o_ref, u_i_ref, core_ref, cross_ref):
    rows = u_o_ref.shape[0]
    ends = [
        stack_rows([band_of(u_o_ref, u_i_ref, j)[r : r + 1, :] for r in pair for j in range(4)])
        for pair in ((0, 1), (rows - 1, rows - 2))
    ]
    put_rows(ends[0], ends[1], core_ref, cross_ref)


def take_rows(core_ref, cross_ref):
    lower = core() == 1
    tile = lax.axis_index("tile")
    cross = cross_ref[...]
    near = core_ref[0 : cross.shape[0], :]
    above = jnp.where(lower, near, jnp.where(tile == 0, 0.0, cross))
    below = jnp.where(lower, jnp.where(tile == lax.axis_size("tile") - 1, 0.0, cross), near)
    return above, below


def fold(total):
    acc = total[:, :128]
    for at in range(128, total.shape[1], 128):
        acc = acc + total[:, at : at + 128]
    return acc


def band_of(u_o_ref, u_i_ref, j):
    return u_o_ref if j == 0 else u_i_ref.at[j - 1]


def in_band(v_ref, cx_ref, cy_ref, carried, below, k, chunks):
    width = v_ref.shape[-1]
    r = k * ROWS
    x = v_ref[r : r + ROWS, :]
    cx = cx_ref[r : r + ROWS, :]
    cy = cy_ref[r : r + ROWS, :]
    after = below if k == chunks - 1 else v_ref[r + ROWS : r + ROWS + 1, :]
    down = jnp.where(row_at(width, ROWS - 1), after, pltpu.roll(x, ROWS - 1, 0))
    flux = cx * x
    up = jnp.where(row_at(width, 0), carried, pltpu.roll(flux, 1, 0))
    total = cx * down + up + cy * pltpu.roll(x, width - 1, 1) + pltpu.roll(cy * x, 1, 1)
    return x, total, flux[ROWS - 1 :, :]


def couple(xs, parts, c_ref, rs):
    parts = list(parts)
    for j in range(1, len(xs)):
        c = c_ref[j, rs, :]
        parts[j] = parts[j] + c * xs[j - 1]
        parts[j - 1] = parts[j - 1] + c * xs[j]
    return parts


def half_of(which, half):
    return pl.ds(pl.multiple_of(which * half, ROWS), half)


def start_copies(pairs, sems):
    copies = [pltpu.make_async_copy(source, to, sems.at[n]) for n, (source, to) in enumerate(pairs)]
    for copy in copies:
        copy.start()
    return copies


def load_kernel(
    cond_x_ref, cond_y_ref, via_ref, mask_ref, cap_ref, pad_ref, observe_ref,
    mine_ref, send_ref, pay_mine_ref, pay_send_ref, last_ref, middle_ref, via_at, mask_at, pad_at, sems,
):
    half = send_ref.shape[1]
    me = core()
    pairs = [(via_ref, via_at), (mask_ref, mask_at), (pad_ref, pad_at)]
    halves = ((send_ref, pay_send_ref, 1 - me), (mine_ref, pay_mine_ref, me))
    for ref, _, which in halves:
        rs = half_of(which, half)
        pairs += [
            (cond_x_ref.at[:, rs, :], ref.at[0:2]),
            (cond_y_ref.at[:, rs, :], ref.at[2:4]),
            (observe_ref.at[1, :, rs, :], ref.at[8:10]),
            (cap_ref.at[:, rs, :], ref.at[10:12]),
        ]
    for ref, _, which in halves:
        pairs.append((observe_ref.at[0, :, half_of(which, half), :], ref.at[12:14]))
    copies = start_copies(pairs, sems)
    for copy in copies[:-2]:
        copy.wait()
    for ref, pay_ref, which in halves:
        rs = half_of(which, half)
        for band in range(2):
            ref[4 + band] = via_at[band, rs, :] * mask_at[band, rs, :].astype(F32)
            ref[6 + band] = ref[10 + band] + pad_conductance * pad_at[band, rs, :].astype(F32)
    for band in range(2):
        own, other = mine_ref[band, half - 1 :, :], send_ref[band, half - 1 :, :]
        last_ref[band : band + 1, :] = jnp.where(me == 1, own, other)
        middle_ref[band : band + 1, :] = jnp.where(me == 1, other, own)
    width = middle_ref.shape[1]
    lane = lax.broadcasted_iota(jnp.int32, (ROWS, width), 1)
    upper = upper_chip()
    band = jnp.where(upper, 0, 1)
    for (ref, pay_ref, which), (other_ref, _, _) in (halves, halves[::-1]):
        carried = jnp.where(which == 0, 0.0, other_ref[band, half - 1 :, :])
        for k in range(half // ROWS):
            rs = slice(k * ROWS, (k + 1) * ROWS)
            cx, cy, seen, via = ref[band, rs, :], ref[2 + band, rs, :], ref[8 + band, rs, :], ref[5, rs, :]
            up = jnp.where(row_at(width, 0), carried, pltpu.roll(cx, 1, 0))
            carried = cx[ROWS - 1 :, :]
            left = jnp.where(lane == 0, 0.0, pltpu.roll(cy, 1, 1))
            diag = ref[6 + band, rs, :] + cx + cy + up + left + ref[4, rs, :]
            pay_ref[rs, :] = jnp.where(upper, diag, via)
            inv = 1.0 / (diag + via)
            pay_ref[half + k * ROWS : half + (k + 1) * ROWS, :] = jnp.where(upper, seen, seen * inv)
            if 2 * k * ROWS >= half:
                at = 3 * half // 2 + k * ROWS
                pay_ref[at : at + ROWS, :] = inv
    none = jnp.zeros((ROWS - 4, width), F32)
    pay_send_ref[5 * half // 2 :, :] = stack_rows([middle_ref[...], last_ref[...], none])
    for copy in copies[-2:]:
        copy.wait()


def pay_kernel(mine_ref, got_ref, last_ref, pay_ref, more_ref, all_last_ref):
    half = pay_ref.shape[0]
    theirs = (core() == 1) == upper_chip()
    pay_ref[...] = jnp.where(theirs, got_ref[0:half, :], mine_ref[0:half, :])
    more_ref[...] = jnp.where(theirs, got_ref[half : 5 * half // 2, :], mine_ref[half:, :])
    at = 5 * half // 2
    own, other = last_ref[...], got_ref[at + 2 : at + 4, :]
    all_last_ref[...] = stack_rows([jnp.where(core() == 0, own, other), jnp.where(core() == 0, other, own)])


def place_of(owner, band):
    n = 2 * owner + band
    return jnp.where(upper_chip(), n, 3 - n)


def prepare_kernel(
    mine_ref, got_ref, middle_ref, more_ref, last_ref,
    cx_ref, cy_ref, c_ref, diag_ref, inv_ref, s_ref, part_ref, seen_o_ref, edge_ref, cap_ref, seen_ref, all_part, all_seen,
):
    half, width = part_ref.shape
    me = core()
    upper = upper_chip()
    lane = lax.broadcasted_iota(jnp.int32, (ROWS, width), 1)
    first_tile = jnp.logical_and(me == 0, lax.axis_index("tile") == 0)
    own_edge = jnp.where(me == 1, middle_ref[...], last_ref[0:2, :])
    got_edge = jnp.where(me == 1, more_ref[5 * half // 2 : 5 * half // 2 + 2, :], last_ref[2:4, :])
    c_ref[0] = jnp.zeros((half, width), F32)
    for owner, ref, edges in ((me, mine_ref, own_edge), (1 - me, got_ref, got_edge)):
        for band in range(2):
            j = place_of(owner, band)
            carried = jnp.where(first_tile, 0.0, edges[band : band + 1, :])
            edge_ref[pl.ds(j, 1), :] = carried
            cx_ref[j] = ref[band]
            cap_ref[j] = ref[10 + band]
            seen_ref[j] = ref[12 + band]
            all_seen[j] = ref[8 + band]
            via_at = jnp.where(upper, j + 1, j)

            @pl.when(via_at < 4)
            def _():
                c_ref[via_at] = ref[4 + band]

            for k in range(half // ROWS):
                rs = slice(k * ROWS, (k + 1) * ROWS)
                cx, cy, diag = (ref[2 * n + band, rs, :] for n in (0, 1, 3))
                cut = jnp.where(lane == width - 1, 0.0, cy)
                up = jnp.where(row_at(width, 0), carried, pltpu.roll(cx, 1, 0))
                carried = cx[ROWS - 1 :, :]
                cy_ref[j, rs, :] = cut
                all_part[j, rs, :] = diag + cx + cy + up + pltpu.roll(cut, 1, 1)
    part_ref[...] = all_part[0] + c_ref[1]
    seen_o_ref[...] = all_seen[0]
    for j in range(1, 4):
        for k in range(half // ROWS):
            rs = slice(k * ROWS, (k + 1) * ROWS)
            diag = all_part[j, rs, :] + c_ref[j, rs, :]
            if j < 3:
                diag = diag + c_ref[j + 1, rs, :]
            inv = 1.0 / diag
            diag_ref[j - 1, rs, :] = diag
            inv_ref[j - 1, rs, :] = inv
            s_ref[j - 1, rs, :] = all_seen[j, rs, :] * inv


def outer_kernel(
    part_ref, seen_ref, link_ref, cx_ref, cy_ref, c_ref, inv_i_ref, s_i_ref,
    c_out_ref, diag_ref, inv_ref, s_ref, core_ref, cross_ref, fix_ref,
):
    rows, width = part_ref.shape
    upper = upper_chip()
    for k in range(rows // ROWS):
        rs = slice(k * ROWS, (k + 1) * ROWS)
        c_out = jnp.where(upper, link_ref[rs, :], c_ref[0, rs, :])
        diag = part_ref[rs, :] + c_out
        inv = 1.0 / diag
        c_out_ref[rs, :] = c_out
        diag_ref[rs, :] = diag
        inv_ref[rs, :] = inv
        s_ref[rs, :] = seen_ref[rs, :] * inv
    ends = []
    for r, beyond in ((0, 0), (rows - 1, rows - 2)):
        at = slice(r, r + 1)
        lines = [band_of(s_ref, s_i_ref, j)[at, :] for j in range(4)]
        lines += [band_of(inv_ref, inv_i_ref, j)[at, :] for j in range(4)]
        lines += [cy_ref[j, at, :] for j in range(4)]
        lines += [c_out_ref[at, :]] + [c_ref[j, at, :] for j in range(1, 4)]
        lines += [cx_ref[j, beyond : beyond + 1, :] for j in range(4)]
        ends.append(stack_rows(lines))
    put_rows(ends[0], ends[1], core_ref, cross_ref)
    fix_ref[...] = jnp.where(upper, diag_ref[0:1, :], s_ref[0:1, :])


def own_parts(u_o_ref, u_i_ref, cx_ref, cy_ref, c_ref, pay_ref, scratch_ref):
    rows, width = u_o_ref.shape
    chunks = rows // ROWS
    none = jnp.zeros((1, width), F32)
    carried = none
    for k in range(chunks):
        rs = slice(k * ROWS, (k + 1) * ROWS)
        x, part, carried = in_band(u_o_ref, cx_ref.at[0], cy_ref.at[0], carried, none, k, chunks)
        pay_ref[rs, :] = x
        scratch_ref[rs, :] = part + c_ref[1, rs, :] * u_i_ref[0, rs, :]
    size = rows // 2
    first = jnp.where(upper_chip(), 0, rows - size)
    pay_ref[rows : rows + size, :] = scratch_ref[pl.ds(pl.multiple_of(first, ROWS), size), :]


def spread_kernel(
    u_o_ref, u_i_ref, core_ref, cross_ref, cx_ref, cy_ref, c_ref, inv_i_ref, edge_ref, v_i_ref, part_ref, sums_ref
):
    above, below = take_rows(core_ref, cross_ref)
    spread_rows(u_o_ref, u_i_ref, above, below, cx_ref, cy_ref, c_ref, inv_i_ref, edge_ref, v_i_ref, part_ref, sums_ref)


def spread_rows(u_o_ref, u_i_ref, above, below, cx_ref, cy_ref, c_ref, inv_i_ref, edge_ref, v_i_ref, part_ref, sums_ref):
    rows, width = u_o_ref.shape
    chunks = rows // ROWS
    carried = [edge_ref[j : j + 1, :] * above[j : j + 1] for j in range(4)]
    sums = [jnp.zeros((ROWS, width), F32) for _ in range(2)]
    for k in range(chunks):
        rs = slice(k * ROWS, (k + 1) * ROWS)
        xs, parts = [], []
        for j in range(4):
            x, part, carried[j] = in_band(
                band_of(u_o_ref, u_i_ref, j), cx_ref.at[j], cy_ref.at[j], carried[j], below[j : j + 1], k, chunks
            )
            xs.append(x)
            parts.append(part)
        parts = couple(xs, parts, c_ref, rs)
        part_ref[rs, :] = parts[0]
        for j in range(1, 4):
            v = inv_i_ref[j - 1, rs, :] * parts[j]
            v_i_ref[j - 1, rs, :] = v
            sums[0] = sums[0] + xs[j] * parts[j]
            sums[1] = sums[1] + v * parts[j]
    sums_ref[0:ROWS, :] = fold(sums[0])
    sums_ref[ROWS : 2 * ROWS, :] = fold(sums[1])


def beside(u_o_ref, u_i_ref, above, below, side_above, side_below, edge_ref, cx_ref):
    rows, width = u_o_ref.shape
    here = stack_rows([above[0:4], below[0:4]])
    beyond = stack_rows([above[4:8], below[4:8]])
    inside = [band_of(u_o_ref, u_i_ref, j)[r : r + 1, :] for r in (0, rows - 1) for j in range(4)]
    toward = stack_rows([edge_ref[...]] + [cx_ref[j, rows - 1 :, :] for j in range(4)])
    inv, cy, c, away = (stack_rows([side_above[n : n + 4], side_below[n : n + 4]]) for n in (4, 8, 12, 16))
    c = jnp.where(jnp.logical_or(row_at(width, 0), row_at(width, 4)), 0.0, c)
    total = toward * stack_rows(inside) + away * beyond
    total = total + cy * pltpu.roll(here, width - 1, 1) + pltpu.roll(cy * here, 1, 1)
    return total + c * pltpu.roll(here, 1, 0) + pltpu.roll(c * here, ROWS - 1, 0), inv


def two_spread_kernel(
    u_o_ref, u_i_ref, core_ref, cross_ref, cx_ref, cy_ref, c_ref, inv_i_ref, edge_ref, side_core_ref, side_cross_ref,
    v_i_ref, part_ref, sums_ref, tail_ref, beside_ref, total_ref, w_ref=None,
):
    rows, width = u_o_ref.shape
    chunks = rows // ROWS
    above, below = take_rows(core_ref, cross_ref)
    spread_rows(u_o_ref, u_i_ref, above, below, cx_ref, cy_ref, c_ref, inv_i_ref, edge_ref, v_i_ref, part_ref, sums_ref)
    fluxes = [edge_ref[0:1, :] * above[0:1], cx_ref[0, rows - 1 :, :] * below[0:1]]
    tail_ref[...] = stack_rows([above[0:1], below[0:1], *fluxes])
    side_above, side_below = take_rows(side_core_ref, side_cross_ref)
    parts_there, inv = beside(u_o_ref, u_i_ref, above, below, side_above, side_below, edge_ref, cx_ref)
    beside_ref[...] = parts_there
    v_there = inv * parts_there
    carried = [edge_ref[j : j + 1, :] * v_there[j : j + 1] for j in range(1, 4)]
    total = jnp.zeros((ROWS, width), F32)
    for k in range(chunks):
        rs = slice(k * ROWS, (k + 1) * ROWS)
        xs, parts = [], []
        for j in range(1, 4):
            x, part, carried[j - 1] = in_band(
                v_i_ref.at[j - 1], cx_ref.at[j], cy_ref.at[j], carried[j - 1], v_there[4 + j : 5 + j], k, chunks
            )
            xs.append(x)
            parts.append(part)
        parts = couple(xs, parts, c_ref.at[pl.ds(1, 3)], rs)
        for j in range(3):
            total = total + xs[j] * parts[j]
            if w_ref is not None:
                w_ref[j, rs, :] = parts[j]
    total_ref[...] = fold(total)


def far_first_kernel(
    u_o_ref, part_ref, got_ref, more_ref, fix_ref, c_out_ref, inv_ref, v_i_ref, sums_ref, cx_ref, cy_ref, c_ref,
    v_ref, core_ref, cross_ref, total_ref, pay_ref, inv_far_ref, scratch_ref,
):
    rows, width = u_o_ref.shape
    upper = upper_chip()
    total = jnp.zeros((ROWS, width), F32)
    for k in range(rows // ROWS):
        rs = slice(k * ROWS, (k + 1) * ROWS)
        c_out = c_out_ref[rs, :]
        diag, far = got_ref[rs, :] + c_out, more_ref[rs, :]
        if k == 0:
            first = jnp.broadcast_to(fix_ref[0:1, :], far.shape)
            diag = jnp.where(row_at(width, 0), first, diag)
            far = jnp.where(jnp.logical_and(upper, row_at(width, 0)), first, far)
        inv_far = 1.0 / jnp.where(upper, 1.0, diag)
        if k * ROWS < rows // 2:
            inv_far_ref[rs, :] = jnp.where(upper, more_ref[rows + k * ROWS : rows + (k + 1) * ROWS, :], inv_far)
        far = jnp.where(upper, far, far * inv_far)
        part = part_ref[rs, :] + c_out * far
        v = inv_ref[rs, :] * part
        v_ref[rs, :] = v
        total = total + v * part
    total_ref[...] = fold(total) + sums_ref[ROWS : 2 * ROWS, :]
    put_two_rows(v_ref, v_i_ref, core_ref, cross_ref)
    own_parts(v_ref, v_i_ref, cx_ref, cy_ref, c_ref, pay_ref, scratch_ref)


def far_kernel(u_o_ref, got_ref, part_ref, sums_ref, c_out_ref, inv_ref, v_ref, totals_ref):
    rows, width = u_o_ref.shape
    sums = [jnp.zeros((ROWS, width), F32) for _ in range(2)]
    for k in range(rows // ROWS):
        rs = slice(k * ROWS, (k + 1) * ROWS)
        part = part_ref[rs, :] + c_out_ref[rs, :] * got_ref[rs, :]
        v = inv_ref[rs, :] * part
        v_ref[rs, :] = v
        sums[0] = sums[0] + u_o_ref[rs, :] * part
        sums[1] = sums[1] + v * part
    totals_ref[0:ROWS, :] = fold(sums[0]) + sums_ref[0:ROWS, :]
    totals_ref[ROWS : 2 * ROWS, :] = fold(sums[1]) + sums_ref[ROWS : 2 * ROWS, :]


def finish_kernel(
    u_o_ref, v_ref, got_ref, tail_ref, v_i_ref, totals_ref, beside_ref, inner_ref, inv_far_ref,
    cx_ref, cy_ref, c_ref, c_out_ref, edge_ref, side_core_ref, side_cross_ref, t0_ref,
    mail_ref, w_ref=None, fix_ref=None,
):
    rows, width = u_o_ref.shape
    chunks = rows // ROWS
    none = jnp.zeros((1, width), F32)
    sums = [jnp.zeros((ROWS, width), F32) for _ in range(2)]
    carried = none
    for k in range(chunks):
        rs = slice(k * ROWS, (k + 1) * ROWS)
        v, part, carried = in_band(v_ref, cx_ref.at[0], cy_ref.at[0], carried, none, k, chunks)
        coupled = c_ref[1, rs, :] * v_i_ref[0, rs, :]
        sums[0] = sums[0] + v * (part + 2.0 * coupled)
        if w_ref is not None:
            w_ref[rs, :] = part + coupled
    side_above, side_below = take_rows(side_core_ref, side_cross_ref)
    up = side_above[4:5] * (beside_ref[0:1, :] + side_above[12:13] * tail_ref[0:1, :])
    down = side_below[4:5] * (beside_ref[4:5, :] + side_below[12:13] * tail_ref[1:2, :])
    up = edge_ref[0:1, :] * up
    down = cx_ref[0, rows - 1 :, :] * down
    if fix_ref is not None:
        fix_ref[...] = stack_rows([up, down])
    size = rows // 2
    first = jnp.where(upper_chip(), rows - size, 0)
    far_up = jnp.where(first == 0, tail_ref[2:3, :], 0.0)
    far_down = jnp.where(first + size == rows, tail_ref[3:4, :], 0.0)
    for k in range(size // ROWS):
        at = pl.ds(pl.multiple_of(first + k * ROWS, ROWS), ROWS)
        c_out = c_out_ref[at, :]
        part = got_ref[rows + k * ROWS : rows + (k + 1) * ROWS, :] + c_out * u_o_ref[at, :]
        if k == 0:
            part = part + jnp.where(row_at(width, 0), far_up, 0.0)
        if k == size // ROWS - 1:
            part = part + jnp.where(row_at(width, ROWS - 1), far_down, 0.0)
        sums[1] = sums[1] + v_ref[at, :] * (c_out * (inv_far_ref[k * ROWS : (k + 1) * ROWS, :] * part))
    ends = up * v_ref[0:1, :] + down * v_ref[rows - 1 :, :]
    last = fold(sums[0] + 2.0 * sums[1] + jnp.where(row_at(width, 0), ends, 0.0)) + inner_ref[...]
    terms = (t0_ref[...], totals_ref[0:ROWS, :], totals_ref[ROWS : 2 * ROWS, :], last)
    lane = lax.broadcasted_iota(jnp.int32, (ROWS, 128), 1)
    row = jnp.zeros((ROWS, 128), F32)
    for n, t in enumerate(terms):
        t = t + pltpu.roll(t, 64, 1)
        t = t + pltpu.roll(t, 32, 1)
        row = jnp.where(lane // 32 == n, t, row)
    row = jnp.broadcast_to(jnp.sum(row, 0, keepdims=True), (ROWS, 128))
    for at in range(0, mail_ref.shape[0], ROWS):
        mail_ref[at : at + ROWS, :] = row


def weights(mail_ref):
    block = mail_ref[0:ROWS, :]
    for at in range(ROWS, mail_ref.shape[0], ROWS):
        block = block + mail_ref[at : at + ROWS, :]
    block = jnp.sum(block, 0, keepdims=True)
    g0, g1, g2, g3 = (jnp.sum(block[:, 32 * k : 32 * (k + 1)], 1, keepdims=True) for k in range(4))
    mu = g1 / g0
    h = g2 - mu * g1
    t = h / (h - (g3 - 2.0 * mu * g2 + mu * mu * g1))
    a = g0 / (g0 - g1 - h * t)
    b = t * a
    return a - mu * b, b


def hand_out(j, value, k, mine_ref, send_ref, first, half):
    n = jnp.where(upper_chip(), j, 3 - j)
    owner, band = n // 2, lax.rem(n, 2)
    size = value.shape[0]

    @pl.when(owner == core())
    def _():
        mine_ref[band, k * ROWS : k * ROWS + size, :] = value

    @pl.when(owner != core())
    def _():
        send_ref[pl.ds(pl.multiple_of(first + band * half + k * ROWS, ROWS), size), :] = value


def step_kernel(
    mail_ref, s_o_ref, s_i_ref, v1_o_ref, v1_i_ref, v2_o_ref, v2_i_ref, part_i_ref, part_ref, far_ref, fix_ref, cap_ref, seen_ref,
    diag_o_ref, diag_i_ref, inv_o_ref, inv_i_ref, cx_ref, cy_ref, c_ref, c_out_ref,
    z_o_ref, z_i_ref, core_ref, cross_ref, total_ref, pay_ref, x_mine_ref, z_mine_ref, scratch_ref,
):
    rows, width = s_o_ref.shape
    chunks = rows // ROWS
    a, b = weights(mail_ref)
    total = jnp.zeros((ROWS, width), F32)
    for j in range(4):
        for k in range(chunks):
            rs = slice(k * ROWS, (k + 1) * ROWS)
            s, p, q, diag, inv = (
                band_of(o, i, j)[rs, :]
                for o, i in (
                    (s_o_ref, s_i_ref), (v1_o_ref, v1_i_ref), (v2_o_ref, v2_i_ref),
                    (diag_o_ref, diag_i_ref), (inv_o_ref, inv_i_ref),
                )
            )
            if j == 0:
                part = part_ref[rs, :] + c_out_ref[rs, :] * far_ref[rs, :]
                if k == 0:
                    part = part + jnp.where(row_at(width, 0), fix_ref[0:1, :], 0.0)
                if k == chunks - 1:
                    part = part + jnp.where(row_at(width, ROWS - 1), fix_ref[1:2, :], 0.0)
            else:
                part = part_i_ref[j - 1, rs, :]
                if j == 1:
                    part = part + c_ref[1, rs, :] * v2_o_ref[rs, :]
            r = inv * part
            x = s + a * p + b * q
            residual = cap_ref[j, rs, :] * x + seen_ref[j, rs, :] - diag * (x - (p + a * q + b * r))
            z = residual * inv
            band_of(z_o_ref, z_i_ref, j)[rs, :] = z
            total = total + residual * z
            hand_out(j, x, k, x_mine_ref, core_ref, ROWS, rows)
            hand_out(j, z, k, z_mine_ref, core_ref, ROWS + 2 * rows, rows)
    total_ref[...] = fold(total)
    put_two_rows(z_o_ref, z_i_ref, core_ref.at[0:ROWS], cross_ref)
    own_parts(z_o_ref, z_i_ref, cx_ref, cy_ref, c_ref, pay_ref, scratch_ref)


def give_kernel(q_o_ref, q_i_ref, mine_ref, send_ref):
    rows = q_o_ref.shape[0]
    for j in range(4):
        hand_out(j, band_of(q_o_ref, q_i_ref, j)[...], 0, mine_ref, send_ref, 0, rows)


def last_kernel(mail_ref, x_mine_ref, z_mine_ref, got_ref, q_mine_ref, q_got_ref, out_ref, answer, sems):
    half = x_mine_ref.shape[1]
    places = []
    for band in range(2):
        mine = [ref.at[band] for ref in (x_mine_ref, z_mine_ref, q_mine_ref)]
        places.append((band, core(), mine))
        at = ROWS + band * half
        got = [got_ref.at[at : at + half], got_ref.at[at + 2 * half : at + 3 * half]]
        places.append((band, 1 - core(), got + [q_got_ref.at[band * half : (band + 1) * half]]))
    copies = []
    for n, (band, which, (x_ref, _, _)) in enumerate(places):
        copies.append(pltpu.make_async_copy(x_ref, out_ref.at[1, band, half_of(which, half), :], sems.at[n]))
        copies[-1].start()
    a, b = weights(mail_ref)
    for n, (band, which, (x_ref, z_ref, q_ref)) in enumerate(places):
        answer[n] = x_ref[...] + a * z_ref[...] + b * q_ref[...]
        copies.append(
            pltpu.make_async_copy(answer.at[n], out_ref.at[0, band, half_of(which, half), :], sems.at[4 + n])
        )
        copies[-1].start()
    for copy in copies:
        copy.wait()


def on_device(cond_x, cond_y, via_cond, via_mask, capacitance, pad_mask, observe):
    _, rows, width = cond_x.shape
    half = rows // 2
    field, three, four, edge = shape(half, width), shape(3, half, width), shape(4, half, width), shape(4, width)
    eight, twenty = shape(ROWS, width), shape(20, width)
    most, part_rows = shape(3 * half // 2, width), shape(half // 2, width)
    rim, pair = shape(2, width), shape(2, half, width)
    mail = shape(lax.axis_size("band") * lax.axis_size("tile"), 128)
    one, two = shape(ROWS, 128), shape(2 * ROWS, 128)
    fourteen = shape(14, half, width)
    whole, whole_int = pltpu.VMEM((2, rows, width), F32), pltpu.VMEM((2, rows, width), jnp.int32)
    own, send, pay, pay_send, last, middle = call(
        load_kernel, [fourteen, fourteen, shape(5 * half // 2, width), shape(5 * half // 2 + ROWS, width), rim, rim],
        cond_x, cond_y, via_cond, via_mask, capacitance, pad_mask, observe, name="load", place=pltpu.HBM,
        scratch=[whole, whole_int, whole_int, pltpu.SemaphoreType.DMA((13,))],
    )
    more = core_swap(pay_send)
    more, send = lax.optimization_barrier((more, send))
    pay, pay_more, last = call(pay_kernel, [field, most, edge], pay, more, last, name="pay")
    link, traded, last = outer_swap(pay), core_swap(send), cross_swap(last)
    pay_more, last = lax.optimization_barrier((pay_more, last))
    far = outer_swap(pay_more)
    cx, cy, c, diag_i, inv_i, s_i, part, seen, cx_edge, cap, earlier = call(
        prepare_kernel, [four, four, four, three, three, three, field, field, edge, four, four],
        own, traded, middle, more, last, name="prepare", cost=0,
        scratch=[pltpu.VMEM((4, half, width), F32), pltpu.VMEM((4, half, width), F32)],
    )
    c_out, diag_o, inv_o, s_o, near, cross, fix = call(
        outer_kernel, [field, field, field, field, twenty, twenty, shape(1, width)],
        part, seen, link, cx, cy, c, inv_i, s_i, name="outer",
    )
    fix, sides = outer_swap(fix), (core_swap(near), cross_swap(cross))

    coeffs = (cx, cy, c, inv_i, cx_edge)
    parts_of = [pltpu.VMEM((half, width), F32)]
    v1_i, part, sums = call(spread_kernel, [three, field, two], s_o, s_i, *sides, *coeffs, name="first_spread", cost=0)
    v1_o, near, cross, t0, pay, inv_far = call(
        far_first_kernel, [field, eight, eight, one, most, part_rows],
        s_o, part, link, far, fix, c_out, inv_o, v1_i, sums, cx, cy, c, name="first_far", scratch=parts_of,
    )

    def stage(u_o, u_i, pay, near, cross, t0, name, further):
        got, cross, near = outer_swap(pay), cross_swap(cross), core_swap(near)
        v_i, part, sums, tail, there, inner, *w_i = call(
            two_spread_kernel, [three, field, two, edge, eight, one] + [three] * further,
            u_o, u_i, near, cross, *coeffs, *sides, name=name + "_spread", cost=0,
        )
        v_o, totals = call(far_kernel, [field, two], u_o, got, part, sums, c_out, inv_o, name=name + "_far")
        if further:
            more = (outer_swap(v_o),)
        else:
            mine, send = call(give_kernel, [pair, shape(2 * half, width)], v_o, v_i, name="give")
            more = mine, core_swap(send)
        parts, *rest = call(
            finish_kernel, [mail] + [field, rim] * further,
            u_o, v_o, got, outer_swap(tail), v_i, totals, there, inner, inv_far,
            cx, cy, c, c_out, cx_edge, *sides, t0, name=name + "_finish",
        )
        more = *w_i, *rest, *more
        return v_o, v_i, all_total(parts), near, more

    v2_o, v2_i, total, _, (part_i, part, fix, far) = stage(v1_o, v1_i, pay, near, cross, t0, "later", True)
    z_o, z_i, near, cross, t0, pay, x_mine, z_mine = call(
        step_kernel,
        [field, three, shape(ROWS + 4 * half, width), eight, one, most, pair, pair],
        total, s_o, s_i, v1_o, v1_i, v2_o, v2_i, part_i, part, far, fix, cap, earlier, diag_o, diag_i, inv_o, inv_i, cx, cy, c, c_out,
        name="step", scratch=parts_of,
    )
    _, _, total, got, given = stage(z_o, z_i, pay, near, cross, t0, "earlier", False)
    (out,) = call(
        last_kernel, [shape(2, 2, rows, width)], total, x_mine, z_mine, got, *given, name="last", out_place=pl.ANY,
        scratch=[pltpu.VMEM((4, half, width), F32), pltpu.SemaphoreType.DMA((8,))],
    )
    return out


def solution(mesh):
    placed = (P("band", "tile", None),) * 6 + (P(None, "band", "tile", None),)
    return jax.shard_map(
        on_device,
        mesh=mesh,
        in_specs=placed,
        out_specs=P(None, "band", "tile", None),
        check_vma=False,
    )
```

```python
import jax
import jax.numpy as jnp
from jax import lax
from jax.experimental import pallas as pl
from jax.experimental.pallas import tpu as pltpu
from jax.sharding import PartitionSpec as P

NB = 8
ROWS = 8
AXES = ("band", "tile")
F32 = jnp.float32

pad_conductance = 4.0

COSTS = {"prepare": 0, "first_spread": 0, "later_spread": 0, "earlier_spread": 0, "later_out": 0}


def sizes():
    return lax.axis_size("band"), lax.axis_size("tile")


def core():
    return lax.rem(lax.axis_index("band"), 2)


def upper_chip():
    return lax.axis_index("band") >= 2


def core_swap(x):
    nb, _ = sizes()
    return lax.ppermute(x, "band", [(b, b ^ 1) for b in range(nb)])


def outer_swap(x):
    nb, _ = sizes()
    return lax.ppermute(x, "band", [(b, b ^ 2) for b in range(nb)])


def cross_swap(x):
    nb, nt = sizes()
    pairs = []
    for b in range(nb):
        for t in range(nt):
            other = (t + 1) % nt if b % 2 else (t - 1) % nt
            pairs.append((b * nt + t, (b ^ 1) * nt + other))
    return lax.ppermute(x, AXES, pairs)


def all_total(parts):
    return lax.all_to_all(parts, AXES, 0, 0, tiled=True)


def call(body, outs, *args, name, place=pltpu.VMEM, out_place=pltpu.VMEM, scratch=(), limit=10, reuse=False):
    cost = COSTS.get(name, 10)
    if place == pltpu.HBM:
        args = [pltpu.with_memory_space_constraint(a, pltpu.HBM) for a in args]
    return pl.pallas_call(
        body,
        out_shape=outs,
        in_specs=[pl.BlockSpec(memory_space=pl.ANY if reuse and n == 0 else place) for n in range(len(args))],
        input_output_aliases={0: 0} if reuse else {},
        out_specs=[pl.BlockSpec(memory_space=out_place)] * len(outs),
        scratch_shapes=list(scratch),
        name=name,
        cost_estimate=pl.CostEstimate(flops=cost * 10**9, bytes_accessed=cost * 10**6, transcendentals=0),
        compiler_params=pltpu.CompilerParams(vmem_limit_bytes=limit * 1024 * 1024),
    )(*args)


def shape(*dims):
    return jax.ShapeDtypeStruct(dims, F32)


def row_at(width, at):
    return lax.broadcasted_iota(jnp.int32, (ROWS, width), 0) == at


def stack_rows(rows):
    return jnp.concatenate(rows, 0)


def put_rows(first, last, core_ref, cross_ref):
    lower = core() == 1
    core_ref[...] = jnp.where(lower, first, last)
    cross_ref[...] = jnp.where(lower, last, first)


def put_two_rows(u_o_ref, u_i_ref, core_ref, cross_ref):
    rows = u_o_ref.shape[0]
    ends = [
        stack_rows([band_of(u_o_ref, u_i_ref, j)[r : r + 1, :] for r in pair for j in range(4)])
        for pair in ((0, 1), (rows - 1, rows - 2))
    ]
    put_rows(ends[0], ends[1], core_ref, cross_ref)


def take_rows(core_ref, cross_ref):
    lower = core() == 1
    tile = lax.axis_index("tile")
    cross = cross_ref[...]
    near = core_ref[0 : cross.shape[0], :]
    above = jnp.where(lower, near, jnp.where(tile == 0, 0.0, cross))
    below = jnp.where(lower, jnp.where(tile == lax.axis_size("tile") - 1, 0.0, cross), near)
    return above, below


def fold(total):
    acc = total[:, :128]
    for at in range(128, total.shape[1], 128):
        acc = acc + total[:, at : at + 128]
    return acc


def band_of(u_o_ref, u_i_ref, j):
    return u_o_ref if j == 0 else u_i_ref.at[j - 1]


def in_band(v_ref, cx_ref, cy_ref, carried, below, k, chunks):
    width = v_ref.shape[-1]
    r = k * ROWS
    x = v_ref[r : r + ROWS, :]
    cx = cx_ref[r : r + ROWS, :]
    cy = cy_ref[r : r + ROWS, :]
    after = below if k == chunks - 1 else v_ref[r + ROWS : r + ROWS + 1, :]
    down = jnp.where(row_at(width, ROWS - 1), after, pltpu.roll(x, ROWS - 1, 0))
    flux = cx * x
    up = jnp.where(row_at(width, 0), carried, pltpu.roll(flux, 1, 0))
    total = cx * down + up + cy * pltpu.roll(x, width - 1, 1) + pltpu.roll(cy * x, 1, 1)
    return x, total, flux[ROWS - 1 :, :]


def couple(xs, parts, c_ref, rs):
    parts = list(parts)
    for j in range(1, len(xs)):
        c = c_ref[j, rs, :]
        parts[j] = parts[j] + c * xs[j - 1]
        parts[j - 1] = parts[j - 1] + c * xs[j]
    return parts


def half_of(which, half):
    return pl.ds(pl.multiple_of(which * half, ROWS), half)


def start_copies(pairs, sems):
    copies = [pltpu.make_async_copy(source, to, sems.at[n]) for n, (source, to) in enumerate(pairs)]
    for copy in copies:
        copy.start()
    return copies


def load_kernel(
    cond_x_ref, cond_y_ref, via_ref, mask_ref, cap_ref, pad_ref, observe_ref,
    mine_ref, send_ref, pay_mine_ref, pay_send_ref, last_ref, middle_ref,
    via_at, mask_at, pad_at, edge_at, sems,
):
    half, width = send_ref.shape[1:]
    me = core()
    upper = upper_chip()
    halves = ((send_ref, pay_send_ref, 1 - me), (mine_ref, pay_mine_ref, me))
    pairs = [(via_ref, via_at), (mask_ref, mask_at), (pad_ref, pad_at)]
    pairs.append((cond_x_ref.at[:, pl.ds(half - ROWS, ROWS), :], edge_at.at[0]))
    pairs.append((cond_x_ref.at[:, pl.ds(2 * half - ROWS, ROWS), :], edge_at.at[1]))
    for ref, _, which in halves:
        rs = half_of(which, half)
        pairs += [
            (cond_x_ref.at[:, rs, :], ref.at[0:2]),
            (cond_y_ref.at[:, rs, :], ref.at[2:4]),
            (observe_ref.at[1, :, rs, :], ref.at[8:10]),
            (cap_ref.at[:, rs, :], ref.at[10:12]),
        ]
    for ref, _, which in halves:
        pairs.append((observe_ref.at[0, :, half_of(which, half), :], ref.at[12:14]))
    copies = start_copies(pairs, sems)
    for copy in copies[:5]:
        copy.wait()
    for band in range(2):
        middle_ref[band : band + 1, :] = edge_at[0, band, ROWS - 1 :, :]
        last_ref[band : band + 1, :] = edge_at[1, band, ROWS - 1 :, :]
    lane = lax.broadcasted_iota(jnp.int32, (ROWS, width), 1)
    facing = jnp.where(upper, 0, 1)
    for n, (ref, pay_ref, which) in enumerate(halves):
        for copy in copies[5 + 4 * n : 9 + 4 * n]:
            copy.wait()
        rs = half_of(which, half)
        for band in range(2):
            ref[4 + band] = via_at[band, rs, :] * mask_at[band, rs, :].astype(F32)
            ref[6 + band] = ref[10 + band] + pad_conductance * pad_at[band, rs, :].astype(F32)
        carried = jnp.where(which == 0, 0.0, edge_at[0, facing, ROWS - 1 :, :])
        for k in range(half // ROWS):
            rs = slice(k * ROWS, (k + 1) * ROWS)
            cx, cy, seen, via = ref[facing, rs, :], ref[2 + facing, rs, :], ref[8 + facing, rs, :], ref[5, rs, :]
            up = jnp.where(row_at(width, 0), carried, pltpu.roll(cx, 1, 0))
            carried = cx[ROWS - 1 :, :]
            left = jnp.where(lane == 0, 0.0, pltpu.roll(cy, 1, 1))
            diag = ref[6 + facing, rs, :] + cx + cy + up + left + ref[4, rs, :]
            inv = 1.0 / (diag + via)
            pay_ref[rs, :] = jnp.where(upper, diag, via)
            pay_ref[half + k * ROWS : half + (k + 1) * ROWS, :] = jnp.where(upper, seen, seen * inv)
            if 2 * k * ROWS >= half:
                at = 3 * half // 2 + k * ROWS
                pay_ref[at : at + ROWS, :] = inv
    pay_send_ref[5 * half // 2 :, :] = stack_rows([middle_ref[...], last_ref[...], jnp.zeros((ROWS - 4, width), F32)])
    for copy in copies[-2:]:
        copy.wait()


def theirs():
    return (core() == 1) == upper_chip()


def pay_kernel(mine_ref, got_ref, last_ref, pay_ref, more_ref, all_last_ref):
    half = pay_ref.shape[0]
    end = 5 * half // 2
    pay_ref[...] = jnp.where(theirs(), got_ref[0:half, :], mine_ref[0:half, :])
    more_ref[...] = jnp.where(theirs(), got_ref[half:end, :], mine_ref[half:, :])
    own, other = last_ref[...], got_ref[end + 2 : end + 4, :]
    all_last_ref[...] = stack_rows([jnp.where(core() == 0, own, other), jnp.where(core() == 0, other, own)])


def place_of(owner, band):
    n = 2 * owner + band
    return jnp.where(upper_chip(), n, 3 - n)


def prepare_kernel(
    mine_ref, got_ref, middle_ref, more_ref, last_ref,
    cx_ref, cy_ref, c_ref, diag_ref, inv_ref, s_ref, part_ref, seen_o_ref, edge_ref, cap_ref, seen_ref, all_part, all_seen,
):
    half, width = part_ref.shape
    me = core()
    upper = upper_chip()
    lane = lax.broadcasted_iota(jnp.int32, (ROWS, width), 1)
    first_tile = jnp.logical_and(me == 0, lax.axis_index("tile") == 0)
    own_edge = jnp.where(me == 1, middle_ref[...], last_ref[0:2, :])
    got_edge = jnp.where(me == 1, more_ref[5 * half // 2 : 5 * half // 2 + 2, :], last_ref[2:4, :])
    c_ref[0] = jnp.zeros((half, width), F32)
    for owner, ref, edges in ((me, mine_ref, own_edge), (1 - me, got_ref, got_edge)):
        for band in range(2):
            j = place_of(owner, band)
            carried = jnp.where(first_tile, 0.0, edges[band : band + 1, :])
            edge_ref[pl.ds(j, 1), :] = carried
            cx_ref[j] = ref[band]
            cap_ref[j] = ref[10 + band]
            seen_ref[j] = ref[12 + band]
            all_seen[j] = ref[8 + band]
            via_at = jnp.where(upper, j + 1, j)

            @pl.when(via_at < 4)
            def _():
                c_ref[via_at] = ref[4 + band]

            for k in range(half // ROWS):
                rs = slice(k * ROWS, (k + 1) * ROWS)
                cx, cy, diag = (ref[2 * n + band, rs, :] for n in (0, 1, 3))
                cut = jnp.where(lane == width - 1, 0.0, cy)
                up = jnp.where(row_at(width, 0), carried, pltpu.roll(cx, 1, 0))
                carried = cx[ROWS - 1 :, :]
                cy_ref[j, rs, :] = cut
                all_part[j, rs, :] = diag + cx + cy + up + pltpu.roll(cut, 1, 1)
    part_ref[...] = all_part[0] + c_ref[1]
    seen_o_ref[...] = all_seen[0]
    for j in range(1, 4):
        for k in range(half // ROWS):
            rs = slice(k * ROWS, (k + 1) * ROWS)
            diag = all_part[j, rs, :] + c_ref[j, rs, :]
            if j < 3:
                diag = diag + c_ref[j + 1, rs, :]
            inv = 1.0 / diag
            diag_ref[j - 1, rs, :] = diag
            inv_ref[j - 1, rs, :] = inv
            s_ref[j - 1, rs, :] = all_seen[j, rs, :] * inv


def outer_kernel(
    part_ref, seen_ref, link_ref, cx_ref, cy_ref, c_ref, inv_i_ref, s_i_ref,
    c_out_ref, diag_ref, inv_ref, s_ref, core_ref, cross_ref, fix_ref,
):
    rows, width = part_ref.shape
    upper = upper_chip()
    for k in range(rows // ROWS):
        rs = slice(k * ROWS, (k + 1) * ROWS)
        c_out = jnp.where(upper, link_ref[rs, :], c_ref[0, rs, :])
        diag = part_ref[rs, :] + c_out
        inv = 1.0 / diag
        c_out_ref[rs, :] = c_out
        diag_ref[rs, :] = diag
        inv_ref[rs, :] = inv
        s_ref[rs, :] = seen_ref[rs, :] * inv
    ends = []
    for r, beyond in ((0, 0), (rows - 1, rows - 2)):
        at = slice(r, r + 1)
        lines = [band_of(s_ref, s_i_ref, j)[at, :] for j in range(4)]
        lines += [band_of(inv_ref, inv_i_ref, j)[at, :] for j in range(4)]
        lines += [cy_ref[j, at, :] for j in range(4)]
        lines += [c_out_ref[at, :]] + [c_ref[j, at, :] for j in range(1, 4)]
        lines += [cx_ref[j, beyond : beyond + 1, :] for j in range(4)]
        ends.append(stack_rows(lines))
    put_rows(ends[0], ends[1], core_ref, cross_ref)
    fix_ref[...] = jnp.where(upper, diag_ref[0:1, :], s_ref[0:1, :])


def own_parts(u_o_ref, u_i_ref, cx_ref, cy_ref, c_ref, pay_ref, scratch_ref):
    rows, width = u_o_ref.shape
    chunks = rows // ROWS
    none = jnp.zeros((1, width), F32)
    carried = none
    for k in range(chunks):
        rs = slice(k * ROWS, (k + 1) * ROWS)
        x, part, carried = in_band(u_o_ref, cx_ref.at[0], cy_ref.at[0], carried, none, k, chunks)
        pay_ref[rs, :] = x
        scratch_ref[rs, :] = part + c_ref[1, rs, :] * u_i_ref[0, rs, :]
    size = rows // 2
    first = jnp.where(upper_chip(), 0, rows - size)
    pay_ref[rows : rows + size, :] = scratch_ref[pl.ds(pl.multiple_of(first, ROWS), size), :]


def spread_kernel(
    u_o_ref, u_i_ref, core_ref, cross_ref, cx_ref, cy_ref, c_ref, inv_i_ref, edge_ref, v_i_ref, part_ref, sums_ref
):
    above, below = take_rows(core_ref, cross_ref)
    spread_rows(u_o_ref, u_i_ref, above, below, cx_ref, cy_ref, c_ref, inv_i_ref, edge_ref, v_i_ref, part_ref, sums_ref)


def spread_rows(u_o_ref, u_i_ref, above, below, cx_ref, cy_ref, c_ref, inv_i_ref, edge_ref, v_i_ref, part_ref, sums_ref):
    rows, width = u_o_ref.shape
    chunks = rows // ROWS
    carried = [edge_ref[j : j + 1, :] * above[j : j + 1] for j in range(4)]
    sums = [jnp.zeros((ROWS, width), F32) for _ in range(2)]
    for k in range(chunks):
        rs = slice(k * ROWS, (k + 1) * ROWS)
        xs, parts = [], []
        for j in range(4):
            x, part, carried[j] = in_band(
                band_of(u_o_ref, u_i_ref, j), cx_ref.at[j], cy_ref.at[j], carried[j], below[j : j + 1], k, chunks
            )
            xs.append(x)
            parts.append(part)
        parts = couple(xs, parts, c_ref, rs)
        part_ref[rs, :] = parts[0]
        for j in range(1, 4):
            v = inv_i_ref[j - 1, rs, :] * parts[j]
            v_i_ref[j - 1, rs, :] = v
            sums[0] = sums[0] + xs[j] * parts[j]
            sums[1] = sums[1] + v * parts[j]
    sums_ref[0:ROWS, :] = fold(sums[0])
    sums_ref[ROWS : 2 * ROWS, :] = fold(sums[1])


def beside(u_o_ref, u_i_ref, above, below, side_above, side_below, edge_ref, cx_ref):
    rows, width = u_o_ref.shape
    here = stack_rows([above[0:4], below[0:4]])
    beyond = stack_rows([above[4:8], below[4:8]])
    inside = [band_of(u_o_ref, u_i_ref, j)[r : r + 1, :] for r in (0, rows - 1) for j in range(4)]
    toward = stack_rows([edge_ref[...]] + [cx_ref[j, rows - 1 :, :] for j in range(4)])
    inv, cy, c, away = (stack_rows([side_above[n : n + 4], side_below[n : n + 4]]) for n in (4, 8, 12, 16))
    c = jnp.where(jnp.logical_or(row_at(width, 0), row_at(width, 4)), 0.0, c)
    total = toward * stack_rows(inside) + away * beyond
    total = total + cy * pltpu.roll(here, width - 1, 1) + pltpu.roll(cy * here, 1, 1)
    return total + c * pltpu.roll(here, 1, 0) + pltpu.roll(c * here, ROWS - 1, 0), inv


def two_spread_kernel(
    u_o_ref, u_i_ref, core_ref, cross_ref, cx_ref, cy_ref, c_ref, inv_i_ref, edge_ref, side_core_ref, side_cross_ref,
    v_i_ref, part_ref, sums_ref, tail_ref, beside_ref, total_ref, w_ref=None,
):
    rows, width = u_o_ref.shape
    chunks = rows // ROWS
    above, below = take_rows(core_ref, cross_ref)
    spread_rows(u_o_ref, u_i_ref, above, below, cx_ref, cy_ref, c_ref, inv_i_ref, edge_ref, v_i_ref, part_ref, sums_ref)
    fluxes = [edge_ref[0:1, :] * above[0:1], cx_ref[0, rows - 1 :, :] * below[0:1]]
    tail_ref[...] = stack_rows([above[0:1], below[0:1], *fluxes])
    side_above, side_below = take_rows(side_core_ref, side_cross_ref)
    parts_there, inv = beside(u_o_ref, u_i_ref, above, below, side_above, side_below, edge_ref, cx_ref)
    beside_ref[...] = parts_there
    v_there = inv * parts_there
    carried = [edge_ref[j : j + 1, :] * v_there[j : j + 1] for j in range(1, 4)]
    total = jnp.zeros((ROWS, width), F32)
    for k in range(chunks):
        rs = slice(k * ROWS, (k + 1) * ROWS)
        xs, parts = [], []
        for j in range(1, 4):
            x, part, carried[j - 1] = in_band(
                v_i_ref.at[j - 1], cx_ref.at[j], cy_ref.at[j], carried[j - 1], v_there[4 + j : 5 + j], k, chunks
            )
            xs.append(x)
            parts.append(part)
        parts = couple(xs, parts, c_ref.at[pl.ds(1, 3)], rs)
        for j in range(3):
            total = total + xs[j] * parts[j]
            if w_ref is not None:
                w_ref[j, rs, :] = parts[j]
    total_ref[...] = fold(total)


def far_first_kernel(
    u_o_ref, part_ref, got_ref, more_ref, fix_ref, c_out_ref, inv_ref, v_i_ref, sums_ref, cx_ref, cy_ref, c_ref,
    v_ref, core_ref, cross_ref, total_ref, pay_ref, inv_far_ref, scratch_ref,
):
    rows, width = u_o_ref.shape
    upper = upper_chip()
    total = jnp.zeros((ROWS, width), F32)
    for k in range(rows // ROWS):
        rs = slice(k * ROWS, (k + 1) * ROWS)
        c_out = c_out_ref[rs, :]
        diag, far = got_ref[rs, :] + c_out, more_ref[rs, :]
        if k == 0:
            first = jnp.broadcast_to(fix_ref[0:1, :], far.shape)
            diag = jnp.where(row_at(width, 0), first, diag)
            far = jnp.where(jnp.logical_and(upper, row_at(width, 0)), first, far)
        inv_far = 1.0 / jnp.where(upper, 1.0, diag)
        if k * ROWS < rows // 2:
            inv_far_ref[rs, :] = jnp.where(upper, more_ref[rows + k * ROWS : rows + (k + 1) * ROWS, :], inv_far)
        far = jnp.where(upper, far, far * inv_far)
        part = part_ref[rs, :] + c_out * far
        v = inv_ref[rs, :] * part
        v_ref[rs, :] = v
        total = total + v * part
    total_ref[...] = fold(total) + sums_ref[ROWS : 2 * ROWS, :]
    put_two_rows(v_ref, v_i_ref, core_ref, cross_ref)
    own_parts(v_ref, v_i_ref, cx_ref, cy_ref, c_ref, pay_ref, scratch_ref)


def far_kernel(u_o_ref, got_ref, part_ref, sums_ref, c_out_ref, inv_ref, v_ref, totals_ref):
    rows, width = u_o_ref.shape
    sums = [jnp.zeros((ROWS, width), F32) for _ in range(2)]
    for k in range(rows // ROWS):
        rs = slice(k * ROWS, (k + 1) * ROWS)
        part = part_ref[rs, :] + c_out_ref[rs, :] * got_ref[rs, :]
        v = inv_ref[rs, :] * part
        v_ref[rs, :] = v
        sums[0] = sums[0] + u_o_ref[rs, :] * part
        sums[1] = sums[1] + v * part
    totals_ref[0:ROWS, :] = fold(sums[0]) + sums_ref[0:ROWS, :]
    totals_ref[ROWS : 2 * ROWS, :] = fold(sums[1]) + sums_ref[ROWS : 2 * ROWS, :]


def finish_kernel(
    u_o_ref, v_ref, got_ref, tail_ref, v_i_ref, totals_ref, beside_ref, inner_ref, inv_far_ref,
    cx_ref, cy_ref, c_ref, c_out_ref, edge_ref, side_core_ref, side_cross_ref, t0_ref,
    mail_ref, w_ref=None, fix_ref=None,
):
    rows, width = u_o_ref.shape
    chunks = rows // ROWS
    none = jnp.zeros((1, width), F32)
    sums = [jnp.zeros((ROWS, width), F32) for _ in range(2)]
    carried = none
    for k in range(chunks):
        rs = slice(k * ROWS, (k + 1) * ROWS)
        v, part, carried = in_band(v_ref, cx_ref.at[0], cy_ref.at[0], carried, none, k, chunks)
        coupled = c_ref[1, rs, :] * v_i_ref[0, rs, :]
        sums[0] = sums[0] + v * (part + 2.0 * coupled)
        if w_ref is not None:
            w_ref[rs, :] = part + coupled
    side_above, side_below = take_rows(side_core_ref, side_cross_ref)
    up = side_above[4:5] * (beside_ref[0:1, :] + side_above[12:13] * tail_ref[0:1, :])
    down = side_below[4:5] * (beside_ref[4:5, :] + side_below[12:13] * tail_ref[1:2, :])
    up = edge_ref[0:1, :] * up
    down = cx_ref[0, rows - 1 :, :] * down
    if fix_ref is not None:
        fix_ref[...] = stack_rows([up, down])
    size = rows // 2
    first = jnp.where(upper_chip(), rows - size, 0)
    far_up = jnp.where(first == 0, tail_ref[2:3, :], 0.0)
    far_down = jnp.where(first + size == rows, tail_ref[3:4, :], 0.0)
    for k in range(size // ROWS):
        at = pl.ds(pl.multiple_of(first + k * ROWS, ROWS), ROWS)
        c_out = c_out_ref[at, :]
        part = got_ref[rows + k * ROWS : rows + (k + 1) * ROWS, :] + c_out * u_o_ref[at, :]
        if k == 0:
            part = part + jnp.where(row_at(width, 0), far_up, 0.0)
        if k == size // ROWS - 1:
            part = part + jnp.where(row_at(width, ROWS - 1), far_down, 0.0)
        sums[1] = sums[1] + v_ref[at, :] * (c_out * (inv_far_ref[k * ROWS : (k + 1) * ROWS, :] * part))
    ends = up * v_ref[0:1, :] + down * v_ref[rows - 1 :, :]
    last = fold(sums[0] + 2.0 * sums[1] + jnp.where(row_at(width, 0), ends, 0.0)) + inner_ref[...]
    terms = (t0_ref[...], totals_ref[0:ROWS, :], totals_ref[ROWS : 2 * ROWS, :], last)
    lane = lax.broadcasted_iota(jnp.int32, (ROWS, 128), 1)
    row = jnp.zeros((ROWS, 128), F32)
    for n, t in enumerate(terms):
        t = t + pltpu.roll(t, 64, 1)
        t = t + pltpu.roll(t, 32, 1)
        row = jnp.where(lane // 32 == n, t, row)
    row = jnp.broadcast_to(jnp.sum(row, 0, keepdims=True), (ROWS, 128))
    for at in range(0, mail_ref.shape[0], ROWS):
        mail_ref[at : at + ROWS, :] = row


def weights(mail_ref):
    block = mail_ref[0:ROWS, :]
    for at in range(ROWS, mail_ref.shape[0], ROWS):
        block = block + mail_ref[at : at + ROWS, :]
    block = jnp.sum(block, 0, keepdims=True)
    g0, g1, g2, g3 = (jnp.sum(block[:, 32 * k : 32 * (k + 1)], 1, keepdims=True) for k in range(4))
    mu = g1 / g0
    h = g2 - mu * g1
    t = h / (h - (g3 - 2.0 * mu * g2 + mu * mu * g1))
    a = g0 / (g0 - g1 - h * t)
    b = t * a
    return a - mu * b, b


def hand_out(j, value, k, holds_outer, mine_ref, send_ref, first, half):
    band = jnp.where(upper_chip(), j % 2, 1 - j % 2)
    size = value.shape[0]
    if holds_outer == (j < 2):
        mine_ref[band, k * ROWS : k * ROWS + size, :] = value
    else:
        send_ref[pl.ds(pl.multiple_of(first + band * half + k * ROWS, ROWS), size), :] = value


def for_holder(body):
    outer = (core() == 1) != upper_chip()
    pl.when(outer)(lambda: body(True))
    pl.when(jnp.logical_not(outer))(lambda: body(False))


def step_kernel(
    mail_ref, s_o_ref, s_i_ref, v1_o_ref, v1_i_ref, v2_o_ref, v2_i_ref, part_i_ref, part_ref, far_ref, fix_ref, cap_ref, seen_ref,
    diag_o_ref, diag_i_ref, inv_o_ref, inv_i_ref, cx_ref, cy_ref, c_ref, c_out_ref,
    z_o_ref, z_i_ref, core_ref, cross_ref, total_ref, pay_ref, x_mine_ref, z_mine_ref, scratch_ref,
):
    rows, width = s_o_ref.shape
    chunks = rows // ROWS
    a, b = weights(mail_ref)

    def run(holds_outer):
        total = jnp.zeros((ROWS, width), F32)
        for j in range(4):
            for k in range(chunks):
                rs = slice(k * ROWS, (k + 1) * ROWS)
                s, p, q, diag, inv = (
                    band_of(o, i, j)[rs, :]
                    for o, i in (
                        (s_o_ref, s_i_ref), (v1_o_ref, v1_i_ref), (v2_o_ref, v2_i_ref),
                        (diag_o_ref, diag_i_ref), (inv_o_ref, inv_i_ref),
                    )
                )
                if j == 0:
                    part = part_ref[rs, :] + c_out_ref[rs, :] * far_ref[rs, :]
                    if k == 0:
                        part = part + jnp.where(row_at(width, 0), fix_ref[0:1, :], 0.0)
                    if k == chunks - 1:
                        part = part + jnp.where(row_at(width, ROWS - 1), fix_ref[1:2, :], 0.0)
                else:
                    part = part_i_ref[j - 1, rs, :]
                    if j == 1:
                        part = part + c_ref[1, rs, :] * v2_o_ref[rs, :]
                r = inv * part
                x = s + a * p + b * q
                residual = cap_ref[j, rs, :] * x + seen_ref[j, rs, :] - diag * (x - (p + a * q + b * r))
                z = residual * inv
                band_of(z_o_ref, z_i_ref, j)[rs, :] = z
                total = total + residual * z
                hand_out(j, x, k, holds_outer, x_mine_ref, core_ref, ROWS, rows)
                hand_out(j, z, k, holds_outer, z_mine_ref, core_ref, ROWS + 2 * rows, rows)
        total_ref[...] = fold(total)

    for_holder(run)
    put_two_rows(z_o_ref, z_i_ref, core_ref.at[0:ROWS], cross_ref)
    own_parts(z_o_ref, z_i_ref, cx_ref, cy_ref, c_ref, pay_ref, scratch_ref)


def give_kernel(q_o_ref, q_i_ref, mine_ref, send_ref):
    rows = q_o_ref.shape[0]

    def run(holds_outer):
        for j in range(4):
            hand_out(j, band_of(q_o_ref, q_i_ref, j)[...], 0, holds_outer, mine_ref, send_ref, 0, rows)

    for_holder(run)


def out_rows(out_ref, step, band, which):
    return out_ref.at[step, band, half_of(which, out_ref.shape[2] // 2), :]


def later_out_kernel(x_mine_ref, got_ref, out_ref, sems):
    half = x_mine_ref.shape[1]
    pairs = []
    for band in range(2):
        at = ROWS + band * half
        pairs.append((x_mine_ref.at[band], out_rows(out_ref, 1, band, core())))
        pairs.append((got_ref.at[at : at + half], out_rows(out_ref, 1, band, 1 - core())))
    for copy in start_copies(pairs, sems):
        copy.wait()


def last_kernel(_, mail_ref, x_mine_ref, z_mine_ref, got_ref, q_mine_ref, q_got_ref, out_ref, answer, sems):
    half = x_mine_ref.shape[1]
    a, b = weights(mail_ref)
    copies = []
    for band in range(2):
        at = ROWS + band * half
        got = got_ref.at[at : at + half], got_ref.at[at + 2 * half : at + 3 * half], q_got_ref.at[band * half : (band + 1) * half]
        mine = [ref.at[band] for ref in (x_mine_ref, z_mine_ref, q_mine_ref)]
        for which, (x_ref, z_ref, q_ref) in ((core(), mine), (1 - core(), got)):
            n = len(copies)
            answer[n] = x_ref[...] + a * z_ref[...] + b * q_ref[...]
            copies.append(pltpu.make_async_copy(answer.at[n], out_rows(out_ref, 0, band, which), sems.at[n]))
            copies[-1].start()
    for copy in copies:
        copy.wait()


def on_device(cond_x, cond_y, via_cond, via_mask, capacitance, pad_mask, observe):
    _, rows, width = cond_x.shape
    half = rows // 2
    field, three, four, edge = shape(half, width), shape(3, half, width), shape(4, half, width), shape(4, width)
    eight, twenty = shape(ROWS, width), shape(20, width)
    most, part_rows = shape(3 * half // 2, width), shape(half // 2, width)
    rim, pair = shape(2, width), shape(2, half, width)
    mail = shape(lax.axis_size("band") * lax.axis_size("tile"), 128)
    one, two = shape(ROWS, 128), shape(2 * ROWS, 128)
    fourteen = shape(14, half, width)
    whole, whole_int = pltpu.VMEM((2, rows, width), F32), pltpu.VMEM((2, rows, width), jnp.int32)
    own, send, pay, pay_send, last, middle = call(
        load_kernel, [fourteen, fourteen, shape(5 * half // 2, width), shape(5 * half // 2 + ROWS, width), rim, rim],
        cond_x, cond_y, via_cond, via_mask, capacitance, pad_mask, observe, name="load", place=pltpu.HBM,
        scratch=[whole, whole_int, whole_int, pltpu.VMEM((2, 2, ROWS, width), F32), pltpu.SemaphoreType.DMA((15,))],
    )
    more = core_swap(pay_send)
    more, send = lax.optimization_barrier((more, send))
    pay, pay_more, last = call(pay_kernel, [field, most, edge], pay, more, last, name="pay")
    link, traded, last = outer_swap(pay), core_swap(send), cross_swap(last)
    pay_more, last = lax.optimization_barrier((pay_more, last))
    far = outer_swap(pay_more)
    cx, cy, c, diag_i, inv_i, s_i, part, seen, cx_edge, cap, earlier = call(
        prepare_kernel, [four, four, four, three, three, three, field, field, edge, four, four],
        own, traded, middle, more, last, name="prepare",
        scratch=[pltpu.VMEM((4, half, width), F32), pltpu.VMEM((4, half, width), F32)],
    )
    c_out, diag_o, inv_o, s_o, near, cross, fix = call(
        outer_kernel, [field, field, field, field, twenty, twenty, shape(1, width)],
        part, seen, link, cx, cy, c, inv_i, s_i, name="outer",
    )
    fix, sides = outer_swap(fix), (core_swap(near), cross_swap(cross))

    coeffs = (cx, cy, c, inv_i, cx_edge)
    parts_of = [pltpu.VMEM((half, width), F32)]
    v1_i, part, sums = call(spread_kernel, [three, field, two], s_o, s_i, *sides, *coeffs, name="first_spread")
    v1_o, near, cross, t0, pay, inv_far = call(
        far_first_kernel, [field, eight, eight, one, most, part_rows],
        s_o, part, link, far, fix, c_out, inv_o, v1_i, sums, cx, cy, c, name="first_far", scratch=parts_of,
    )

    def stage(u_o, u_i, pay, near, cross, t0, name, x_mine=None):
        further = x_mine is None
        got, cross, near = outer_swap(pay), cross_swap(cross), core_swap(near)
        v_i, part, sums, tail, there, inner, *w_i = call(
            two_spread_kernel, [three, field, two, edge, eight, one] + [three] * further,
            u_o, u_i, near, cross, *coeffs, *sides, name=name + "_spread",
        )
        if not further:
            (out,) = call(
                later_out_kernel, [shape(2, 2, rows, width)], x_mine, near, name="later_out", out_place=pl.ANY,
                scratch=[pltpu.SemaphoreType.DMA((4,))],
            )
            part, out = lax.optimization_barrier((part, out))
        v_o, totals = call(far_kernel, [field, two], u_o, got, part, sums, c_out, inv_o, name=name + "_far")
        if further:
            more = (outer_swap(v_o),)
        else:
            mine, send = call(give_kernel, [pair, shape(2 * half, width)], v_o, v_i, name="give")
            more = out, near, mine, core_swap(send)
        parts, *rest = call(
            finish_kernel, [mail] + [field, rim] * further,
            u_o, v_o, got, outer_swap(tail), v_i, totals, there, inner, inv_far,
            cx, cy, c, c_out, cx_edge, *sides, t0, name=name + "_finish",
        )
        more = *w_i, *rest, *more
        return v_o, v_i, all_total(parts), more

    v2_o, v2_i, total, (part_i, part, fix, far) = stage(v1_o, v1_i, pay, near, cross, t0, "later")
    z_o, z_i, near, cross, t0, pay, x_mine, z_mine = call(
        step_kernel,
        [field, three, shape(ROWS + 4 * half, width), eight, one, most, pair, pair],
        total, s_o, s_i, v1_o, v1_i, v2_o, v2_i, part_i, part, far, fix, cap, earlier, diag_o, diag_i, inv_o, inv_i, cx, cy, c, c_out,
        name="step", scratch=parts_of,
    )
    _, _, total, (out, got, q_mine, q_got) = stage(z_o, z_i, pay, near, cross, t0, "earlier", x_mine)
    (out,) = call(
        last_kernel, [shape(2, 2, rows, width)], out, total, x_mine, z_mine, got, q_mine, q_got, name="last",
        out_place=pl.ANY, scratch=[pltpu.VMEM((4, half, width), F32), pltpu.SemaphoreType.DMA((4,))], reuse=True,
    )
    return out


def solution(mesh):
    placed = (P("band", "tile", None),) * 6 + (P(None, "band", "tile", None),)
    return jax.shard_map(
        on_device,
        mesh=mesh,
        in_specs=placed,
        out_specs=P(None, "band", "tile", None),
        check_vma=False,
    )
```

```python
import jax
import jax.numpy as jnp
from jax import lax
from jax.experimental import pallas as pl
from jax.experimental.pallas import tpu as pltpu
from jax.sharding import PartitionSpec as P

NB = 8
ROWS = 8
AXES = ("band", "tile")
F32 = jnp.float32

pad_conductance = 4.0

COSTS = {"prepare": 0, "first_spread": 0, "later_spread": 0, "earlier_spread": 0, "later_out": 0}


def sizes():
    return lax.axis_size("band"), lax.axis_size("tile")


def core():
    return lax.rem(lax.axis_index("band"), 2)


def upper_chip():
    return lax.axis_index("band") >= 2


def core_swap(x):
    nb, _ = sizes()
    return lax.ppermute(x, "band", [(b, b ^ 1) for b in range(nb)])


def outer_swap(x):
    nb, _ = sizes()
    return lax.ppermute(x, "band", [(b, b ^ 2) for b in range(nb)])


def cross_swap(x):
    nb, nt = sizes()
    pairs = []
    for b in range(nb):
        for t in range(nt):
            other = (t + 1) % nt if b % 2 else (t - 1) % nt
            pairs.append((b * nt + t, (b ^ 1) * nt + other))
    return lax.ppermute(x, AXES, pairs)


def all_total(parts):
    return lax.all_to_all(parts, AXES, 0, 0, tiled=True)


def call(body, outs, *args, name, place=pltpu.VMEM, out_place=pltpu.VMEM, scratch=(), limit=10, reuse=False):
    cost = COSTS.get(name, 10)
    if place == pltpu.HBM:
        args = [pltpu.with_memory_space_constraint(a, pltpu.HBM) for a in args]
    return pl.pallas_call(
        body,
        out_shape=outs,
        in_specs=[pl.BlockSpec(memory_space=pl.ANY if reuse and n == 0 else place) for n in range(len(args))],
        input_output_aliases={0: 0} if reuse else {},
        out_specs=[pl.BlockSpec(memory_space=out_place)] * len(outs),
        scratch_shapes=list(scratch),
        name=name,
        cost_estimate=pl.CostEstimate(flops=cost * 10**9, bytes_accessed=cost * 10**6, transcendentals=0),
        compiler_params=pltpu.CompilerParams(vmem_limit_bytes=limit * 1024 * 1024),
    )(*args)


def shape(*dims):
    return jax.ShapeDtypeStruct(dims, F32)


def row_at(width, at):
    return lax.broadcasted_iota(jnp.int32, (ROWS, width), 0) == at


def stack_rows(rows):
    return jnp.concatenate(rows, 0)


def put_rows(first, last, core_ref, cross_ref):
    lower = core() == 1
    core_ref[...] = jnp.where(lower, first, last)
    cross_ref[...] = jnp.where(lower, last, first)


def put_two_rows(u_o_ref, u_i_ref, core_ref, cross_ref):
    rows = u_o_ref.shape[0]
    ends = [
        stack_rows([band_of(u_o_ref, u_i_ref, j)[r : r + 1, :] for r in pair for j in range(4)])
        for pair in ((0, 1), (rows - 1, rows - 2))
    ]
    put_rows(ends[0], ends[1], core_ref, cross_ref)


def take_rows(core_ref, cross_ref):
    lower = core() == 1
    tile = lax.axis_index("tile")
    cross = cross_ref[...]
    near = core_ref[0 : cross.shape[0], :]
    above = jnp.where(lower, near, jnp.where(tile == 0, 0.0, cross))
    below = jnp.where(lower, jnp.where(tile == lax.axis_size("tile") - 1, 0.0, cross), near)
    return above, below


def fold(total):
    acc = total[:, :128]
    for at in range(128, total.shape[1], 128):
        acc = acc + total[:, at : at + 128]
    return acc


def band_of(u_o_ref, u_i_ref, j):
    return u_o_ref if j == 0 else u_i_ref.at[j - 1]


def in_band(v_ref, cx_ref, cy_ref, carried, below, k, chunks):
    width = v_ref.shape[-1]
    r = k * ROWS
    x = v_ref[r : r + ROWS, :]
    cx = cx_ref[r : r + ROWS, :]
    cy = cy_ref[r : r + ROWS, :]
    after = below if k == chunks - 1 else v_ref[r + ROWS : r + ROWS + 1, :]
    down = jnp.where(row_at(width, ROWS - 1), after, pltpu.roll(x, ROWS - 1, 0))
    flux = cx * x
    up = jnp.where(row_at(width, 0), carried, pltpu.roll(flux, 1, 0))
    total = cx * down + up + cy * pltpu.roll(x, width - 1, 1) + pltpu.roll(cy * x, 1, 1)
    return x, total, flux[ROWS - 1 :, :]


def couple(xs, parts, c_ref, rs):
    parts = list(parts)
    for j in range(1, len(xs)):
        c = c_ref[j, rs, :]
        parts[j] = parts[j] + c * xs[j - 1]
        parts[j - 1] = parts[j - 1] + c * xs[j]
    return parts


def half_of(which, half):
    return pl.ds(pl.multiple_of(which * half, ROWS), half)


def start_copies(pairs, sems):
    copies = [pltpu.make_async_copy(source, to, sems.at[n]) for n, (source, to) in enumerate(pairs)]
    for copy in copies:
        copy.start()
    return copies


def load_kernel(
    cond_x_ref, cond_y_ref, via_ref, mask_ref, cap_ref, pad_ref, observe_ref,
    mine_ref, send_ref, pay_mine_ref, pay_send_ref, last_ref, middle_ref,
    via_at, mask_at, pad_at, edge_at, sems,
):
    half, width = send_ref.shape[1:]
    me = core()
    upper = upper_chip()
    halves = ((send_ref, pay_send_ref, 1 - me), (mine_ref, pay_mine_ref, me))
    pairs = [(via_ref, via_at), (mask_ref, mask_at), (pad_ref, pad_at)]
    pairs.append((cond_x_ref.at[:, pl.ds(half - ROWS, ROWS), :], edge_at.at[0]))
    pairs.append((cond_x_ref.at[:, pl.ds(2 * half - ROWS, ROWS), :], edge_at.at[1]))
    for ref, _, which in halves:
        rs = half_of(which, half)
        pairs += [
            (cond_x_ref.at[:, rs, :], ref.at[0:2]),
            (cond_y_ref.at[:, rs, :], ref.at[2:4]),
            (observe_ref.at[1, :, rs, :], ref.at[8:10]),
            (cap_ref.at[:, rs, :], ref.at[10:12]),
        ]
    for ref, _, which in halves:
        pairs.append((observe_ref.at[0, :, half_of(which, half), :], ref.at[12:14]))
    copies = start_copies(pairs, sems)
    for copy in copies[:5]:
        copy.wait()
    for band in range(2):
        middle_ref[band : band + 1, :] = edge_at[0, band, ROWS - 1 :, :]
        last_ref[band : band + 1, :] = edge_at[1, band, ROWS - 1 :, :]
    lane = lax.broadcasted_iota(jnp.int32, (ROWS, width), 1)
    facing = jnp.where(upper, 0, 1)
    for n, (ref, pay_ref, which) in enumerate(halves):
        for copy in copies[5 + 4 * n : 9 + 4 * n]:
            copy.wait()
        rs = half_of(which, half)
        for band in range(2):
            ref[4 + band] = via_at[band, rs, :] * mask_at[band, rs, :].astype(F32)
            ref[6 + band] = ref[10 + band] + pad_conductance * pad_at[band, rs, :].astype(F32)
        carried = jnp.where(which == 0, 0.0, edge_at[0, facing, ROWS - 1 :, :])
        for k in range(half // ROWS):
            rs = slice(k * ROWS, (k + 1) * ROWS)
            cx, cy, seen, via = ref[facing, rs, :], ref[2 + facing, rs, :], ref[8 + facing, rs, :], ref[5, rs, :]
            up = jnp.where(row_at(width, 0), carried, pltpu.roll(cx, 1, 0))
            carried = cx[ROWS - 1 :, :]
            left = jnp.where(lane == 0, 0.0, pltpu.roll(cy, 1, 1))
            diag = ref[6 + facing, rs, :] + cx + cy + up + left + ref[4, rs, :]
            inv = 1.0 / (diag + via)
            pay_ref[rs, :] = jnp.where(upper, diag, via)
            pay_ref[half + k * ROWS : half + (k + 1) * ROWS, :] = jnp.where(upper, seen, seen * inv)
            if 2 * k * ROWS >= half:
                at = 3 * half // 2 + k * ROWS
                pay_ref[at : at + ROWS, :] = inv
    pay_send_ref[5 * half // 2 :, :] = stack_rows([middle_ref[...], last_ref[...], jnp.zeros((ROWS - 4, width), F32)])
    for copy in copies[-2:]:
        copy.wait()


def theirs():
    return (core() == 1) == upper_chip()


def pay_kernel(mine_ref, got_ref, last_ref, pay_ref, more_ref, all_last_ref):
    half = pay_ref.shape[0]
    end = 5 * half // 2
    pay_ref[...] = jnp.where(theirs(), got_ref[0:half, :], mine_ref[0:half, :])
    more_ref[...] = jnp.where(theirs(), got_ref[half:end, :], mine_ref[half:, :])
    own, other = last_ref[...], got_ref[end + 2 : end + 4, :]
    all_last_ref[...] = stack_rows([jnp.where(core() == 0, own, other), jnp.where(core() == 0, other, own)])


def place_of(owner, band):
    n = 2 * owner + band
    return jnp.where(upper_chip(), n, 3 - n)


def prepare_kernel(
    mine_ref, got_ref, middle_ref, more_ref, last_ref,
    cx_ref, cy_ref, c_ref, diag_ref, inv_ref, s_ref, part_ref, seen_o_ref, edge_ref, cap_ref, seen_ref, all_part, all_seen,
):
    half, width = part_ref.shape
    me = core()
    upper = upper_chip()
    lane = lax.broadcasted_iota(jnp.int32, (ROWS, width), 1)
    first_tile = jnp.logical_and(me == 0, lax.axis_index("tile") == 0)
    own_edge = jnp.where(me == 1, middle_ref[...], last_ref[0:2, :])
    got_edge = jnp.where(me == 1, more_ref[5 * half // 2 : 5 * half // 2 + 2, :], last_ref[2:4, :])
    c_ref[0] = jnp.zeros((half, width), F32)
    for owner, ref, edges in ((me, mine_ref, own_edge), (1 - me, got_ref, got_edge)):
        for band in range(2):
            j = place_of(owner, band)
            carried = jnp.where(first_tile, 0.0, edges[band : band + 1, :])
            edge_ref[pl.ds(j, 1), :] = carried
            cx_ref[j] = ref[band]
            cap_ref[j] = ref[10 + band]
            seen_ref[j] = ref[12 + band]
            all_seen[j] = ref[8 + band]
            via_at = jnp.where(upper, j + 1, j)

            @pl.when(via_at < 4)
            def _():
                c_ref[via_at] = ref[4 + band]

            for k in range(half // ROWS):
                rs = slice(k * ROWS, (k + 1) * ROWS)
                cx, cy, diag = (ref[2 * n + band, rs, :] for n in (0, 1, 3))
                cut = jnp.where(lane == width - 1, 0.0, cy)
                up = jnp.where(row_at(width, 0), carried, pltpu.roll(cx, 1, 0))
                carried = cx[ROWS - 1 :, :]
                cy_ref[j, rs, :] = cut
                all_part[j, rs, :] = diag + cx + cy + up + pltpu.roll(cut, 1, 1)
    part_ref[...] = all_part[0] + c_ref[1]
    seen_o_ref[...] = all_seen[0]
    for j in range(1, 4):
        for k in range(half // ROWS):
            rs = slice(k * ROWS, (k + 1) * ROWS)
            diag = all_part[j, rs, :] + c_ref[j, rs, :]
            if j < 3:
                diag = diag + c_ref[j + 1, rs, :]
            inv = 1.0 / diag
            diag_ref[j - 1, rs, :] = diag
            inv_ref[j - 1, rs, :] = inv
            s_ref[j - 1, rs, :] = all_seen[j, rs, :] * inv


def outer_kernel(
    part_ref, seen_ref, link_ref, cx_ref, cy_ref, c_ref, inv_i_ref, s_i_ref,
    c_out_ref, diag_ref, inv_ref, s_ref, core_ref, cross_ref, fix_ref,
):
    rows, width = part_ref.shape
    upper = upper_chip()
    for k in range(rows // ROWS):
        rs = slice(k * ROWS, (k + 1) * ROWS)
        c_out = jnp.where(upper, link_ref[rs, :], c_ref[0, rs, :])
        diag = part_ref[rs, :] + c_out
        inv = 1.0 / diag
        c_out_ref[rs, :] = c_out
        diag_ref[rs, :] = diag
        inv_ref[rs, :] = inv
        s_ref[rs, :] = seen_ref[rs, :] * inv
    ends = []
    for r, beyond in ((0, 0), (rows - 1, rows - 2)):
        at = slice(r, r + 1)
        lines = [band_of(s_ref, s_i_ref, j)[at, :] for j in range(4)]
        lines += [band_of(inv_ref, inv_i_ref, j)[at, :] for j in range(4)]
        lines += [cy_ref[j, at, :] for j in range(4)]
        lines += [c_out_ref[at, :]] + [c_ref[j, at, :] for j in range(1, 4)]
        lines += [cx_ref[j, beyond : beyond + 1, :] for j in range(4)]
        ends.append(stack_rows(lines))
    put_rows(ends[0], ends[1], core_ref, cross_ref)
    fix_ref[...] = jnp.where(upper, diag_ref[0:1, :], s_ref[0:1, :])


def own_parts(u_o_ref, u_i_ref, cx_ref, cy_ref, c_ref, pay_ref, scratch_ref):
    rows, width = u_o_ref.shape
    chunks = rows // ROWS
    none = jnp.zeros((1, width), F32)
    carried = none
    for k in range(chunks):
        rs = slice(k * ROWS, (k + 1) * ROWS)
        x, part, carried = in_band(u_o_ref, cx_ref.at[0], cy_ref.at[0], carried, none, k, chunks)
        pay_ref[rs, :] = x
        scratch_ref[rs, :] = part + c_ref[1, rs, :] * u_i_ref[0, rs, :]
    size = rows // 2
    first = jnp.where(upper_chip(), 0, rows - size)
    pay_ref[rows : rows + size, :] = scratch_ref[pl.ds(pl.multiple_of(first, ROWS), size), :]


def spread_kernel(
    u_o_ref, u_i_ref, core_ref, cross_ref, cx_ref, cy_ref, c_ref, inv_i_ref, edge_ref, v_i_ref, part_ref, sums_ref
):
    above, below = take_rows(core_ref, cross_ref)
    spread_rows(u_o_ref, u_i_ref, above, below, cx_ref, cy_ref, c_ref, inv_i_ref, edge_ref, v_i_ref, part_ref, sums_ref)


def spread_rows(u_o_ref, u_i_ref, above, below, cx_ref, cy_ref, c_ref, inv_i_ref, edge_ref, v_i_ref, part_ref, sums_ref):
    rows, width = u_o_ref.shape
    chunks = rows // ROWS
    carried = [edge_ref[j : j + 1, :] * above[j : j + 1] for j in range(4)]
    sums = [jnp.zeros((ROWS, width), F32) for _ in range(2)]
    for k in range(chunks):
        rs = slice(k * ROWS, (k + 1) * ROWS)
        xs, parts = [], []
        for j in range(4):
            x, part, carried[j] = in_band(
                band_of(u_o_ref, u_i_ref, j), cx_ref.at[j], cy_ref.at[j], carried[j], below[j : j + 1], k, chunks
            )
            xs.append(x)
            parts.append(part)
        parts = couple(xs, parts, c_ref, rs)
        part_ref[rs, :] = parts[0]
        for j in range(1, 4):
            v = inv_i_ref[j - 1, rs, :] * parts[j]
            v_i_ref[j - 1, rs, :] = v
            sums[0] = sums[0] + xs[j] * parts[j]
            sums[1] = sums[1] + v * parts[j]
    sums_ref[0:ROWS, :] = fold(sums[0])
    sums_ref[ROWS : 2 * ROWS, :] = fold(sums[1])


def beside(u_o_ref, u_i_ref, above, below, side_above, side_below, edge_ref, cx_ref):
    rows, width = u_o_ref.shape
    here = stack_rows([above[0:4], below[0:4]])
    beyond = stack_rows([above[4:8], below[4:8]])
    inside = [band_of(u_o_ref, u_i_ref, j)[r : r + 1, :] for r in (0, rows - 1) for j in range(4)]
    toward = stack_rows([edge_ref[...]] + [cx_ref[j, rows - 1 :, :] for j in range(4)])
    inv, cy, c, away = (stack_rows([side_above[n : n + 4], side_below[n : n + 4]]) for n in (4, 8, 12, 16))
    c = jnp.where(jnp.logical_or(row_at(width, 0), row_at(width, 4)), 0.0, c)
    total = toward * stack_rows(inside) + away * beyond
    total = total + cy * pltpu.roll(here, width - 1, 1) + pltpu.roll(cy * here, 1, 1)
    return total + c * pltpu.roll(here, 1, 0) + pltpu.roll(c * here, ROWS - 1, 0), inv


def two_spread_kernel(
    u_o_ref, u_i_ref, core_ref, cross_ref, cx_ref, cy_ref, c_ref, inv_i_ref, edge_ref, side_core_ref, side_cross_ref,
    v_i_ref, part_ref, sums_ref, tail_ref, beside_ref, total_ref, w_ref=None,
):
    rows, width = u_o_ref.shape
    chunks = rows // ROWS
    above, below = take_rows(core_ref, cross_ref)
    spread_rows(u_o_ref, u_i_ref, above, below, cx_ref, cy_ref, c_ref, inv_i_ref, edge_ref, v_i_ref, part_ref, sums_ref)
    fluxes = [edge_ref[0:1, :] * above[0:1], cx_ref[0, rows - 1 :, :] * below[0:1]]
    tail_ref[...] = stack_rows([above[0:1], below[0:1], *fluxes])
    side_above, side_below = take_rows(side_core_ref, side_cross_ref)
    parts_there, inv = beside(u_o_ref, u_i_ref, above, below, side_above, side_below, edge_ref, cx_ref)
    beside_ref[...] = parts_there
    v_there = inv * parts_there
    carried = [edge_ref[j : j + 1, :] * v_there[j : j + 1] for j in range(1, 4)]
    total = jnp.zeros((ROWS, width), F32)
    for k in range(chunks):
        rs = slice(k * ROWS, (k + 1) * ROWS)
        xs, parts = [], []
        for j in range(1, 4):
            x, part, carried[j - 1] = in_band(
                v_i_ref.at[j - 1], cx_ref.at[j], cy_ref.at[j], carried[j - 1], v_there[4 + j : 5 + j], k, chunks
            )
            xs.append(x)
            parts.append(part)
        parts = couple(xs, parts, c_ref.at[pl.ds(1, 3)], rs)
        for j in range(3):
            total = total + xs[j] * parts[j]
            if w_ref is not None:
                w_ref[j, rs, :] = parts[j]
    total_ref[...] = fold(total)


def far_first_kernel(
    u_o_ref, part_ref, got_ref, more_ref, fix_ref, c_out_ref, inv_ref, v_i_ref, sums_ref, cx_ref, cy_ref, c_ref,
    v_ref, core_ref, cross_ref, total_ref, pay_ref, inv_far_ref, scratch_ref,
):
    rows, width = u_o_ref.shape
    upper = upper_chip()
    total = jnp.zeros((ROWS, width), F32)
    for k in range(rows // ROWS):
        rs = slice(k * ROWS, (k + 1) * ROWS)
        c_out = c_out_ref[rs, :]
        diag, far = got_ref[rs, :] + c_out, more_ref[rs, :]
        if k == 0:
            first = jnp.broadcast_to(fix_ref[0:1, :], far.shape)
            diag = jnp.where(row_at(width, 0), first, diag)
            far = jnp.where(jnp.logical_and(upper, row_at(width, 0)), first, far)
        inv_far = 1.0 / jnp.where(upper, 1.0, diag)
        if k * ROWS < rows // 2:
            inv_far_ref[rs, :] = jnp.where(upper, more_ref[rows + k * ROWS : rows + (k + 1) * ROWS, :], inv_far)
        far = jnp.where(upper, far, far * inv_far)
        part = part_ref[rs, :] + c_out * far
        v = inv_ref[rs, :] * part
        v_ref[rs, :] = v
        total = total + v * part
    total_ref[...] = fold(total) + sums_ref[ROWS : 2 * ROWS, :]
    put_two_rows(v_ref, v_i_ref, core_ref, cross_ref)
    own_parts(v_ref, v_i_ref, cx_ref, cy_ref, c_ref, pay_ref, scratch_ref)


def far_kernel(u_o_ref, got_ref, part_ref, sums_ref, c_out_ref, inv_ref, v_ref, totals_ref):
    rows, width = u_o_ref.shape
    sums = [jnp.zeros((ROWS, width), F32) for _ in range(2)]
    for k in range(rows // ROWS):
        rs = slice(k * ROWS, (k + 1) * ROWS)
        part = part_ref[rs, :] + c_out_ref[rs, :] * got_ref[rs, :]
        v = inv_ref[rs, :] * part
        v_ref[rs, :] = v
        sums[0] = sums[0] + u_o_ref[rs, :] * part
        sums[1] = sums[1] + v * part
    totals_ref[0:ROWS, :] = fold(sums[0]) + sums_ref[0:ROWS, :]
    totals_ref[ROWS : 2 * ROWS, :] = fold(sums[1]) + sums_ref[ROWS : 2 * ROWS, :]


def finish_kernel(
    u_o_ref, v_ref, got_ref, tail_ref, v_i_ref, totals_ref, beside_ref, inner_ref, inv_far_ref,
    cx_ref, cy_ref, c_ref, c_out_ref, edge_ref, side_core_ref, side_cross_ref, t0_ref,
    mail_ref, w_ref=None, fix_ref=None,
):
    rows, width = u_o_ref.shape
    chunks = rows // ROWS
    none = jnp.zeros((1, width), F32)
    sums = [jnp.zeros((ROWS, width), F32) for _ in range(2)]
    carried = none
    for k in range(chunks):
        rs = slice(k * ROWS, (k + 1) * ROWS)
        v, part, carried = in_band(v_ref, cx_ref.at[0], cy_ref.at[0], carried, none, k, chunks)
        coupled = c_ref[1, rs, :] * v_i_ref[0, rs, :]
        sums[0] = sums[0] + v * (part + 2.0 * coupled)
        if w_ref is not None:
            w_ref[rs, :] = part + coupled
    side_above, side_below = take_rows(side_core_ref, side_cross_ref)
    up = side_above[4:5] * (beside_ref[0:1, :] + side_above[12:13] * tail_ref[0:1, :])
    down = side_below[4:5] * (beside_ref[4:5, :] + side_below[12:13] * tail_ref[1:2, :])
    up = edge_ref[0:1, :] * up
    down = cx_ref[0, rows - 1 :, :] * down
    if fix_ref is not None:
        fix_ref[...] = stack_rows([up, down])
    size = rows // 2
    first = jnp.where(upper_chip(), rows - size, 0)
    far_up = jnp.where(first == 0, tail_ref[2:3, :], 0.0)
    far_down = jnp.where(first + size == rows, tail_ref[3:4, :], 0.0)
    for k in range(size // ROWS):
        at = pl.ds(pl.multiple_of(first + k * ROWS, ROWS), ROWS)
        c_out = c_out_ref[at, :]
        part = got_ref[rows + k * ROWS : rows + (k + 1) * ROWS, :] + c_out * u_o_ref[at, :]
        if k == 0:
            part = part + jnp.where(row_at(width, 0), far_up, 0.0)
        if k == size // ROWS - 1:
            part = part + jnp.where(row_at(width, ROWS - 1), far_down, 0.0)
        sums[1] = sums[1] + v_ref[at, :] * (c_out * (inv_far_ref[k * ROWS : (k + 1) * ROWS, :] * part))
    ends = up * v_ref[0:1, :] + down * v_ref[rows - 1 :, :]
    last = fold(sums[0] + 2.0 * sums[1] + jnp.where(row_at(width, 0), ends, 0.0)) + inner_ref[...]
    terms = (t0_ref[...], totals_ref[0:ROWS, :], totals_ref[ROWS : 2 * ROWS, :], last)
    lane = lax.broadcasted_iota(jnp.int32, (ROWS, 128), 1)
    row = jnp.zeros((ROWS, 128), F32)
    for n, t in enumerate(terms):
        t = t + pltpu.roll(t, 64, 1)
        t = t + pltpu.roll(t, 32, 1)
        row = jnp.where(lane // 32 == n, t, row)
    row = jnp.broadcast_to(jnp.sum(row, 0, keepdims=True), (ROWS, 128))
    for at in range(0, mail_ref.shape[0], ROWS):
        mail_ref[at : at + ROWS, :] = row


def weights(mail_ref):
    block = mail_ref[0:ROWS, :]
    for at in range(ROWS, mail_ref.shape[0], ROWS):
        block = block + mail_ref[at : at + ROWS, :]
    block = jnp.sum(block, 0, keepdims=True)
    g0, g1, g2, g3 = (jnp.sum(block[:, 32 * k : 32 * (k + 1)], 1, keepdims=True) for k in range(4))
    mu = g1 / g0
    h = g2 - mu * g1
    t = jnp.clip(h / (h - (g3 - 2.0 * mu * g2 + mu * mu * g1)), 0.5, 80.0)
    a = g0 / (g0 - g1 - h * t)
    b = t * a
    return a - mu * b, b


def hand_out(j, value, k, holds_outer, mine_ref, send_ref, first, half):
    band = jnp.where(upper_chip(), j % 2, 1 - j % 2)
    size = value.shape[0]
    if holds_outer == (j < 2):
        mine_ref[band, k * ROWS : k * ROWS + size, :] = value
    else:
        send_ref[pl.ds(pl.multiple_of(first + band * half + k * ROWS, ROWS), size), :] = value


def for_holder(body):
    outer = (core() == 1) != upper_chip()
    pl.when(outer)(lambda: body(True))
    pl.when(jnp.logical_not(outer))(lambda: body(False))


def step_kernel(
    mail_ref, s_o_ref, s_i_ref, v1_o_ref, v1_i_ref, v2_o_ref, v2_i_ref, part_i_ref, part_ref, far_ref, fix_ref, cap_ref, seen_ref,
    diag_o_ref, diag_i_ref, inv_o_ref, inv_i_ref, cx_ref, cy_ref, c_ref, c_out_ref,
    z_o_ref, z_i_ref, core_ref, cross_ref, total_ref, pay_ref, x_mine_ref, z_mine_ref, scratch_ref,
):
    rows, width = s_o_ref.shape
    chunks = rows // ROWS
    a, b = weights(mail_ref)

    def run(holds_outer):
        total = jnp.zeros((ROWS, width), F32)
        for j in range(4):
            for k in range(chunks):
                rs = slice(k * ROWS, (k + 1) * ROWS)
                s, p, q, diag, inv = (
                    band_of(o, i, j)[rs, :]
                    for o, i in (
                        (s_o_ref, s_i_ref), (v1_o_ref, v1_i_ref), (v2_o_ref, v2_i_ref),
                        (diag_o_ref, diag_i_ref), (inv_o_ref, inv_i_ref),
                    )
                )
                if j == 0:
                    part = part_ref[rs, :] + c_out_ref[rs, :] * far_ref[rs, :]
                    if k == 0:
                        part = part + jnp.where(row_at(width, 0), fix_ref[0:1, :], 0.0)
                    if k == chunks - 1:
                        part = part + jnp.where(row_at(width, ROWS - 1), fix_ref[1:2, :], 0.0)
                else:
                    part = part_i_ref[j - 1, rs, :]
                    if j == 1:
                        part = part + c_ref[1, rs, :] * v2_o_ref[rs, :]
                r = inv * part
                x = s + a * p + b * q
                residual = cap_ref[j, rs, :] * x + seen_ref[j, rs, :] - diag * (x - (p + a * q + b * r))
                z = residual * inv
                band_of(z_o_ref, z_i_ref, j)[rs, :] = z
                total = total + residual * z
                hand_out(j, x, k, holds_outer, x_mine_ref, core_ref, ROWS, rows)
                hand_out(j, z, k, holds_outer, z_mine_ref, core_ref, ROWS + 2 * rows, rows)
        total_ref[...] = fold(total)

    for_holder(run)
    put_two_rows(z_o_ref, z_i_ref, core_ref.at[0:ROWS], cross_ref)
    own_parts(z_o_ref, z_i_ref, cx_ref, cy_ref, c_ref, pay_ref, scratch_ref)


def give_kernel(q_o_ref, q_i_ref, mine_ref, send_ref):
    rows = q_o_ref.shape[0]

    def run(holds_outer):
        for j in range(4):
            hand_out(j, band_of(q_o_ref, q_i_ref, j)[...], 0, holds_outer, mine_ref, send_ref, 0, rows)

    for_holder(run)


def out_rows(out_ref, step, band, which):
    return out_ref.at[step, band, half_of(which, out_ref.shape[2] // 2), :]


def later_out_kernel(x_mine_ref, got_ref, out_ref, sems):
    half = x_mine_ref.shape[1]
    pairs = []
    for band in range(2):
        at = ROWS + band * half
        pairs.append((x_mine_ref.at[band], out_rows(out_ref, 1, band, core())))
        pairs.append((got_ref.at[at : at + half], out_rows(out_ref, 1, band, 1 - core())))
    for copy in start_copies(pairs, sems):
        copy.wait()


def last_kernel(_, mail_ref, x_mine_ref, z_mine_ref, got_ref, q_mine_ref, q_got_ref, out_ref, answer, sems):
    half = x_mine_ref.shape[1]
    a, b = weights(mail_ref)
    copies = []
    for band in range(2):
        at = ROWS + band * half
        got = got_ref.at[at : at + half], got_ref.at[at + 2 * half : at + 3 * half], q_got_ref.at[band * half : (band + 1) * half]
        mine = [ref.at[band] for ref in (x_mine_ref, z_mine_ref, q_mine_ref)]
        for which, (x_ref, z_ref, q_ref) in ((core(), mine), (1 - core(), got)):
            n = len(copies)
            answer[n] = x_ref[...] + a * z_ref[...] + b * q_ref[...]
            copies.append(pltpu.make_async_copy(answer.at[n], out_rows(out_ref, 0, band, which), sems.at[n]))
            copies[-1].start()
    for copy in copies:
        copy.wait()


def on_device(cond_x, cond_y, via_cond, via_mask, capacitance, pad_mask, observe):
    _, rows, width = cond_x.shape
    half = rows // 2
    field, three, four, edge = shape(half, width), shape(3, half, width), shape(4, half, width), shape(4, width)
    eight, twenty = shape(ROWS, width), shape(20, width)
    most, part_rows = shape(3 * half // 2, width), shape(half // 2, width)
    rim, pair = shape(2, width), shape(2, half, width)
    mail = shape(lax.axis_size("band") * lax.axis_size("tile"), 128)
    one, two = shape(ROWS, 128), shape(2 * ROWS, 128)
    fourteen = shape(14, half, width)
    whole, whole_int = pltpu.VMEM((2, rows, width), F32), pltpu.VMEM((2, rows, width), jnp.int32)
    own, send, pay, pay_send, last, middle = call(
        load_kernel, [fourteen, fourteen, shape(5 * half // 2, width), shape(5 * half // 2 + ROWS, width), rim, rim],
        cond_x, cond_y, via_cond, via_mask, capacitance, pad_mask, observe, name="load", place=pltpu.HBM,
        scratch=[whole, whole_int, whole_int, pltpu.VMEM((2, 2, ROWS, width), F32), pltpu.SemaphoreType.DMA((15,))],
    )
    more = core_swap(pay_send)
    more, send = lax.optimization_barrier((more, send))
    pay, pay_more, last = call(pay_kernel, [field, most, edge], pay, more, last, name="pay")
    link, traded, last = outer_swap(pay), core_swap(send), cross_swap(last)
    pay_more, last = lax.optimization_barrier((pay_more, last))
    far = outer_swap(pay_more)
    cx, cy, c, diag_i, inv_i, s_i, part, seen, cx_edge, cap, earlier = call(
        prepare_kernel, [four, four, four, three, three, three, field, field, edge, four, four],
        own, traded, middle, more, last, name="prepare",
        scratch=[pltpu.VMEM((4, half, width), F32), pltpu.VMEM((4, half, width), F32)],
    )
    c_out, diag_o, inv_o, s_o, near, cross, fix = call(
        outer_kernel, [field, field, field, field, twenty, twenty, shape(1, width)],
        part, seen, link, cx, cy, c, inv_i, s_i, name="outer",
    )
    fix, sides = outer_swap(fix), (core_swap(near), cross_swap(cross))

    coeffs = (cx, cy, c, inv_i, cx_edge)
    parts_of = [pltpu.VMEM((half, width), F32)]
    v1_i, part, sums = call(spread_kernel, [three, field, two], s_o, s_i, *sides, *coeffs, name="first_spread")
    v1_o, near, cross, t0, pay, inv_far = call(
        far_first_kernel, [field, eight, eight, one, most, part_rows],
        s_o, part, link, far, fix, c_out, inv_o, v1_i, sums, cx, cy, c, name="first_far", scratch=parts_of,
    )

    def stage(u_o, u_i, pay, near, cross, t0, name, x_mine=None):
        further = x_mine is None
        got, cross, near = outer_swap(pay), cross_swap(cross), core_swap(near)
        v_i, part, sums, tail, there, inner, *w_i = call(
            two_spread_kernel, [three, field, two, edge, eight, one] + [three] * further,
            u_o, u_i, near, cross, *coeffs, *sides, name=name + "_spread",
        )
        if not further:
            (out,) = call(
                later_out_kernel, [shape(2, 2, rows, width)], x_mine, near, name="later_out", out_place=pl.ANY,
                scratch=[pltpu.SemaphoreType.DMA((4,))],
            )
            part, out = lax.optimization_barrier((part, out))
        v_o, totals = call(far_kernel, [field, two], u_o, got, part, sums, c_out, inv_o, name=name + "_far")
        if further:
            more = (outer_swap(v_o),)
        else:
            mine, send = call(give_kernel, [pair, shape(2 * half, width)], v_o, v_i, name="give")
            more = out, near, mine, core_swap(send)
        parts, *rest = call(
            finish_kernel, [mail] + [field, rim] * further,
            u_o, v_o, got, outer_swap(tail), v_i, totals, there, inner, inv_far,
            cx, cy, c, c_out, cx_edge, *sides, t0, name=name + "_finish",
        )
        more = *w_i, *rest, *more
        return v_o, v_i, all_total(parts), more

    v2_o, v2_i, total, (part_i, part, fix, far) = stage(v1_o, v1_i, pay, near, cross, t0, "later")
    z_o, z_i, near, cross, t0, pay, x_mine, z_mine = call(
        step_kernel,
        [field, three, shape(ROWS + 4 * half, width), eight, one, most, pair, pair],
        total, s_o, s_i, v1_o, v1_i, v2_o, v2_i, part_i, part, far, fix, cap, earlier, diag_o, diag_i, inv_o, inv_i, cx, cy, c, c_out,
        name="step", scratch=parts_of,
    )
    _, _, total, (out, got, q_mine, q_got) = stage(z_o, z_i, pay, near, cross, t0, "earlier", x_mine)
    (out,) = call(
        last_kernel, [shape(2, 2, rows, width)], out, total, x_mine, z_mine, got, q_mine, q_got, name="last",
        out_place=pl.ANY, scratch=[pltpu.VMEM((4, half, width), F32), pltpu.SemaphoreType.DMA((4,))], reuse=True,
    )
    return out


def solution(mesh):
    placed = (P("band", "tile", None),) * 6 + (P(None, "band", "tile", None),)
    return jax.shard_map(
        on_device,
        mesh=mesh,
        in_specs=placed,
        out_specs=P(None, "band", "tile", None),
        check_vma=False,
    )
```

```python
import jax
import jax.numpy as jnp
from jax import lax
from jax.experimental import pallas as pl
from jax.experimental.pallas import tpu as pltpu
from jax.sharding import PartitionSpec as P

NB = 8
ROWS = 8
AXES = ("band", "tile")
F32 = jnp.float32

pad_conductance = 4.0

COSTS = {"prepare": 0, "first_spread": 0, "later_spread": 0, "earlier_spread": 0, "later_out": 0}


def sizes():
    return lax.axis_size("band"), lax.axis_size("tile")


def core():
    return lax.rem(lax.axis_index("band"), 2)


def upper_chip():
    return lax.axis_index("band") >= 2


def core_swap(x):
    nb, _ = sizes()
    return lax.ppermute(x, "band", [(b, b ^ 1) for b in range(nb)])


def outer_swap(x):
    nb, _ = sizes()
    return lax.ppermute(x, "band", [(b, b ^ 2) for b in range(nb)])


def cross_swap(x):
    nb, nt = sizes()
    pairs = []
    for b in range(nb):
        for t in range(nt):
            other = (t + 1) % nt if b % 2 else (t - 1) % nt
            pairs.append((b * nt + t, (b ^ 1) * nt + other))
    return lax.ppermute(x, AXES, pairs)


def all_total(parts):
    return lax.all_to_all(parts, AXES, 0, 0, tiled=True)


def call(body, outs, *args, name, place=pltpu.VMEM, out_place=pltpu.VMEM, scratch=(), limit=10, reuse=False):
    cost = COSTS.get(name, 10)
    if place == pltpu.HBM:
        args = [pltpu.with_memory_space_constraint(a, pltpu.HBM) for a in args]
    return pl.pallas_call(
        body,
        out_shape=outs,
        in_specs=[pl.BlockSpec(memory_space=pl.ANY if reuse and n == 0 else place) for n in range(len(args))],
        input_output_aliases={0: 0} if reuse else {},
        out_specs=[pl.BlockSpec(memory_space=out_place)] * len(outs),
        scratch_shapes=list(scratch),
        name=name,
        cost_estimate=pl.CostEstimate(flops=cost * 10**9, bytes_accessed=cost * 10**6, transcendentals=0),
        compiler_params=pltpu.CompilerParams(vmem_limit_bytes=limit * 1024 * 1024),
    )(*args)


def shape(*dims):
    return jax.ShapeDtypeStruct(dims, F32)


def row_at(width, at):
    return lax.broadcasted_iota(jnp.int32, (ROWS, width), 0) == at


def stack_rows(rows):
    return jnp.concatenate(rows, 0)


def put_rows(first, last, core_ref, cross_ref):
    lower = core() == 1
    core_ref[...] = jnp.where(lower, first, last)
    cross_ref[...] = jnp.where(lower, last, first)


def put_two_rows(u_o_ref, u_i_ref, core_ref, cross_ref):
    rows = u_o_ref.shape[0]
    ends = [
        stack_rows([band_of(u_o_ref, u_i_ref, j)[r : r + 1, :] for r in pair for j in range(4)])
        for pair in ((0, 1), (rows - 1, rows - 2))
    ]
    put_rows(ends[0], ends[1], core_ref, cross_ref)


def take_rows(core_ref, cross_ref):
    lower = core() == 1
    tile = lax.axis_index("tile")
    cross = cross_ref[...]
    near = core_ref[0 : cross.shape[0], :]
    above = jnp.where(lower, near, jnp.where(tile == 0, 0.0, cross))
    below = jnp.where(lower, jnp.where(tile == lax.axis_size("tile") - 1, 0.0, cross), near)
    return above, below


def fold(total):
    acc = total[:, :128]
    for at in range(128, total.shape[1], 128):
        acc = acc + total[:, at : at + 128]
    return acc


def band_of(u_o_ref, u_i_ref, j):
    return u_o_ref if j == 0 else u_i_ref.at[j - 1]


def in_band(v_ref, cx_ref, cy_ref, carried, below, k, chunks):
    width = v_ref.shape[-1]
    r = k * ROWS
    x = v_ref[r : r + ROWS, :]
    cx = cx_ref[r : r + ROWS, :]
    cy = cy_ref[r : r + ROWS, :]
    after = below if k == chunks - 1 else v_ref[r + ROWS : r + ROWS + 1, :]
    down = jnp.where(row_at(width, ROWS - 1), after, pltpu.roll(x, ROWS - 1, 0))
    flux = cx * x
    up = jnp.where(row_at(width, 0), carried, pltpu.roll(flux, 1, 0))
    total = cx * down + up + cy * pltpu.roll(x, width - 1, 1) + pltpu.roll(cy * x, 1, 1)
    return x, total, flux[ROWS - 1 :, :]


def couple(xs, parts, c_ref, rs):
    parts = list(parts)
    for j in range(1, len(xs)):
        c = c_ref[j, rs, :]
        parts[j] = parts[j] + c * xs[j - 1]
        parts[j - 1] = parts[j - 1] + c * xs[j]
    return parts


def half_of(which, half):
    return pl.ds(pl.multiple_of(which * half, ROWS), half)


def start_copies(pairs, sems):
    copies = [pltpu.make_async_copy(source, to, sems.at[n]) for n, (source, to) in enumerate(pairs)]
    for copy in copies:
        copy.start()
    return copies


def load_kernel(
    cond_x_ref, cond_y_ref, via_ref, mask_ref, cap_ref, pad_ref, observe_ref,
    mine_ref, send_ref, pay_mine_ref, pay_send_ref, last_ref, middle_ref,
    via_at, mask_at, pad_at, edge_at, sems,
):
    half, width = send_ref.shape[1:]
    me = core()
    upper = upper_chip()
    halves = ((send_ref, pay_send_ref, 1 - me), (mine_ref, pay_mine_ref, me))
    pairs = [(via_ref, via_at), (mask_ref, mask_at), (pad_ref, pad_at)]
    pairs.append((cond_x_ref.at[:, pl.ds(half - ROWS, ROWS), :], edge_at.at[0]))
    pairs.append((cond_x_ref.at[:, pl.ds(2 * half - ROWS, ROWS), :], edge_at.at[1]))
    for ref, _, which in halves:
        rs = half_of(which, half)
        pairs += [
            (cond_x_ref.at[:, rs, :], ref.at[0:2]),
            (cond_y_ref.at[:, rs, :], ref.at[2:4]),
            (observe_ref.at[1, :, rs, :], ref.at[8:10]),
            (cap_ref.at[:, rs, :], ref.at[10:12]),
        ]
    for ref, _, which in halves:
        pairs.append((observe_ref.at[0, :, half_of(which, half), :], ref.at[12:14]))
    copies = start_copies(pairs, sems)
    for copy in copies[:5]:
        copy.wait()
    for band in range(2):
        middle_ref[band : band + 1, :] = edge_at[0, band, ROWS - 1 :, :]
        last_ref[band : band + 1, :] = edge_at[1, band, ROWS - 1 :, :]
    lane = lax.broadcasted_iota(jnp.int32, (ROWS, width), 1)
    facing = jnp.where(upper, 0, 1)
    for n, (ref, pay_ref, which) in enumerate(halves):
        for copy in copies[5 + 4 * n : 9 + 4 * n]:
            copy.wait()
        rs = half_of(which, half)
        for band in range(2):
            ref[4 + band] = via_at[band, rs, :] * mask_at[band, rs, :].astype(F32)
            ref[6 + band] = ref[10 + band] + pad_conductance * pad_at[band, rs, :].astype(F32)
        carried = jnp.where(which == 0, 0.0, edge_at[0, facing, ROWS - 1 :, :])
        for k in range(half // ROWS):
            rs = slice(k * ROWS, (k + 1) * ROWS)
            cx, cy, seen, via = ref[facing, rs, :], ref[2 + facing, rs, :], ref[8 + facing, rs, :], ref[5, rs, :]
            up = jnp.where(row_at(width, 0), carried, pltpu.roll(cx, 1, 0))
            carried = cx[ROWS - 1 :, :]
            left = jnp.where(lane == 0, 0.0, pltpu.roll(cy, 1, 1))
            diag = ref[6 + facing, rs, :] + cx + cy + up + left + ref[4, rs, :]
            inv = 1.0 / (diag + via)
            pay_ref[rs, :] = jnp.where(upper, diag, via)
            pay_ref[half + k * ROWS : half + (k + 1) * ROWS, :] = jnp.where(upper, seen, seen * inv)
            if 2 * k * ROWS >= half:
                at = 3 * half // 2 + k * ROWS
                pay_ref[at : at + ROWS, :] = inv
    pay_send_ref[5 * half // 2 :, :] = stack_rows([middle_ref[...], last_ref[...], jnp.zeros((ROWS - 4, width), F32)])
    for copy in copies[-2:]:
        copy.wait()


def theirs():
    return (core() == 1) == upper_chip()


def pay_kernel(mine_ref, got_ref, last_ref, pay_ref, more_ref, all_last_ref):
    half = pay_ref.shape[0]
    end = 5 * half // 2
    pay_ref[...] = jnp.where(theirs(), got_ref[0:half, :], mine_ref[0:half, :])
    more_ref[...] = jnp.where(theirs(), got_ref[half:end, :], mine_ref[half:, :])
    own, other = last_ref[...], got_ref[end + 2 : end + 4, :]
    all_last_ref[...] = stack_rows([jnp.where(core() == 0, own, other), jnp.where(core() == 0, other, own)])


def place_of(owner, band):
    n = 2 * owner + band
    return jnp.where(upper_chip(), n, 3 - n)


def prepare_kernel(
    mine_ref, got_ref, middle_ref, more_ref, last_ref,
    cx_ref, cy_ref, c_ref, diag_ref, inv_ref, s_ref, part_ref, seen_o_ref, edge_ref, cap_ref, seen_ref, all_part, all_seen,
):
    half, width = part_ref.shape
    me = core()
    upper = upper_chip()
    lane = lax.broadcasted_iota(jnp.int32, (ROWS, width), 1)
    first_tile = jnp.logical_and(me == 0, lax.axis_index("tile") == 0)
    own_edge = jnp.where(me == 1, middle_ref[...], last_ref[0:2, :])
    got_edge = jnp.where(me == 1, more_ref[5 * half // 2 : 5 * half // 2 + 2, :], last_ref[2:4, :])
    c_ref[0] = jnp.zeros((half, width), F32)
    for owner, ref, edges in ((me, mine_ref, own_edge), (1 - me, got_ref, got_edge)):
        for band in range(2):
            j = place_of(owner, band)
            carried = jnp.where(first_tile, 0.0, edges[band : band + 1, :])
            edge_ref[pl.ds(j, 1), :] = carried
            cx_ref[j] = ref[band]
            cap_ref[j] = ref[10 + band]
            seen_ref[j] = ref[12 + band]
            all_seen[j] = ref[8 + band]
            via_at = jnp.where(upper, j + 1, j)

            @pl.when(via_at < 4)
            def _():
                c_ref[via_at] = ref[4 + band]

            for k in range(half // ROWS):
                rs = slice(k * ROWS, (k + 1) * ROWS)
                cx, cy, diag = (ref[2 * n + band, rs, :] for n in (0, 1, 3))
                cut = jnp.where(lane == width - 1, 0.0, cy)
                up = jnp.where(row_at(width, 0), carried, pltpu.roll(cx, 1, 0))
                carried = cx[ROWS - 1 :, :]
                cy_ref[j, rs, :] = cut
                all_part[j, rs, :] = diag + cx + cy + up + pltpu.roll(cut, 1, 1)
    part_ref[...] = all_part[0] + c_ref[1]
    seen_o_ref[...] = all_seen[0]
    for j in range(1, 4):
        for k in range(half // ROWS):
            rs = slice(k * ROWS, (k + 1) * ROWS)
            diag = all_part[j, rs, :] + c_ref[j, rs, :]
            if j < 3:
                diag = diag + c_ref[j + 1, rs, :]
            inv = 1.0 / diag
            diag_ref[j - 1, rs, :] = diag
            inv_ref[j - 1, rs, :] = inv
            s_ref[j - 1, rs, :] = all_seen[j, rs, :] * inv


def outer_kernel(
    part_ref, seen_ref, link_ref, cx_ref, cy_ref, c_ref, inv_i_ref, s_i_ref,
    c_out_ref, diag_ref, inv_ref, s_ref, core_ref, cross_ref, fix_ref,
):
    rows, width = part_ref.shape
    upper = upper_chip()
    for k in range(rows // ROWS):
        rs = slice(k * ROWS, (k + 1) * ROWS)
        c_out = jnp.where(upper, link_ref[rs, :], c_ref[0, rs, :])
        diag = part_ref[rs, :] + c_out
        inv = 1.0 / diag
        c_out_ref[rs, :] = c_out
        diag_ref[rs, :] = diag
        inv_ref[rs, :] = inv
        s_ref[rs, :] = seen_ref[rs, :] * inv
    ends = []
    for r, beyond in ((0, 0), (rows - 1, rows - 2)):
        at = slice(r, r + 1)
        lines = [band_of(s_ref, s_i_ref, j)[at, :] for j in range(4)]
        lines += [band_of(inv_ref, inv_i_ref, j)[at, :] for j in range(4)]
        lines += [cy_ref[j, at, :] for j in range(4)]
        lines += [c_out_ref[at, :]] + [c_ref[j, at, :] for j in range(1, 4)]
        lines += [cx_ref[j, beyond : beyond + 1, :] for j in range(4)]
        ends.append(stack_rows(lines))
    put_rows(ends[0], ends[1], core_ref, cross_ref)
    fix_ref[...] = jnp.where(upper, diag_ref[0:1, :], s_ref[0:1, :])


def own_parts(u_o_ref, u_i_ref, cx_ref, cy_ref, c_ref, pay_ref, scratch_ref):
    rows, width = u_o_ref.shape
    chunks = rows // ROWS
    none = jnp.zeros((1, width), F32)
    carried = none
    for k in range(chunks):
        rs = slice(k * ROWS, (k + 1) * ROWS)
        x, part, carried = in_band(u_o_ref, cx_ref.at[0], cy_ref.at[0], carried, none, k, chunks)
        pay_ref[rs, :] = x
        scratch_ref[rs, :] = part + c_ref[1, rs, :] * u_i_ref[0, rs, :]
    size = rows // 2
    first = jnp.where(upper_chip(), 0, rows - size)
    pay_ref[rows : rows + size, :] = scratch_ref[pl.ds(pl.multiple_of(first, ROWS), size), :]


def spread_kernel(
    u_o_ref, u_i_ref, core_ref, cross_ref, cx_ref, cy_ref, c_ref, inv_i_ref, edge_ref, v_i_ref, part_ref, sums_ref
):
    above, below = take_rows(core_ref, cross_ref)
    spread_rows(u_o_ref, u_i_ref, above, below, cx_ref, cy_ref, c_ref, inv_i_ref, edge_ref, v_i_ref, part_ref, sums_ref)


def spread_rows(
    u_o_ref, u_i_ref, above, below, cx_ref, cy_ref, c_ref, inv_i_ref, edge_ref, v_i_ref, part_ref, sums_ref, diag_i_ref=None
):
    rows, width = u_o_ref.shape
    chunks = rows // ROWS
    carried = [edge_ref[j : j + 1, :] * above[j : j + 1] for j in range(4)]
    sums = [jnp.zeros((ROWS, width), F32) for _ in range(2)]
    for k in range(chunks):
        rs = slice(k * ROWS, (k + 1) * ROWS)
        xs, parts = [], []
        for j in range(4):
            x, part, carried[j] = in_band(
                band_of(u_o_ref, u_i_ref, j), cx_ref.at[j], cy_ref.at[j], carried[j], below[j : j + 1], k, chunks
            )
            xs.append(x)
            parts.append(part)
        parts = couple(xs, parts, c_ref, rs)
        part_ref[rs, :] = parts[0]
        for j in range(1, 4):
            v = inv_i_ref[j - 1, rs, :] * parts[j]
            weighted = parts[j]
            if diag_i_ref is not None:
                v = xs[j] - v
                weighted = diag_i_ref[j - 1, rs, :] * xs[j] - weighted
            v_i_ref[j - 1, rs, :] = v
            sums[0] = sums[0] + xs[j] * weighted
            sums[1] = sums[1] + v * weighted
    sums_ref[0:ROWS, :] = fold(sums[0])
    sums_ref[ROWS : 2 * ROWS, :] = fold(sums[1])


def beside(u_o_ref, u_i_ref, above, below, side_above, side_below, edge_ref, cx_ref):
    rows, width = u_o_ref.shape
    here = stack_rows([above[0:4], below[0:4]])
    beyond = stack_rows([above[4:8], below[4:8]])
    inside = [band_of(u_o_ref, u_i_ref, j)[r : r + 1, :] for r in (0, rows - 1) for j in range(4)]
    toward = stack_rows([edge_ref[...]] + [cx_ref[j, rows - 1 :, :] for j in range(4)])
    inv, cy, c, away = (stack_rows([side_above[n : n + 4], side_below[n : n + 4]]) for n in (4, 8, 12, 16))
    c = jnp.where(jnp.logical_or(row_at(width, 0), row_at(width, 4)), 0.0, c)
    total = toward * stack_rows(inside) + away * beyond
    total = total + cy * pltpu.roll(here, width - 1, 1) + pltpu.roll(cy * here, 1, 1)
    return total + c * pltpu.roll(here, 1, 0) + pltpu.roll(c * here, ROWS - 1, 0), inv


def two_spread_kernel(
    u_o_ref, u_i_ref, core_ref, cross_ref, cx_ref, cy_ref, c_ref, inv_i_ref, edge_ref, side_core_ref, side_cross_ref,
    diag_i_ref, d_i_ref, part_ref, sums_ref, tail_ref, beside_ref, total_ref, w_ref=None,
):
    rows, width = u_o_ref.shape
    chunks = rows // ROWS
    above, below = take_rows(core_ref, cross_ref)
    spread_rows(u_o_ref, u_i_ref, above, below, cx_ref, cy_ref, c_ref, inv_i_ref, edge_ref, d_i_ref, part_ref, sums_ref, diag_i_ref)
    fluxes = [edge_ref[0:1, :] * above[0:1], cx_ref[0, rows - 1 :, :] * below[0:1]]
    tail_ref[...] = stack_rows([above[0:1], below[0:1], *fluxes])
    side_above, side_below = take_rows(side_core_ref, side_cross_ref)
    parts_there, inv = beside(u_o_ref, u_i_ref, above, below, side_above, side_below, edge_ref, cx_ref)
    beside_ref[...] = parts_there
    there = stack_rows([above[0:4], below[0:4]]) - inv * parts_there
    carried = [edge_ref[j : j + 1, :] * there[j : j + 1] for j in range(1, 4)]
    total = jnp.zeros((ROWS, width), F32)
    for k in range(chunks):
        rs = slice(k * ROWS, (k + 1) * ROWS)
        xs, parts = [], []
        for j in range(1, 4):
            x, part, carried[j - 1] = in_band(
                d_i_ref.at[j - 1], cx_ref.at[j], cy_ref.at[j], carried[j - 1], there[4 + j : 5 + j], k, chunks
            )
            xs.append(x)
            parts.append(part)
        parts = couple(xs, parts, c_ref.at[pl.ds(1, 3)], rs)
        for j in range(3):
            total = total + xs[j] * parts[j]
            if w_ref is not None:
                w_ref[j, rs, :] = parts[j]
    total_ref[...] = fold(total)


def far_first_kernel(
    u_o_ref, part_ref, got_ref, more_ref, fix_ref, c_out_ref, inv_ref, v_i_ref, sums_ref, cx_ref, cy_ref, c_ref,
    v_ref, core_ref, cross_ref, total_ref, pay_ref, inv_far_ref, scratch_ref,
):
    rows, width = u_o_ref.shape
    upper = upper_chip()
    total = jnp.zeros((ROWS, width), F32)
    for k in range(rows // ROWS):
        rs = slice(k * ROWS, (k + 1) * ROWS)
        c_out = c_out_ref[rs, :]
        diag, far = got_ref[rs, :] + c_out, more_ref[rs, :]
        if k == 0:
            first = jnp.broadcast_to(fix_ref[0:1, :], far.shape)
            diag = jnp.where(row_at(width, 0), first, diag)
            far = jnp.where(jnp.logical_and(upper, row_at(width, 0)), first, far)
        inv_far = 1.0 / jnp.where(upper, 1.0, diag)
        if k * ROWS < rows // 2:
            inv_far_ref[rs, :] = jnp.where(upper, more_ref[rows + k * ROWS : rows + (k + 1) * ROWS, :], inv_far)
        far = jnp.where(upper, far, far * inv_far)
        part = part_ref[rs, :] + c_out * far
        v = inv_ref[rs, :] * part
        v_ref[rs, :] = v
        total = total + v * part
    total_ref[...] = fold(total) + sums_ref[ROWS : 2 * ROWS, :]
    put_two_rows(v_ref, v_i_ref, core_ref, cross_ref)
    own_parts(v_ref, v_i_ref, cx_ref, cy_ref, c_ref, pay_ref, scratch_ref)


def far_kernel(u_o_ref, got_ref, part_ref, sums_ref, c_out_ref, inv_ref, diag_ref, d_ref, totals_ref):
    rows, width = u_o_ref.shape
    sums = [jnp.zeros((ROWS, width), F32) for _ in range(2)]
    for k in range(rows // ROWS):
        rs = slice(k * ROWS, (k + 1) * ROWS)
        u = u_o_ref[rs, :]
        part = part_ref[rs, :] + c_out_ref[rs, :] * got_ref[rs, :]
        d = u - inv_ref[rs, :] * part
        weighted = diag_ref[rs, :] * u - part
        d_ref[rs, :] = d
        sums[0] = sums[0] + u * weighted
        sums[1] = sums[1] + d * weighted
    totals_ref[0:ROWS, :] = fold(sums[0]) + sums_ref[0:ROWS, :]
    totals_ref[ROWS : 2 * ROWS, :] = fold(sums[1]) + sums_ref[ROWS : 2 * ROWS, :]


def finish_kernel(
    u_o_ref, d_ref, got_ref, tail_ref, own_tail_ref, d_i_ref, totals_ref, beside_ref, inner_ref, inv_far_ref,
    cx_ref, cy_ref, c_ref, c_out_ref, edge_ref, side_core_ref, side_cross_ref, t0_ref,
    mail_ref, w_ref=None, fix_ref=None,
):
    rows, width = u_o_ref.shape
    chunks = rows // ROWS
    none = jnp.zeros((1, width), F32)
    sums = [jnp.zeros((ROWS, width), F32) for _ in range(2)]
    carried = none
    for k in range(chunks):
        rs = slice(k * ROWS, (k + 1) * ROWS)
        d, part, carried = in_band(d_ref, cx_ref.at[0], cy_ref.at[0], carried, none, k, chunks)
        coupled = c_ref[1, rs, :] * d_i_ref[0, rs, :]
        sums[0] = sums[0] + d * (part + 2.0 * coupled)
        if w_ref is not None:
            w_ref[rs, :] = part + coupled
    side_above, side_below = take_rows(side_core_ref, side_cross_ref)
    up = side_above[4:5] * (beside_ref[0:1, :] + side_above[12:13] * tail_ref[0:1, :])
    down = side_below[4:5] * (beside_ref[4:5, :] + side_below[12:13] * tail_ref[1:2, :])
    up = edge_ref[0:1, :] * (own_tail_ref[0:1, :] - up)
    down = cx_ref[0, rows - 1 :, :] * (own_tail_ref[1:2, :] - down)
    if fix_ref is not None:
        fix_ref[...] = stack_rows([up, down])
    size = rows // 2
    first = jnp.where(upper_chip(), rows - size, 0)
    far_up = jnp.where(first == 0, tail_ref[2:3, :], 0.0)
    far_down = jnp.where(first + size == rows, tail_ref[3:4, :], 0.0)
    for k in range(size // ROWS):
        at = pl.ds(pl.multiple_of(first + k * ROWS, ROWS), ROWS)
        c_out = c_out_ref[at, :]
        part = got_ref[rows + k * ROWS : rows + (k + 1) * ROWS, :] + c_out * u_o_ref[at, :]
        if k == 0:
            part = part + jnp.where(row_at(width, 0), far_up, 0.0)
        if k == size // ROWS - 1:
            part = part + jnp.where(row_at(width, ROWS - 1), far_down, 0.0)
        far = got_ref[at, :] - inv_far_ref[k * ROWS : (k + 1) * ROWS, :] * part
        sums[1] = sums[1] + d_ref[at, :] * (c_out * far)
    ends = up * d_ref[0:1, :] + down * d_ref[rows - 1 :, :]
    last = fold(sums[0] + 2.0 * sums[1] + jnp.where(row_at(width, 0), ends, 0.0)) + inner_ref[...]
    terms = (t0_ref[...], totals_ref[0:ROWS, :], totals_ref[ROWS : 2 * ROWS, :], last)
    lane = lax.broadcasted_iota(jnp.int32, (ROWS, 128), 1)
    row = jnp.zeros((ROWS, 128), F32)
    for n, t in enumerate(terms):
        t = t + pltpu.roll(t, 64, 1)
        t = t + pltpu.roll(t, 32, 1)
        row = jnp.where(lane // 32 == n, t, row)
    row = jnp.broadcast_to(jnp.sum(row, 0, keepdims=True), (ROWS, 128))
    for at in range(0, mail_ref.shape[0], ROWS):
        mail_ref[at : at + ROWS, :] = row


def weights(mail_ref):
    block = mail_ref[0:ROWS, :]
    for at in range(ROWS, mail_ref.shape[0], ROWS):
        block = block + mail_ref[at : at + ROWS, :]
    block = jnp.sum(block, 0, keepdims=True)
    k0, k1, k2, spread = (jnp.sum(block[:, 32 * k : 32 * (k + 1)], 1, keepdims=True) for k in range(4))
    k3 = k2 - spread
    nu = k1 / k0
    h = k2 - nu * k1
    t = jnp.clip(h / (k3 - 2.0 * nu * k2 + nu * nu * k1), 0.5, 80.0)
    a = k0 / (k1 - h * t)
    return a * (1.0 + t * nu), -t * a


def hand_out(j, value, k, holds_outer, mine_ref, send_ref, first, half):
    band = jnp.where(upper_chip(), j % 2, 1 - j % 2)
    size = value.shape[0]
    if holds_outer == (j < 2):
        mine_ref[band, k * ROWS : k * ROWS + size, :] = value
    else:
        send_ref[pl.ds(pl.multiple_of(first + band * half + k * ROWS, ROWS), size), :] = value


def for_holder(body):
    outer = (core() == 1) != upper_chip()
    pl.when(outer)(lambda: body(True))
    pl.when(jnp.logical_not(outer))(lambda: body(False))


def step_kernel(
    mail_ref, s_o_ref, s_i_ref, v1_o_ref, v1_i_ref, d_o_ref, d_i_ref, part_i_ref, part_ref, far_ref, fix_ref, cap_ref, seen_ref,
    diag_o_ref, diag_i_ref, inv_o_ref, inv_i_ref, cx_ref, cy_ref, c_ref, c_out_ref,
    z_o_ref, z_i_ref, core_ref, cross_ref, total_ref, pay_ref, x_mine_ref, z_mine_ref, scratch_ref,
):
    rows, width = s_o_ref.shape
    chunks = rows // ROWS
    a, b = weights(mail_ref)

    def run(holds_outer):
        total = jnp.zeros((ROWS, width), F32)
        for j in range(4):
            for k in range(chunks):
                rs = slice(k * ROWS, (k + 1) * ROWS)
                s, p, d, diag, inv = (
                    band_of(o, i, j)[rs, :]
                    for o, i in (
                        (s_o_ref, s_i_ref), (v1_o_ref, v1_i_ref), (d_o_ref, d_i_ref),
                        (diag_o_ref, diag_i_ref), (inv_o_ref, inv_i_ref),
                    )
                )
                if j == 0:
                    part = part_ref[rs, :] + c_out_ref[rs, :] * far_ref[rs, :]
                    if k == 0:
                        part = part + jnp.where(row_at(width, 0), fix_ref[0:1, :], 0.0)
                    if k == chunks - 1:
                        part = part + jnp.where(row_at(width, ROWS - 1), fix_ref[1:2, :], 0.0)
                else:
                    part = part_i_ref[j - 1, rs, :]
                    if j == 1:
                        part = part + c_ref[1, rs, :] * d_o_ref[rs, :]
                r = inv * part
                x = s + a * p + b * d
                residual = cap_ref[j, rs, :] * x + seen_ref[j, rs, :] - diag * (x - (p + a * (p - d) + b * r))
                z = residual * inv
                band_of(z_o_ref, z_i_ref, j)[rs, :] = z
                total = total + residual * z
                hand_out(j, x, k, holds_outer, x_mine_ref, core_ref, ROWS, rows)
                hand_out(j, z, k, holds_outer, z_mine_ref, core_ref, ROWS + 2 * rows, rows)
        total_ref[...] = fold(total)

    for_holder(run)
    put_two_rows(z_o_ref, z_i_ref, core_ref.at[0:ROWS], cross_ref)
    own_parts(z_o_ref, z_i_ref, cx_ref, cy_ref, c_ref, pay_ref, scratch_ref)


def give_kernel(q_o_ref, q_i_ref, mine_ref, send_ref):
    rows = q_o_ref.shape[0]

    def run(holds_outer):
        for j in range(4):
            hand_out(j, band_of(q_o_ref, q_i_ref, j)[...], 0, holds_outer, mine_ref, send_ref, 0, rows)

    for_holder(run)


def out_rows(out_ref, step, band, which):
    return out_ref.at[step, band, half_of(which, out_ref.shape[2] // 2), :]


def later_out_kernel(x_mine_ref, got_ref, out_ref, sems):
    half = x_mine_ref.shape[1]
    pairs = []
    for band in range(2):
        at = ROWS + band * half
        pairs.append((x_mine_ref.at[band], out_rows(out_ref, 1, band, core())))
        pairs.append((got_ref.at[at : at + half], out_rows(out_ref, 1, band, 1 - core())))
    for copy in start_copies(pairs, sems):
        copy.wait()


def last_kernel(_, mail_ref, x_mine_ref, z_mine_ref, got_ref, q_mine_ref, q_got_ref, out_ref, answer, sems):
    half = x_mine_ref.shape[1]
    a, b = weights(mail_ref)
    copies = []
    for band in range(2):
        at = ROWS + band * half
        got = got_ref.at[at : at + half], got_ref.at[at + 2 * half : at + 3 * half], q_got_ref.at[band * half : (band + 1) * half]
        mine = [ref.at[band] for ref in (x_mine_ref, z_mine_ref, q_mine_ref)]
        for which, (x_ref, z_ref, q_ref) in ((core(), mine), (1 - core(), got)):
            n = len(copies)
            answer[n] = x_ref[...] + a * z_ref[...] + b * q_ref[...]
            copies.append(pltpu.make_async_copy(answer.at[n], out_rows(out_ref, 0, band, which), sems.at[n]))
            copies[-1].start()
    for copy in copies:
        copy.wait()


def on_device(cond_x, cond_y, via_cond, via_mask, capacitance, pad_mask, observe):
    _, rows, width = cond_x.shape
    half = rows // 2
    field, three, four, edge = shape(half, width), shape(3, half, width), shape(4, half, width), shape(4, width)
    eight, twenty = shape(ROWS, width), shape(20, width)
    most, part_rows = shape(3 * half // 2, width), shape(half // 2, width)
    rim, pair = shape(2, width), shape(2, half, width)
    mail = shape(lax.axis_size("band") * lax.axis_size("tile"), 128)
    one, two = shape(ROWS, 128), shape(2 * ROWS, 128)
    fourteen = shape(14, half, width)
    whole, whole_int = pltpu.VMEM((2, rows, width), F32), pltpu.VMEM((2, rows, width), jnp.int32)
    own, send, pay, pay_send, last, middle = call(
        load_kernel, [fourteen, fourteen, shape(5 * half // 2, width), shape(5 * half // 2 + ROWS, width), rim, rim],
        cond_x, cond_y, via_cond, via_mask, capacitance, pad_mask, observe, name="load", place=pltpu.HBM,
        scratch=[whole, whole_int, whole_int, pltpu.VMEM((2, 2, ROWS, width), F32), pltpu.SemaphoreType.DMA((15,))],
    )
    more = core_swap(pay_send)
    more, send = lax.optimization_barrier((more, send))
    pay, pay_more, last = call(pay_kernel, [field, most, edge], pay, more, last, name="pay")
    link, traded, last = outer_swap(pay), core_swap(send), cross_swap(last)
    pay_more, last = lax.optimization_barrier((pay_more, last))
    far = outer_swap(pay_more)
    cx, cy, c, diag_i, inv_i, s_i, part, seen, cx_edge, cap, earlier = call(
        prepare_kernel, [four, four, four, three, three, three, field, field, edge, four, four],
        own, traded, middle, more, last, name="prepare",
        scratch=[pltpu.VMEM((4, half, width), F32), pltpu.VMEM((4, half, width), F32)],
    )
    c_out, diag_o, inv_o, s_o, near, cross, fix = call(
        outer_kernel, [field, field, field, field, twenty, twenty, shape(1, width)],
        part, seen, link, cx, cy, c, inv_i, s_i, name="outer",
    )
    fix, sides = outer_swap(fix), (core_swap(near), cross_swap(cross))

    coeffs = (cx, cy, c, inv_i, cx_edge)
    parts_of = [pltpu.VMEM((half, width), F32)]
    v1_i, part, sums = call(spread_kernel, [three, field, two], s_o, s_i, *sides, *coeffs, name="first_spread")
    v1_o, near, cross, t0, pay, inv_far = call(
        far_first_kernel, [field, eight, eight, one, most, part_rows],
        s_o, part, link, far, fix, c_out, inv_o, v1_i, sums, cx, cy, c, name="first_far", scratch=parts_of,
    )

    def stage(u_o, u_i, pay, near, cross, t0, name, x_mine=None):
        further = x_mine is None
        got, cross, near = outer_swap(pay), cross_swap(cross), core_swap(near)
        d_i, part, sums, tail, there, inner, *w_i = call(
            two_spread_kernel, [three, field, two, edge, eight, one] + [three] * further,
            u_o, u_i, near, cross, *coeffs, *sides, diag_i, name=name + "_spread",
        )
        if not further:
            (out,) = call(
                later_out_kernel, [shape(2, 2, rows, width)], x_mine, near, name="later_out", out_place=pl.ANY,
                scratch=[pltpu.SemaphoreType.DMA((4,))],
            )
            part, out = lax.optimization_barrier((part, out))
        d_o, totals = call(far_kernel, [field, two], u_o, got, part, sums, c_out, inv_o, diag_o, name=name + "_far")
        if further:
            more = (outer_swap(d_o),)
        else:
            mine, send = call(give_kernel, [pair, shape(2 * half, width)], d_o, d_i, name="give")
            more = out, near, mine, core_swap(send)
        parts, *rest = call(
            finish_kernel, [mail] + [field, rim] * further,
            u_o, d_o, got, outer_swap(tail), tail, d_i, totals, there, inner, inv_far,
            cx, cy, c, c_out, cx_edge, *sides, t0, name=name + "_finish",
        )
        more = *w_i, *rest, *more
        return d_o, d_i, all_total(parts), more

    d_o, d_i, total, (part_i, part, fix, far) = stage(v1_o, v1_i, pay, near, cross, t0, "later")
    z_o, z_i, near, cross, t0, pay, x_mine, z_mine = call(
        step_kernel,
        [field, three, shape(ROWS + 4 * half, width), eight, one, most, pair, pair],
        total, s_o, s_i, v1_o, v1_i, d_o, d_i, part_i, part, far, fix, cap, earlier, diag_o, diag_i, inv_o, inv_i, cx, cy, c, c_out,
        name="step", scratch=parts_of,
    )
    _, _, total, (out, got, q_mine, q_got) = stage(z_o, z_i, pay, near, cross, t0, "earlier", x_mine)
    (out,) = call(
        last_kernel, [shape(2, 2, rows, width)], out, total, x_mine, z_mine, got, q_mine, q_got, name="last",
        out_place=pl.ANY, scratch=[pltpu.VMEM((4, half, width), F32), pltpu.SemaphoreType.DMA((4,))], reuse=True,
    )
    return out


def solution(mesh):
    placed = (P("band", "tile", None),) * 6 + (P(None, "band", "tile", None),)
    return jax.shard_map(
        on_device,
        mesh=mesh,
        in_specs=placed,
        out_specs=P(None, "band", "tile", None),
        check_vma=False,
    )
```

```python
import jax
import jax.numpy as jnp
from jax import lax
from jax.experimental import pallas as pl
from jax.experimental.pallas import tpu as pltpu
from jax.sharding import PartitionSpec as P

NB = 8
ROWS = 8
AXES = ("band", "tile")
F32 = jnp.float32

pad_conductance = 4.0

COSTS = {"prepare": 0, "first_spread": 0, "later_spread": 0, "earlier_spread": 0, "later_out": 0}


def sizes():
    return lax.axis_size("band"), lax.axis_size("tile")


def core():
    return lax.rem(lax.axis_index("band"), 2)


def upper_chip():
    return lax.axis_index("band") >= 2


def core_swap(x):
    nb, _ = sizes()
    return lax.ppermute(x, "band", [(b, b ^ 1) for b in range(nb)])


def outer_swap(x):
    nb, _ = sizes()
    return lax.ppermute(x, "band", [(b, b ^ 2) for b in range(nb)])


def cross_swap(x):
    nb, nt = sizes()
    pairs = []
    for b in range(nb):
        for t in range(nt):
            other = (t + 1) % nt if b % 2 else (t - 1) % nt
            pairs.append((b * nt + t, (b ^ 1) * nt + other))
    return lax.ppermute(x, AXES, pairs)


def all_total(parts):
    return lax.all_to_all(parts, AXES, 0, 0, tiled=True)


def call(body, outs, *args, name, place=pltpu.VMEM, out_place=pltpu.VMEM, scratch=(), limit=10, reuse=False):
    cost = COSTS.get(name, 10)
    if place == pltpu.HBM:
        args = [pltpu.with_memory_space_constraint(a, pltpu.HBM) for a in args]
    return pl.pallas_call(
        body,
        out_shape=outs,
        in_specs=[pl.BlockSpec(memory_space=pl.ANY if reuse and n == 0 else place) for n in range(len(args))],
        input_output_aliases={0: 0} if reuse else {},
        out_specs=[pl.BlockSpec(memory_space=out_place)] * len(outs),
        scratch_shapes=list(scratch),
        name=name,
        cost_estimate=pl.CostEstimate(flops=cost * 10**9, bytes_accessed=cost * 10**6, transcendentals=0),
        compiler_params=pltpu.CompilerParams(vmem_limit_bytes=limit * 1024 * 1024),
    )(*args)


def shape(*dims):
    return jax.ShapeDtypeStruct(dims, F32)


def row_at(width, at):
    return lax.broadcasted_iota(jnp.int32, (ROWS, width), 0) == at


def stack_rows(rows):
    return jnp.concatenate(rows, 0)


def put_rows(first, last, core_ref, cross_ref):
    lower = core() == 1
    core_ref[...] = jnp.where(lower, first, last)
    cross_ref[...] = jnp.where(lower, last, first)


def put_two_rows(u_o_ref, u_i_ref, core_ref, cross_ref):
    rows = u_o_ref.shape[0]
    ends = [
        stack_rows([band_of(u_o_ref, u_i_ref, j)[r : r + 1, :] for r in pair for j in range(4)])
        for pair in ((0, 1), (rows - 1, rows - 2))
    ]
    put_rows(ends[0], ends[1], core_ref, cross_ref)


def take_rows(core_ref, cross_ref):
    lower = core() == 1
    tile = lax.axis_index("tile")
    cross = cross_ref[...]
    near = core_ref[0 : cross.shape[0], :]
    above = jnp.where(lower, near, jnp.where(tile == 0, 0.0, cross))
    below = jnp.where(lower, jnp.where(tile == lax.axis_size("tile") - 1, 0.0, cross), near)
    return above, below


def fold(total):
    acc = total[:, :128]
    for at in range(128, total.shape[1], 128):
        acc = acc + total[:, at : at + 128]
    return acc


def band_of(u_o_ref, u_i_ref, j):
    return u_o_ref if j == 0 else u_i_ref.at[j - 1]


def in_band(v_ref, cx_ref, cy_ref, carried, below, k, chunks):
    width = v_ref.shape[-1]
    r = k * ROWS
    x = v_ref[r : r + ROWS, :]
    cx = cx_ref[r : r + ROWS, :]
    cy = cy_ref[r : r + ROWS, :]
    after = below if k == chunks - 1 else v_ref[r + ROWS : r + ROWS + 1, :]
    down = jnp.where(row_at(width, ROWS - 1), after, pltpu.roll(x, ROWS - 1, 0))
    flux = cx * x
    up = jnp.where(row_at(width, 0), carried, pltpu.roll(flux, 1, 0))
    total = cx * down + up + cy * pltpu.roll(x, width - 1, 1) + pltpu.roll(cy * x, 1, 1)
    return x, total, flux[ROWS - 1 :, :]


def couple(xs, parts, c_ref, rs):
    parts = list(parts)
    for j in range(1, len(xs)):
        c = c_ref[j, rs, :]
        parts[j] = parts[j] + c * xs[j - 1]
        parts[j - 1] = parts[j - 1] + c * xs[j]
    return parts


def half_of(which, half):
    return pl.ds(pl.multiple_of(which * half, ROWS), half)


def start_copies(pairs, sems):
    copies = [pltpu.make_async_copy(source, to, sems.at[n]) for n, (source, to) in enumerate(pairs)]
    for copy in copies:
        copy.start()
    return copies


def load_kernel(
    cond_x_ref, cond_y_ref, via_ref, mask_ref, cap_ref, pad_ref, observe_ref,
    mine_ref, send_ref, pay_mine_ref, pay_send_ref, last_ref, middle_ref,
    via_at, mask_at, pad_at, edge_at, sems,
):
    half, width = send_ref.shape[1:]
    me = core()
    upper = upper_chip()
    halves = ((send_ref, pay_send_ref, 1 - me), (mine_ref, pay_mine_ref, me))
    pairs = [(via_ref, via_at), (mask_ref, mask_at), (pad_ref, pad_at)]
    pairs.append((cond_x_ref.at[:, pl.ds(half - ROWS, ROWS), :], edge_at.at[0]))
    pairs.append((cond_x_ref.at[:, pl.ds(2 * half - ROWS, ROWS), :], edge_at.at[1]))
    for ref, _, which in halves:
        rs = half_of(which, half)
        pairs += [
            (cond_x_ref.at[:, rs, :], ref.at[0:2]),
            (cond_y_ref.at[:, rs, :], ref.at[2:4]),
            (observe_ref.at[1, :, rs, :], ref.at[8:10]),
            (cap_ref.at[:, rs, :], ref.at[10:12]),
        ]
    for ref, _, which in halves:
        pairs.append((observe_ref.at[0, :, half_of(which, half), :], ref.at[12:14]))
    copies = start_copies(pairs, sems)
    for copy in copies[:5]:
        copy.wait()
    for band in range(2):
        middle_ref[band : band + 1, :] = edge_at[0, band, ROWS - 1 :, :]
        last_ref[band : band + 1, :] = edge_at[1, band, ROWS - 1 :, :]
    lane = lax.broadcasted_iota(jnp.int32, (ROWS, width), 1)
    facing = jnp.where(upper, 0, 1)
    for n, (ref, pay_ref, which) in enumerate(halves):
        for copy in copies[5 + 4 * n : 9 + 4 * n]:
            copy.wait()
        rs = half_of(which, half)
        for band in range(2):
            ref[4 + band] = via_at[band, rs, :] * mask_at[band, rs, :].astype(F32)
            ref[6 + band] = ref[10 + band] + pad_conductance * pad_at[band, rs, :].astype(F32)
        carried = jnp.where(which == 0, 0.0, edge_at[0, facing, ROWS - 1 :, :])
        for k in range(half // ROWS):
            rs = slice(k * ROWS, (k + 1) * ROWS)
            cx, cy, seen, via = ref[facing, rs, :], ref[2 + facing, rs, :], ref[8 + facing, rs, :], ref[5, rs, :]
            up = jnp.where(row_at(width, 0), carried, pltpu.roll(cx, 1, 0))
            carried = cx[ROWS - 1 :, :]
            left = jnp.where(lane == 0, 0.0, pltpu.roll(cy, 1, 1))
            diag = ref[6 + facing, rs, :] + cx + cy + up + left + ref[4, rs, :]
            inv = 1.0 / (diag + via)
            pay_ref[rs, :] = jnp.where(upper, diag, via)
            pay_ref[half + k * ROWS : half + (k + 1) * ROWS, :] = jnp.where(upper, seen, seen * inv)
            if 2 * k * ROWS >= half:
                at = 3 * half // 2 + k * ROWS
                pay_ref[at : at + ROWS, :] = inv
    pay_send_ref[5 * half // 2 :, :] = stack_rows([middle_ref[...], last_ref[...], jnp.zeros((ROWS - 4, width), F32)])
    for copy in copies[-2:]:
        copy.wait()


def theirs():
    return (core() == 1) == upper_chip()


def pay_kernel(mine_ref, got_ref, last_ref, pay_ref, more_ref, all_last_ref):
    half = pay_ref.shape[0]
    end = 5 * half // 2
    pay_ref[...] = jnp.where(theirs(), got_ref[0:half, :], mine_ref[0:half, :])
    more_ref[...] = jnp.where(theirs(), got_ref[half:end, :], mine_ref[half:, :])
    own, other = last_ref[...], got_ref[end + 2 : end + 4, :]
    all_last_ref[...] = stack_rows([jnp.where(core() == 0, own, other), jnp.where(core() == 0, other, own)])


def place_of(owner, band):
    n = 2 * owner + band
    return jnp.where(upper_chip(), n, 3 - n)


def prepare_kernel(
    mine_ref, got_ref, middle_ref, more_ref, last_ref,
    cx_ref, cy_ref, c_ref, diag_ref, inv_ref, s_ref, part_ref, seen_o_ref, edge_ref, cap_ref, seen_ref, all_part, all_seen,
):
    half, width = part_ref.shape
    me = core()
    upper = upper_chip()
    lane = lax.broadcasted_iota(jnp.int32, (ROWS, width), 1)
    first_tile = jnp.logical_and(me == 0, lax.axis_index("tile") == 0)
    own_edge = jnp.where(me == 1, middle_ref[...], last_ref[0:2, :])
    got_edge = jnp.where(me == 1, more_ref[5 * half // 2 : 5 * half // 2 + 2, :], last_ref[2:4, :])
    c_ref[0] = jnp.zeros((half, width), F32)
    for owner, ref, edges in ((me, mine_ref, own_edge), (1 - me, got_ref, got_edge)):
        for band in range(2):
            j = place_of(owner, band)
            carried = jnp.where(first_tile, 0.0, edges[band : band + 1, :])
            edge_ref[pl.ds(j, 1), :] = carried
            cx_ref[j] = ref[band]
            cap_ref[j] = ref[10 + band]
            seen_ref[j] = ref[12 + band]
            all_seen[j] = ref[8 + band]
            via_at = jnp.where(upper, j + 1, j)

            @pl.when(via_at < 4)
            def _():
                c_ref[via_at] = ref[4 + band]

            for k in range(half // ROWS):
                rs = slice(k * ROWS, (k + 1) * ROWS)
                cx, cy, diag = (ref[2 * n + band, rs, :] for n in (0, 1, 3))
                cut = jnp.where(lane == width - 1, 0.0, cy)
                up = jnp.where(row_at(width, 0), carried, pltpu.roll(cx, 1, 0))
                carried = cx[ROWS - 1 :, :]
                cy_ref[j, rs, :] = cut
                all_part[j, rs, :] = diag + cx + cy + up + pltpu.roll(cut, 1, 1)
    part_ref[...] = all_part[0] + c_ref[1]
    seen_o_ref[...] = all_seen[0]
    for j in range(1, 4):
        for k in range(half // ROWS):
            rs = slice(k * ROWS, (k + 1) * ROWS)
            diag = all_part[j, rs, :] + c_ref[j, rs, :]
            if j < 3:
                diag = diag + c_ref[j + 1, rs, :]
            inv = 1.0 / diag
            diag_ref[j - 1, rs, :] = diag
            inv_ref[j - 1, rs, :] = inv
            s_ref[j - 1, rs, :] = all_seen[j, rs, :] * inv


def outer_kernel(
    part_ref, seen_ref, link_ref, cx_ref, cy_ref, c_ref, inv_i_ref, s_i_ref,
    c_out_ref, diag_ref, inv_ref, s_ref, core_ref, cross_ref, fix_ref,
):
    rows, width = part_ref.shape
    upper = upper_chip()
    for k in range(rows // ROWS):
        rs = slice(k * ROWS, (k + 1) * ROWS)
        c_out = jnp.where(upper, link_ref[rs, :], c_ref[0, rs, :])
        diag = part_ref[rs, :] + c_out
        inv = 1.0 / diag
        c_out_ref[rs, :] = c_out
        diag_ref[rs, :] = diag
        inv_ref[rs, :] = inv
        s_ref[rs, :] = seen_ref[rs, :] * inv
    ends = []
    for r, beyond in ((0, 0), (rows - 1, rows - 2)):
        at = slice(r, r + 1)
        lines = [band_of(s_ref, s_i_ref, j)[at, :] for j in range(4)]
        lines += [band_of(inv_ref, inv_i_ref, j)[at, :] for j in range(4)]
        lines += [cy_ref[j, at, :] for j in range(4)]
        lines += [c_out_ref[at, :]] + [c_ref[j, at, :] for j in range(1, 4)]
        lines += [cx_ref[j, beyond : beyond + 1, :] for j in range(4)]
        ends.append(stack_rows(lines))
    put_rows(ends[0], ends[1], core_ref, cross_ref)
    fix_ref[...] = jnp.where(upper, diag_ref[0:1, :], s_ref[0:1, :])


def own_parts(u_o_ref, u_i_ref, cx_ref, cy_ref, c_ref, pay_ref, scratch_ref):
    rows, width = u_o_ref.shape
    chunks = rows // ROWS
    none = jnp.zeros((1, width), F32)
    carried = none
    for k in range(chunks):
        rs = slice(k * ROWS, (k + 1) * ROWS)
        x, part, carried = in_band(u_o_ref, cx_ref.at[0], cy_ref.at[0], carried, none, k, chunks)
        pay_ref[rs, :] = x
        scratch_ref[rs, :] = part + c_ref[1, rs, :] * u_i_ref[0, rs, :]
    size = rows // 2
    first = jnp.where(upper_chip(), 0, rows - size)
    pay_ref[rows : rows + size, :] = scratch_ref[pl.ds(pl.multiple_of(first, ROWS), size), :]


def spread_kernel(
    u_o_ref, u_i_ref, core_ref, cross_ref, cx_ref, cy_ref, c_ref, inv_i_ref, edge_ref, v_i_ref, part_ref, sums_ref
):
    above, below = take_rows(core_ref, cross_ref)
    spread_rows(u_o_ref, u_i_ref, above, below, cx_ref, cy_ref, c_ref, inv_i_ref, edge_ref, v_i_ref, part_ref, sums_ref)


def spread_rows(
    u_o_ref, u_i_ref, above, below, cx_ref, cy_ref, c_ref, inv_i_ref, edge_ref, v_i_ref, part_ref, sums_ref, diag_i_ref=None
):
    rows, width = u_o_ref.shape
    chunks = rows // ROWS
    carried = [edge_ref[j : j + 1, :] * above[j : j + 1] for j in range(4)]
    sums = [jnp.zeros((ROWS, width), F32) for _ in range(2)]
    for k in range(chunks):
        rs = slice(k * ROWS, (k + 1) * ROWS)
        xs, parts = [], []
        for j in range(4):
            x, part, carried[j] = in_band(
                band_of(u_o_ref, u_i_ref, j), cx_ref.at[j], cy_ref.at[j], carried[j], below[j : j + 1], k, chunks
            )
            xs.append(x)
            parts.append(part)
        parts = couple(xs, parts, c_ref, rs)
        part_ref[rs, :] = parts[0]
        for j in range(1, 4):
            v = inv_i_ref[j - 1, rs, :] * parts[j]
            weighted = parts[j]
            if diag_i_ref is not None:
                v = xs[j] - v
                weighted = diag_i_ref[j - 1, rs, :] * xs[j] - weighted
            v_i_ref[j - 1, rs, :] = v
            if diag_i_ref is not None:
                sums[0] = sums[0] + xs[j] * weighted
            sums[1] = sums[1] + v * weighted
    sums_ref[0:ROWS, :] = fold(sums[0])
    sums_ref[ROWS : 2 * ROWS, :] = fold(sums[1])


def beside(u_o_ref, u_i_ref, above, below, side_above, side_below, edge_ref, cx_ref):
    rows, width = u_o_ref.shape
    here = stack_rows([above[0:4], below[0:4]])
    beyond = stack_rows([above[4:8], below[4:8]])
    inside = [band_of(u_o_ref, u_i_ref, j)[r : r + 1, :] for r in (0, rows - 1) for j in range(4)]
    toward = stack_rows([edge_ref[...]] + [cx_ref[j, rows - 1 :, :] for j in range(4)])
    inv, cy, c, away = (stack_rows([side_above[n : n + 4], side_below[n : n + 4]]) for n in (4, 8, 12, 16))
    c = jnp.where(jnp.logical_or(row_at(width, 0), row_at(width, 4)), 0.0, c)
    total = toward * stack_rows(inside) + away * beyond
    total = total + cy * pltpu.roll(here, width - 1, 1) + pltpu.roll(cy * here, 1, 1)
    return total + c * pltpu.roll(here, 1, 0) + pltpu.roll(c * here, ROWS - 1, 0), inv


def two_spread_kernel(
    u_o_ref, u_i_ref, core_ref, cross_ref, cx_ref, cy_ref, c_ref, inv_i_ref, edge_ref, side_core_ref, side_cross_ref,
    diag_i_ref, d_i_ref, part_ref, sums_ref, tail_ref, beside_ref, total_ref, w_ref=None,
):
    rows, width = u_o_ref.shape
    chunks = rows // ROWS
    above, below = take_rows(core_ref, cross_ref)
    spread_rows(u_o_ref, u_i_ref, above, below, cx_ref, cy_ref, c_ref, inv_i_ref, edge_ref, d_i_ref, part_ref, sums_ref, diag_i_ref)
    fluxes = [edge_ref[0:1, :] * above[0:1], cx_ref[0, rows - 1 :, :] * below[0:1]]
    tail_ref[...] = stack_rows([above[0:1], below[0:1], *fluxes])
    side_above, side_below = take_rows(side_core_ref, side_cross_ref)
    parts_there, inv = beside(u_o_ref, u_i_ref, above, below, side_above, side_below, edge_ref, cx_ref)
    beside_ref[...] = parts_there
    there = stack_rows([above[0:4], below[0:4]]) - inv * parts_there
    carried = [edge_ref[j : j + 1, :] * there[j : j + 1] for j in range(1, 4)]
    total = jnp.zeros((ROWS, width), F32)
    for k in range(chunks):
        rs = slice(k * ROWS, (k + 1) * ROWS)
        xs, parts = [], []
        for j in range(1, 4):
            x, part, carried[j - 1] = in_band(
                d_i_ref.at[j - 1], cx_ref.at[j], cy_ref.at[j], carried[j - 1], there[4 + j : 5 + j], k, chunks
            )
            xs.append(x)
            parts.append(part)
        parts = couple(xs, parts, c_ref.at[pl.ds(1, 3)], rs)
        for j in range(3):
            total = total + xs[j] * parts[j]
            if w_ref is not None:
                w_ref[j, rs, :] = parts[j]
    total_ref[...] = fold(total)


def far_first_kernel(
    u_o_ref, part_ref, got_ref, more_ref, fix_ref, c_out_ref, inv_ref, v_i_ref, sums_ref, cx_ref, cy_ref, c_ref,
    v_ref, core_ref, cross_ref, total_ref, pay_ref, inv_far_ref, scratch_ref,
):
    rows, width = u_o_ref.shape
    upper = upper_chip()
    total = jnp.zeros((ROWS, width), F32)
    for k in range(rows // ROWS):
        rs = slice(k * ROWS, (k + 1) * ROWS)
        c_out = c_out_ref[rs, :]
        diag, far = got_ref[rs, :] + c_out, more_ref[rs, :]
        if k == 0:
            first = jnp.broadcast_to(fix_ref[0:1, :], far.shape)
            diag = jnp.where(row_at(width, 0), first, diag)
            far = jnp.where(jnp.logical_and(upper, row_at(width, 0)), first, far)
        inv_far = 1.0 / jnp.where(upper, 1.0, diag)
        if k * ROWS < rows // 2:
            inv_far_ref[rs, :] = jnp.where(upper, more_ref[rows + k * ROWS : rows + (k + 1) * ROWS, :], inv_far)
        far = jnp.where(upper, far, far * inv_far)
        part = part_ref[rs, :] + c_out * far
        v = inv_ref[rs, :] * part
        v_ref[rs, :] = v
        total = total + v * part
    total_ref[...] = fold(total) + sums_ref[ROWS : 2 * ROWS, :]
    put_two_rows(v_ref, v_i_ref, core_ref, cross_ref)
    own_parts(v_ref, v_i_ref, cx_ref, cy_ref, c_ref, pay_ref, scratch_ref)


def far_kernel(u_o_ref, got_ref, part_ref, sums_ref, c_out_ref, inv_ref, diag_ref, d_ref, totals_ref):
    rows, width = u_o_ref.shape
    sums = [jnp.zeros((ROWS, width), F32) for _ in range(2)]
    for k in range(rows // ROWS):
        rs = slice(k * ROWS, (k + 1) * ROWS)
        u = u_o_ref[rs, :]
        part = part_ref[rs, :] + c_out_ref[rs, :] * got_ref[rs, :]
        d = u - inv_ref[rs, :] * part
        weighted = diag_ref[rs, :] * u - part
        d_ref[rs, :] = d
        sums[0] = sums[0] + u * weighted
        sums[1] = sums[1] + d * weighted
    totals_ref[0:ROWS, :] = fold(sums[0]) + sums_ref[0:ROWS, :]
    totals_ref[ROWS : 2 * ROWS, :] = fold(sums[1]) + sums_ref[ROWS : 2 * ROWS, :]


def finish_kernel(
    u_o_ref, d_ref, got_ref, tail_ref, own_tail_ref, d_i_ref, totals_ref, beside_ref, inner_ref, inv_far_ref,
    cx_ref, cy_ref, c_ref, c_out_ref, edge_ref, side_core_ref, side_cross_ref, t0_ref,
    mail_ref, w_ref=None, fix_ref=None,
):
    rows, width = u_o_ref.shape
    chunks = rows // ROWS
    none = jnp.zeros((1, width), F32)
    sums = [jnp.zeros((ROWS, width), F32) for _ in range(2)]
    carried = none
    for k in range(chunks):
        rs = slice(k * ROWS, (k + 1) * ROWS)
        d, part, carried = in_band(d_ref, cx_ref.at[0], cy_ref.at[0], carried, none, k, chunks)
        coupled = c_ref[1, rs, :] * d_i_ref[0, rs, :]
        sums[0] = sums[0] + d * (part + 2.0 * coupled)
        if w_ref is not None:
            w_ref[rs, :] = part + coupled
    side_above, side_below = take_rows(side_core_ref, side_cross_ref)
    up = side_above[4:5] * (beside_ref[0:1, :] + side_above[12:13] * tail_ref[0:1, :])
    down = side_below[4:5] * (beside_ref[4:5, :] + side_below[12:13] * tail_ref[1:2, :])
    up = edge_ref[0:1, :] * (own_tail_ref[0:1, :] - up)
    down = cx_ref[0, rows - 1 :, :] * (own_tail_ref[1:2, :] - down)
    if fix_ref is not None:
        fix_ref[...] = stack_rows([up, down])
    size = rows // 2
    first = jnp.where(upper_chip(), rows - size, 0)
    far_up = jnp.where(first == 0, tail_ref[2:3, :], 0.0)
    far_down = jnp.where(first + size == rows, tail_ref[3:4, :], 0.0)
    for k in range(size // ROWS):
        at = pl.ds(pl.multiple_of(first + k * ROWS, ROWS), ROWS)
        c_out = c_out_ref[at, :]
        part = got_ref[rows + k * ROWS : rows + (k + 1) * ROWS, :] + c_out * u_o_ref[at, :]
        if k == 0:
            part = part + jnp.where(row_at(width, 0), far_up, 0.0)
        if k == size // ROWS - 1:
            part = part + jnp.where(row_at(width, ROWS - 1), far_down, 0.0)
        far = got_ref[at, :] - inv_far_ref[k * ROWS : (k + 1) * ROWS, :] * part
        sums[1] = sums[1] + d_ref[at, :] * (c_out * far)
    ends = up * d_ref[0:1, :] + down * d_ref[rows - 1 :, :]
    last = fold(sums[0] + 2.0 * sums[1] + jnp.where(row_at(width, 0), ends, 0.0)) + inner_ref[...]
    terms = (t0_ref[...], totals_ref[0:ROWS, :], totals_ref[ROWS : 2 * ROWS, :], last)
    lane = lax.broadcasted_iota(jnp.int32, (ROWS, 128), 1)
    row = jnp.zeros((ROWS, 128), F32)
    for n, t in enumerate(terms):
        t = t + pltpu.roll(t, 64, 1)
        t = t + pltpu.roll(t, 32, 1)
        row = jnp.where(lane // 32 == n, t, row)
    row = jnp.broadcast_to(jnp.sum(row, 0, keepdims=True), (ROWS, 128))
    for at in range(0, mail_ref.shape[0], ROWS):
        mail_ref[at : at + ROWS, :] = row


def weights(mail_ref):
    block = mail_ref[0:ROWS, :]
    for at in range(ROWS, mail_ref.shape[0], ROWS):
        block = block + mail_ref[at : at + ROWS, :]
    block = jnp.sum(block, 0, keepdims=True)
    k0, k1, k2, spread = (jnp.sum(block[:, 32 * k : 32 * (k + 1)], 1, keepdims=True) for k in range(4))
    k3 = k2 - spread
    nu = k1 / k0
    h = k2 - nu * k1
    t = jnp.clip(h / (k3 - 2.0 * nu * k2 + nu * nu * k1), 0.5, 80.0)
    a = k0 / (k1 - h * t)
    return a * (1.0 + t * nu), -t * a


def hand_out(j, value, k, holds_outer, mine_ref, send_ref, first, half):
    band = jnp.where(upper_chip(), j % 2, 1 - j % 2)
    size = value.shape[0]
    if holds_outer == (j < 2):
        mine_ref[band, k * ROWS : k * ROWS + size, :] = value
    else:
        send_ref[pl.ds(pl.multiple_of(first + band * half + k * ROWS, ROWS), size), :] = value


def for_holder(body):
    outer = (core() == 1) != upper_chip()
    pl.when(outer)(lambda: body(True))
    pl.when(jnp.logical_not(outer))(lambda: body(False))


def step_kernel(
    mail_ref, s_o_ref, s_i_ref, v1_o_ref, v1_i_ref, d_o_ref, d_i_ref, part_i_ref, part_ref, far_ref, fix_ref, cap_ref, seen_ref,
    diag_o_ref, diag_i_ref, inv_o_ref, inv_i_ref, cx_ref, cy_ref, c_ref, c_out_ref,
    z_o_ref, z_i_ref, core_ref, cross_ref, total_ref, pay_ref, x_mine_ref, z_mine_ref, scratch_ref,
):
    rows, width = s_o_ref.shape
    chunks = rows // ROWS
    a, b = weights(mail_ref)

    def run(holds_outer):
        total = jnp.zeros((ROWS, width), F32)
        for j in range(4):
            for k in range(chunks):
                rs = slice(k * ROWS, (k + 1) * ROWS)
                s, p, d, diag, inv = (
                    band_of(o, i, j)[rs, :]
                    for o, i in (
                        (s_o_ref, s_i_ref), (v1_o_ref, v1_i_ref), (d_o_ref, d_i_ref),
                        (diag_o_ref, diag_i_ref), (inv_o_ref, inv_i_ref),
                    )
                )
                if j == 0:
                    part = part_ref[rs, :] + c_out_ref[rs, :] * far_ref[rs, :]
                    if k == 0:
                        part = part + jnp.where(row_at(width, 0), fix_ref[0:1, :], 0.0)
                    if k == chunks - 1:
                        part = part + jnp.where(row_at(width, ROWS - 1), fix_ref[1:2, :], 0.0)
                else:
                    part = part_i_ref[j - 1, rs, :]
                    if j == 1:
                        part = part + c_ref[1, rs, :] * d_o_ref[rs, :]
                r = inv * part
                x = s + a * p + b * d
                residual = cap_ref[j, rs, :] * x + seen_ref[j, rs, :] - diag * (x - (p + a * (p - d) + b * r))
                z = residual * inv
                band_of(z_o_ref, z_i_ref, j)[rs, :] = z
                total = total + residual * z
                hand_out(j, x, k, holds_outer, x_mine_ref, core_ref, ROWS, rows)
                hand_out(j, z, k, holds_outer, z_mine_ref, core_ref, ROWS + 2 * rows, rows)
        total_ref[...] = fold(total)

    for_holder(run)
    put_two_rows(z_o_ref, z_i_ref, core_ref.at[0:ROWS], cross_ref)
    own_parts(z_o_ref, z_i_ref, cx_ref, cy_ref, c_ref, pay_ref, scratch_ref)


def give_kernel(q_o_ref, q_i_ref, mine_ref, send_ref):
    rows = q_o_ref.shape[0]

    def run(holds_outer):
        for j in range(4):
            hand_out(j, band_of(q_o_ref, q_i_ref, j)[...], 0, holds_outer, mine_ref, send_ref, 0, rows)

    for_holder(run)


def out_rows(out_ref, step, band, which):
    return out_ref.at[step, band, half_of(which, out_ref.shape[2] // 2), :]


def later_out_kernel(x_mine_ref, got_ref, out_ref, sems):
    half = x_mine_ref.shape[1]
    pairs = []
    for band in range(2):
        at = ROWS + band * half
        pairs.append((x_mine_ref.at[band], out_rows(out_ref, 1, band, core())))
        pairs.append((got_ref.at[at : at + half], out_rows(out_ref, 1, band, 1 - core())))
    for copy in start_copies(pairs, sems):
        copy.wait()


def last_kernel(_, mail_ref, x_mine_ref, z_mine_ref, got_ref, q_mine_ref, q_got_ref, out_ref, answer, sems):
    half = x_mine_ref.shape[1]
    a, b = weights(mail_ref)
    copies = []
    for band in range(2):
        at = ROWS + band * half
        got = got_ref.at[at : at + half], got_ref.at[at + 2 * half : at + 3 * half], q_got_ref.at[band * half : (band + 1) * half]
        mine = [ref.at[band] for ref in (x_mine_ref, z_mine_ref, q_mine_ref)]
        for which, (x_ref, z_ref, q_ref) in ((core(), mine), (1 - core(), got)):
            n = len(copies)
            answer[n] = x_ref[...] + a * z_ref[...] + b * q_ref[...]
            copies.append(pltpu.make_async_copy(answer.at[n], out_rows(out_ref, 0, band, which), sems.at[n]))
            copies[-1].start()
    for copy in copies:
        copy.wait()


def on_device(cond_x, cond_y, via_cond, via_mask, capacitance, pad_mask, observe):
    _, rows, width = cond_x.shape
    half = rows // 2
    field, three, four, edge = shape(half, width), shape(3, half, width), shape(4, half, width), shape(4, width)
    eight, twenty = shape(ROWS, width), shape(20, width)
    most, part_rows = shape(3 * half // 2, width), shape(half // 2, width)
    rim, pair = shape(2, width), shape(2, half, width)
    mail = shape(lax.axis_size("band") * lax.axis_size("tile"), 128)
    one, two = shape(ROWS, 128), shape(2 * ROWS, 128)
    fourteen = shape(14, half, width)
    whole, whole_int = pltpu.VMEM((2, rows, width), F32), pltpu.VMEM((2, rows, width), jnp.int32)
    own, send, pay, pay_send, last, middle = call(
        load_kernel, [fourteen, fourteen, shape(5 * half // 2, width), shape(5 * half // 2 + ROWS, width), rim, rim],
        cond_x, cond_y, via_cond, via_mask, capacitance, pad_mask, observe, name="load", place=pltpu.HBM,
        scratch=[whole, whole_int, whole_int, pltpu.VMEM((2, 2, ROWS, width), F32), pltpu.SemaphoreType.DMA((15,))],
    )
    more = core_swap(pay_send)
    more, send = lax.optimization_barrier((more, send))
    pay, pay_more, last = call(pay_kernel, [field, most, edge], pay, more, last, name="pay")
    link, traded, last = outer_swap(pay), core_swap(send), cross_swap(last)
    pay_more, last = lax.optimization_barrier((pay_more, last))
    far = outer_swap(pay_more)
    cx, cy, c, diag_i, inv_i, s_i, part, seen, cx_edge, cap, earlier = call(
        prepare_kernel, [four, four, four, three, three, three, field, field, edge, four, four],
        own, traded, middle, more, last, name="prepare",
        scratch=[pltpu.VMEM((4, half, width), F32), pltpu.VMEM((4, half, width), F32)],
    )
    c_out, diag_o, inv_o, s_o, near, cross, fix = call(
        outer_kernel, [field, field, field, field, twenty, twenty, shape(1, width)],
        part, seen, link, cx, cy, c, inv_i, s_i, name="outer",
    )
    fix, sides = outer_swap(fix), (core_swap(near), cross_swap(cross))

    coeffs = (cx, cy, c, inv_i, cx_edge)
    parts_of = [pltpu.VMEM((half, width), F32)]
    v1_i, part, sums = call(spread_kernel, [three, field, two], s_o, s_i, *sides, *coeffs, name="first_spread")
    v1_o, near, cross, t0, pay, inv_far = call(
        far_first_kernel, [field, eight, eight, one, most, part_rows],
        s_o, part, link, far, fix, c_out, inv_o, v1_i, sums, cx, cy, c, name="first_far", scratch=parts_of,
    )

    def stage(u_o, u_i, pay, near, cross, t0, name, x_mine=None):
        further = x_mine is None
        got, cross, near = outer_swap(pay), cross_swap(cross), core_swap(near)
        d_i, part, sums, tail, there, inner, *w_i = call(
            two_spread_kernel, [three, field, two, edge, eight, one] + [three] * further,
            u_o, u_i, near, cross, *coeffs, *sides, diag_i, name=name + "_spread",
        )
        if not further:
            (out,) = call(
                later_out_kernel, [shape(2, 2, rows, width)], x_mine, near, name="later_out", out_place=pl.ANY,
                scratch=[pltpu.SemaphoreType.DMA((4,))],
            )
            part, out = lax.optimization_barrier((part, out))
        d_o, totals = call(far_kernel, [field, two], u_o, got, part, sums, c_out, inv_o, diag_o, name=name + "_far")
        if further:
            more = (outer_swap(d_o),)
        else:
            mine, send = call(give_kernel, [pair, shape(2 * half, width)], d_o, d_i, name="give")
            more = out, near, mine, core_swap(send)
        parts, *rest = call(
            finish_kernel, [mail] + [field, rim] * further,
            u_o, d_o, got, outer_swap(tail), tail, d_i, totals, there, inner, inv_far,
            cx, cy, c, c_out, cx_edge, *sides, t0, name=name + "_finish",
        )
        more = *w_i, *rest, *more
        return d_o, d_i, all_total(parts), more

    d_o, d_i, total, (part_i, part, fix, far) = stage(v1_o, v1_i, pay, near, cross, t0, "later")
    z_o, z_i, near, cross, t0, pay, x_mine, z_mine = call(
        step_kernel,
        [field, three, shape(ROWS + 4 * half, width), eight, one, most, pair, pair],
        total, s_o, s_i, v1_o, v1_i, d_o, d_i, part_i, part, far, fix, cap, earlier, diag_o, diag_i, inv_o, inv_i, cx, cy, c, c_out,
        name="step", scratch=parts_of,
    )
    _, _, total, (out, got, q_mine, q_got) = stage(z_o, z_i, pay, near, cross, t0, "earlier", x_mine)
    (out,) = call(
        last_kernel, [shape(2, 2, rows, width)], out, total, x_mine, z_mine, got, q_mine, q_got, name="last",
        out_place=pl.ANY, scratch=[pltpu.VMEM((4, half, width), F32), pltpu.SemaphoreType.DMA((4,))], reuse=True,
    )
    return out


def solution(mesh):
    placed = (P("band", "tile", None),) * 6 + (P(None, "band", "tile", None),)
    return jax.shard_map(
        on_device,
        mesh=mesh,
        in_specs=placed,
        out_specs=P(None, "band", "tile", None),
        check_vma=False,
    )
```
